32 devices in a mesh: seq: 8 (over y, x, core), dp: 4 (over z).
Axes of the slice: x: 2, y: 2, z: 4, core: 2. Of those that a mesh axis runs over, the one named last changes fastest.
Arguments:
- tokens: bfloat16 [2048, 8, 512], P('seq', 'dp'), may hold values from -6 to 6
- cotangent: bfloat16 [2048, 8, 512], P('seq', 'dp'), may hold values from -6 to 6
- query_weight: bfloat16 [512, 512], replicated, may hold values from -0.5 to 0.5
- key_weight: bfloat16 [512, 512], replicated, may hold values from -0.25 to 0.25
- value_weight: bfloat16 [512, 512], replicated, may hold values from -0.25 to 0.25
- output_weight: bfloat16 [512, 512], replicated, may hold values from -2 to 2
- attn_gate_weight: bfloat16 [512, 512], replicated, may hold values from -0.25 to 0.25
- attn_gate_bias: float32 [512], replicated, may hold values from -4 to 4
- up_weight: bfloat16 [512, 2048], replicated, may hold values from -0.25 to 0.25
- down_weight: bfloat16 [2048, 512], replicated, may hold values from -0.1875 to 0.1875
- ffn_gate_weight: bfloat16 [512, 512], replicated, may hold values from -0.25 to 0.25
- ffn_gate_bias: float32 [512], replicated, may hold values from -4 to 4
- first_gain: float32 [512], replicated, may hold values from 0.5 to 1.5
- first_shift: float32 [512], replicated, may hold values from -3 to 3
- second_gain: float32 [512], replicated, may hold values from 0.5 to 1.5
- second_shift: float32 [512], replicated, may hold values from -3 to 3
- row_kind: int32 [8], P('dp'), may hold values from 1 to 2, as said below
- block_order: int32 [8, 16], P('dp'), may hold values from 0 to 15, as said below
Outputs:
- mixed: bfloat16 [2048, 8, 512], P('seq', 'dp')
- tokens_grad: bfloat16 [2048, 8, 512], P('seq', 'dp')
- query_grad: float32 [512, 512], replicated
- key_grad: float32 [512, 512], replicated
- value_grad: float32 [512, 512], replicated
- output_grad: float32 [512, 512], replicated
- attn_gate_grad: float32 [512, 512], replicated
- attn_bias_grad: float32 [512], replicated
- up_grad: float32 [512, 2048], replicated
- down_grad: float32 [2048, 512], replicated
- ffn_gate_grad: float32 [512, 512], replicated
- ffn_bias_grad: float32 [512], replicated
- first_gain_grad: float32 [512], replicated
- first_shift_grad: float32 [512], replicated
- second_gain_grad: float32 [512], replicated
- second_shift_grad: float32 [512], replicated
The draws below stay inside these ranges and needn't reach their ends.
Inputs may be any that keep to these rules, and one draw needn't show every extreme that they name: A buffer holds one sequence of 2048 tokens where row_kind is 1, or two of 1024 tokens (positions below and from 1024) where it is 2; every draw has buffers of both kinds. `block_order`: each row is a permutation of the half-blocks; stored half-blocks 2 t and 2 t + 1 (those of the t-th device along seq) hold a half-block of the first half of the positions and one of the second half.
All inputs are finite; a program needn't handle non-finite values.
Results may differ from the reference program's by a relative error of at most 0.024.
Values may be sent and summed in bfloat16 or wider, within the bound.
A program may use at most 192 MiB of HBM per device.

```python
import math
import jax
import jax.numpy as jnp
from jax import lax

D = 512
H = 8
HD = 64
FF = 2048
LONG = 2048
ROWS = 8
N_SEQ = 8


def shuffle_range(item_key):
    return jax.random.permutation(item_key, N_SEQ).astype(jnp.int32)


def draw_row_kind(key, part):
    key = jax.random.fold_in(key, 11)
    key_kinds, key_spots = jax.random.split(key)
    buffer_kinds = jax.random.randint(key_kinds, (ROWS,), 1, 3, dtype=jnp.int32)
    shuffled = jax.random.permutation(key_spots, ROWS)
    buffer_kinds = buffer_kinds.at[shuffled[0]].set(1).at[shuffled[1]].set(2)
    return buffer_kinds


def draw_block_order(key, part):
    key = jax.random.fold_in(key, 23)
    key_lower, key_upper = jax.random.split(key)
    lower = jax.vmap(shuffle_range)(jax.random.split(key_lower, ROWS))
    upper = jax.vmap(shuffle_range)(jax.random.split(key_upper, ROWS)) + N_SEQ
    return jnp.stack([lower, upper], axis=-1).reshape(ROWS, 2 * N_SEQ).astype(jnp.int32)


def levels(key, shape, shards, smallest, top_value):
    loudness = 1.0
    for dim, parts in shards:
        draws = jax.random.uniform(jax.random.fold_in(jax.random.fold_in(key, 6), dim), (parts,), jnp.float32, smallest / len(shards), top_value / len(shards))
        loudness = loudness * jnp.repeat(jnp.exp(draws), shape[dim] // parts).reshape((-1,) + (1,) * (len(shape) - 1 - dim))
    return loudness


def gaussian(stream_key, extent, scale, reach, shards=(), kind=jnp.bfloat16):
    entries = scale * jax.random.normal(stream_key, extent, jnp.float32)
    if shards:
        entries = entries * levels(stream_key, extent, shards, -0.22, 0.18)
    return jnp.clip(entries, -reach, reach).astype(kind)


def setup_inputs(seed: int = 0) -> dict:
    streams_of = jax.random.split(jax.random.key(seed), 19)
    return {
        "tokens": gaussian(streams_of[0], (LONG, ROWS, D), 1.0, 6.0, ((0, 8), (1, 4))),
        "cotangent": gaussian(streams_of[1], (LONG, ROWS, D), 1.0, 6.0, ((0, 8), (1, 4))),
        "query_weight": gaussian(streams_of[2], (D, D), (D // 4) ** -0.5, 0.5),
        "key_weight": gaussian(streams_of[3], (D, D), D ** -0.5, 0.25),
        "value_weight": gaussian(streams_of[4], (D, D), D ** -0.5, 0.25),
        "output_weight": gaussian(streams_of[5], (D, D), (max(D // 64, 1)) ** -0.5, 2.0),
        "attn_gate_weight": gaussian(streams_of[6], (D, D), D ** -0.5, 0.25),
        "attn_gate_bias": gaussian(streams_of[7], (D,), 1.0, 4.0, (), jnp.float32),
        "up_weight": gaussian(streams_of[8], (D, FF), D ** -0.5, 0.25),
        "down_weight": gaussian(streams_of[9], (FF, D), (FF // 2) ** -0.5, 0.1875),
        "ffn_gate_weight": gaussian(streams_of[10], (D, D), D ** -0.5, 0.25),
        "ffn_gate_bias": gaussian(streams_of[11], (D,), 1.0, 4.0, (), jnp.float32),
        "first_gain": jnp.clip(1.0 + 0.1 * jax.random.normal(streams_of[12], (D,), jnp.float32), 0.5, 1.5),
        "first_shift": gaussian(streams_of[13], (D,), 0.5, 3.0, (), jnp.float32),
        "second_gain": jnp.clip(1.0 + 0.1 * jax.random.normal(streams_of[14], (D,), jnp.float32), 0.5, 1.5),
        "second_shift": gaussian(streams_of[15], (D,), 0.5, 3.0, (), jnp.float32),
        "row_kind": draw_row_kind(jax.random.fold_in(streams_of[18], 71), 0),
        "block_order": draw_block_order(jax.random.fold_in(streams_of[18], 71), 0),
    }


@jax.custom_vjp
def low(v):
    return lax.optimization_barrier(v.astype(jnp.bfloat16)).astype(jnp.float32)

@jax.custom_vjp
def low_back(v):
    return v

def low_keep(v):
    return (low(v), None)

def low_pass(kept, grad):
    return (grad,)

def back_keep(v):
    return (v, None)

def back_low(kept, grad):
    return (low(grad),)
low.defvjp(low_keep, low_pass)
low_back.defvjp(back_keep, back_low)
NEG = -1e+30
EPS = 1e-05
HIGH = lax.Precision.HIGHEST

def layer_norm(values, norm_gain, norm_shift):
    average = lax.optimization_barrier(jnp.mean(values, axis=-1, keepdims=True))
    centred = values - average
    variance = lax.optimization_barrier(jnp.mean(centred * centred, axis=-1, keepdims=True))
    return centred * lax.rsqrt(variance + EPS) * norm_gain + norm_shift

def place_table(order_rows, kind_rows, row_start, row_count, long_len, half_len):
    row_index = row_start + jnp.arange(row_count, dtype=jnp.int32)
    slot_index = row_index // half_len
    onehot = (slot_index[:, None] == jnp.arange(order_rows.shape[-1], dtype=jnp.int32)[None, :]).astype(jnp.int32)
    chosen = lax.optimization_barrier(jnp.sum(order_rows[:, None, :] * onehot[None, :, :], axis=-1))
    position = chosen * half_len + row_index % half_len
    document = jnp.where(kind_rows[:, None] == 2, (position >= long_len // 2).astype(jnp.int32), 0)
    return (position, document)

def matrix_product(left, right):
    return jnp.dot(left, right, precision=HIGH, preferred_element_type=jnp.float32)

def buffer_layer(weights, pieces):
    query_weight, key_weight, value_weight, output_weight, attn_gate_weight, attn_gate_bias, up_weight, down_weight, ffn_gate_weight, ffn_gate_bias, first_gain, first_shift, second_gain, second_shift = weights
    buffer_rows, buffer_kind, order_row = pieces
    half_len = LONG // (2 * N_SEQ)
    score_scale = 1.0 / math.sqrt(HD)
    normed_one = low(layer_norm(buffer_rows, first_gain, first_shift))
    query_rows = low_back(low(matrix_product(normed_one, query_weight))).reshape(LONG, H, HD)
    key_rows = low_back(low(matrix_product(normed_one, key_weight))).reshape(LONG, H, HD)
    value_rows = low_back(low(matrix_product(normed_one, value_weight))).reshape(LONG, H, HD)
    attn_gate = jax.nn.sigmoid(low_back(matrix_product(normed_one, attn_gate_weight) + attn_gate_bias))
    place_all, doc_all = place_table(order_row[None, :], buffer_kind[None], 0, LONG, LONG, half_len)
    place_all = place_all[0]
    doc_all = doc_all[0]
    query_span = 512 if LONG % 512 == 0 else LONG
    blocks = LONG // query_span

    def attend_block(block_pieces):
        block_query, block_place, block_doc = block_pieces
        raw_scores = low_back(jnp.einsum('qhd,khd->hqk', block_query, key_rows, precision=HIGH) * score_scale)
        allowed = ((place_all[None, :] <= block_place[:, None]) & (doc_all[None, :] == block_doc[:, None]))[None]
        masked = jnp.where(allowed, raw_scores, NEG)
        top_score = lax.optimization_barrier(jnp.max(masked, axis=-1, keepdims=True))
        exp_terms = jnp.where(allowed, jnp.exp(masked - top_score), 0.0)
        prob_low = low(exp_terms / lax.optimization_barrier(jnp.sum(exp_terms, axis=-1, keepdims=True)))
        return jnp.einsum('hqk,khd->qhd', prob_low, value_rows, precision=HIGH)
    attended = lax.map(jax.checkpoint(attend_block), (query_rows.reshape(blocks, query_span, H, HD), place_all.reshape(blocks, query_span), doc_all.reshape(blocks, query_span)))
    attended = low_back(low(attended.reshape(LONG, D)))
    branch_attn = low_back(matrix_product(attended, output_weight))
    middle = buffer_rows + attn_gate * (branch_attn - buffer_rows)
    normed_two = low(layer_norm(middle, second_gain, second_shift))
    up_pre = low_back(matrix_product(normed_two, up_weight))
    hidden = low(jax.nn.gelu(up_pre))
    branch_ffn = low_back(matrix_product(hidden, down_weight))
    ffn_gate = jax.nn.sigmoid(low_back(matrix_product(normed_two, ffn_gate_weight) + ffn_gate_bias))
    return middle + ffn_gate * (branch_ffn - middle)

def whole_layer(tokens_full, weights, row_kind, block_order):
    per_buffer = jnp.transpose(tokens_full, (1, 0, 2))
    saved_layer = jax.checkpoint(buffer_layer)

    def per_step(pieces):
        return saved_layer(weights, pieces)
    outputs = lax.map(per_step, (per_buffer, row_kind, block_order))
    return jnp.transpose(outputs, (1, 0, 2))

def reference(tokens, cotangent, query_weight, key_weight, value_weight, output_weight, attn_gate_weight, attn_gate_bias, up_weight, down_weight, ffn_gate_weight, ffn_gate_bias, first_gain, first_shift, second_gain, second_shift, row_kind, block_order):
    weights = (query_weight.astype(jnp.float32), key_weight.astype(jnp.float32), value_weight.astype(jnp.float32), output_weight.astype(jnp.float32), attn_gate_weight.astype(jnp.float32), attn_gate_bias.astype(jnp.float32), up_weight.astype(jnp.float32), down_weight.astype(jnp.float32), ffn_gate_weight.astype(jnp.float32), ffn_gate_bias.astype(jnp.float32), first_gain.astype(jnp.float32), first_shift.astype(jnp.float32), second_gain.astype(jnp.float32), second_shift.astype(jnp.float32))

    def layer_of(tokens_in, weights_in):
        return whole_layer(tokens_in, weights_in, row_kind, block_order)
    output, pullback = jax.vjp(layer_of, tokens.astype(jnp.float32), weights)
    tokens_grad, grads = pullback(cotangent.astype(jnp.float32))
    return (output.astype(jnp.bfloat16), tokens_grad.astype(jnp.bfloat16), grads[0], grads[1], grads[2], grads[3], grads[4], grads[5], grads[6], grads[7], grads[8], grads[9], grads[10], grads[11], grads[12], grads[13])
```

```python
import functools
import math
from types import SimpleNamespace

import jax
import jax.numpy as jnp
from jax import lax
from jax.experimental import pallas as pl
from jax.experimental.pallas import tpu as pltpu
from jax.sharding import PartitionSpec as P

H = 8
HD = 64
NEG = -1e30
EPS = 1e-05
MESH = pl.DeviceIdType.MESH
F32 = jnp.float32
BF16 = jnp.bfloat16
LANES = 128


def dot(a, b):
    return jnp.dot(a, b, preferred_element_type=F32)


def dot_nt(a, b):
    return lax.dot_general(a, b, (((1,), (1,)), ((), ())), preferred_element_type=F32)


def dot_tn(a, b):
    return lax.dot_general(a, b, (((0,), (0,)), ((), ())), preferred_element_type=F32)


def log2(value):
    return value.bit_length() - 1


def sizes(n, nd, rows, buffers, features, hidden):
    c = SimpleNamespace(n=n, nd=nd, L=rows, B=buffers, D=features, FF=hidden)
    c.T = rows * buffers
    c.N = rows * n
    c.HB = rows // 2
    c.G = n // buffers
    c.hpd = H // c.G
    c.W = c.hpd * HD
    c.QB = min(256, c.N // 2)
    c.NB = c.N // c.QB
    c.HALF = c.NB // 2
    c.FC = 512
    c.NC = hidden // c.FC
    c.LP = features // LANES
    unit = 16 * n * nd
    c.rows_a = hidden * c.LP
    c.rows_b = (hidden // LANES) * features
    c.rows_c = -(-(3 * features * c.LP) // unit) * unit
    c.used_c = 3 * features * c.LP
    c.np3 = -(-(3 * c.W) // LANES)
    c.rows_q = c.np3 * features
    c.seq_bits = log2(n)
    c.dp_bits = log2(nd)
    c.remotes = 10 * n + 2 * nd + 10 * (c.seq_bits + c.dp_bits)
    c.credits = 4 * (c.seq_bits + c.dp_bits)
    c.locals = 20 + c.NC * c.LP + hidden // LANES + 3 * c.LP + 3 * c.G
    return c


def scratch(c):
    v = pltpu.VMEM
    spaces = dict(
        tok=v((c.L, c.B * c.D), BF16),
        cot=v((c.L, c.B * c.D), BF16),
        win=v((3, c.D, LANES), BF16),
        wqkv=v((c.D, 3 * c.W), BF16),
        wg=v((c.D, c.D), BF16),
        wo=v((c.D, c.D), BF16),
        wup=v((c.D, c.FF), BF16),
        wdn=v((c.FF, c.D), BF16),
        wfg=v((c.D, c.D), BF16),
        n1=v((c.B, 2, c.HB, c.D), BF16),
        gat=v((c.n, 2, c.HB, c.D), BF16),
        nsrt=v((c.N // 2, c.D), BF16),
        qkvst=v((2 * c.n, c.HB, 3 * c.W), BF16),
        q=v((c.hpd, c.N, HD), BF16),
        k=v((c.hpd, c.N, HD), BF16),
        v=v((c.hpd, c.N, HD), BF16),
        do=v((c.hpd, c.N, HD), BF16),
        qT=v((c.W, c.N), BF16),
        vT=v((c.W, c.N), BF16),
        doT=v((c.W, c.N), BF16),
        oT=v((c.W, c.N), F32),
        dqT=v((c.W, c.N), F32),
        lseA=v((c.hpd, 1, c.N), F32),
        lseB=v((c.hpd, 1, c.N), F32),
        odot=v((c.hpd, 1, c.N), F32),
        osrt=v((2 * c.n, c.HB, c.W), BF16),
        ou=v((2 * c.n, c.HB, c.W), BF16),
        orr=v((2 * c.n, c.HB, c.W), BF16),
        dor=v((2 * c.n, c.HB, c.W), BF16),
        att=v((c.T, c.D), BF16),
        ag=v((c.T, c.D), F32),
        mid=v((c.T, c.D), F32),
        bamx=v((c.T, c.D), F32),
        acc=v((c.T, c.D), F32),
        dxr=v((c.T, c.D), F32),
        n2=v((c.T, c.D), BF16),
        n2T=v((c.D, c.T), BF16),
        gp=v((c.NC, c.T, c.FC), F32),
        hid=v((c.NC, c.T, c.FC), BF16),
        dffn=v((c.T, c.D), BF16),
        dpre=v((c.T, c.D), BF16),
        datt=v((c.T, c.D), BF16),
        dapre=v((c.T, c.D), BF16),
        wacc=v((c.D, 3 * c.W), F32),
        dns=v((2 * c.n, c.HB, c.D), BF16),
        sibs=v((2, c.n // 2, c.HB, c.D), BF16),
        sibr=v((2, c.n // 2, c.HB, c.D), BF16),
        dnr=v((c.n // 2, 2, c.HB, c.D), BF16),
        fa=v((c.rows_a, LANES), BF16),
        fb=v((c.rows_b, LANES), BF16),
        fc=v((c.rows_c, LANES), BF16),
        fq=v((c.rows_q, LANES), BF16),
        sa=v((c.rows_a, LANES), BF16),
        sb=v((c.rows_b, LANES), BF16),
        sc=v((c.rows_c, LANES), BF16),
        sq=v((c.rows_q, LANES), BF16),
        resq=v((c.G, c.rows_q, LANES), BF16),
        gqkv=v((3, c.D, c.D) if c.W < LANES else (3, 16, LANES), BF16),
        mixst=v((c.L, c.B * c.D), BF16),
        sm=v((8, c.D), F32),
        smr=v((c.n, 8, c.D), F32),
        smd=v((8, c.D), F32),
        smdr=v((c.nd, 8, c.D), F32),
        sm2=v((8, c.D), F32),
        sm2r=v((c.n, 8, c.D), F32),
        sm2d=v((8, c.D), F32),
        sm2dr=v((c.nd, 8, c.D), F32),
        ss=pltpu.SemaphoreType.DMA((c.remotes,)),
        rs=pltpu.SemaphoreType.DMA((c.remotes,)),
        ls=pltpu.SemaphoreType.DMA((c.locals,)),
        free=pltpu.SemaphoreType.REGULAR((c.credits,)),
    )
    return spaces


IN_NAMES = [
    "i_order",
    "i_kind",
    "i_bg",
    "i_bfg",
    "i_g1",
    "i_s1",
    "i_g2",
    "i_s2",
    "i_tok",
    "i_cot",
    "i_wq",
    "i_wk",
    "i_wv",
    "i_wo",
    "i_wg",
    "i_wup",
    "i_wdn",
    "i_wfg",
]
OUT_NAMES = [
    "o_mix",
    "o_tok",
    "o_q",
    "o_k",
    "o_v",
    "o_out",
    "o_ag",
    "o_up",
    "o_dn",
    "o_fg",
    "o_sm",
    "o_sm2",
]


def norm_stats(values):
    average = jnp.mean(values, axis=-1, keepdims=True)
    centred = values - average
    variance = jnp.mean(centred * centred, axis=-1, keepdims=True)
    scale = lax.rsqrt(variance + EPS)
    return centred * scale, scale


def norm_back(grad, gain, normal, scale):
    e = grad * gain
    return scale * (
        e
        - jnp.mean(e, axis=-1, keepdims=True)
        - normal * jnp.mean(e * normal, axis=-1, keepdims=True)
    )


def kernel(c, names, *refs):
    r = SimpleNamespace(**dict(zip(names, refs)))
    n, nd, L, B, D, T, N, HB, G, W = c.n, c.nd, c.L, c.B, c.D, c.T, c.N, c.HB, c.G, c.W
    QB, NB, HALF, FC, NC = c.QB, c.NB, c.HALF, c.FC, c.NC
    s = lax.axis_index("seq")
    d = lax.axis_index("dp")
    b = s // G
    g = s % G
    core = s % 2
    pair = s // 2
    pairs = n // 2
    sibling = s + 1 - 2 * core
    count = dict(remote=0, local=0, credit=0)

    def remote(src, dst, device):
        i = count["remote"]
        assert i < c.remotes
        count["remote"] += 1
        copy = pltpu.make_async_remote_copy(
            src_ref=src,
            dst_ref=dst,
            send_sem=r.ss.at[i],
            recv_sem=r.rs.at[i],
            device_id=device,
            device_id_type=MESH,
        )
        copy.start()
        return copy

    def local(src, dst):
        i = count["local"]
        assert i < c.locals
        count["local"] += 1
        copy = pltpu.make_async_copy(src, dst, r.ls.at[i])
        copy.start()
        return copy

    def at_seq(t):
        return {"seq": t, "dp": d}

    def at_dp(t):
        return {"seq": s, "dp": t}

    get_tok = local(r.i_tok, r.tok)
    window = pl.multiple_of((g * W) // LANES * LANES, LANES)
    get_win = [
        local(ref.at[:, pl.ds(window, LANES)], r.win.at[i])
        for i, ref in enumerate((r.i_wq, r.i_wk, r.i_wv))
    ]
    get_wg = local(r.i_wg, r.wg)
    get_cot = local(r.i_cot, r.cot)
    get_wo = local(r.i_wo, r.wo)
    get_wup = local(r.i_wup, r.wup)
    get_wfg = local(r.i_wfg, r.wfg)
    get_wdn = local(r.i_wdn, r.wdn)
    barrier = pltpu.get_barrier_semaphore()
    for k in range(1, n):
        pl.semaphore_signal(barrier, inc=1, device_id=at_seq((s + k) % n), device_id_type=MESH)
    for k in range(1, nd):
        pl.semaphore_signal(barrier, inc=1, device_id=at_dp((d + k) % nd), device_id_type=MESH)

    get_tok.wait()

    def inputs():
        return jnp.concatenate(
            [r.tok[:, i * D : (i + 1) * D].astype(F32) for i in range(B)], axis=0
        )

    x = inputs()
    normal, _ = norm_stats(x)
    n1 = (normal * r.i_g1[...] + r.i_s1[...]).astype(BF16)
    for i in range(B):
        r.n1[i] = n1[i * L : (i + 1) * L].reshape(2, HB, D)

    pl.semaphore_wait(barrier, n - 1 + nd - 1)

    def slot(t):
        return pl.ds(2 * t, 2)

    rows_of = r.n1
    gather = {}
    for k in range(1, pairs):
        t = 2 * ((pair + k) % pairs) + core
        gather[k] = remote(rows_of.at[t // G], r.gat.at[s], at_seq(t))
    relay = {0: remote(rows_of.at[b], r.gat.at[s], at_seq(sibling))}
    r.gat[s] = r.n1[b]

    for copy in get_win:
        copy.wait()
    if W == LANES:
        wqkv = jnp.concatenate([r.win[0], r.win[1], r.win[2]], axis=1)
    else:
        upper = (g * W) % LANES != 0
        wqkv = jnp.concatenate(
            [jnp.where(upper, r.win[i][:, W:], r.win[i][:, :W]) for i in range(3)], axis=1
        )
    r.wqkv[...] = wqkv
    get_wg.wait()
    r.ag[...] = jax.nn.sigmoid(dot(n1, r.wg[...]) + r.i_bg[...])

    order = [r.i_order[b, i] for i in range(2 * n)]
    inverse = []
    for p in range(2 * n):
        found = jnp.int32(0)
        for i in range(2 * n):
            found = jnp.where(order[i] == p, i, found)
        inverse.append(found)
    low_block = [jnp.minimum(order[2 * t], order[2 * t + 1]) for t in range(n)]
    top_block = [jnp.maximum(order[2 * t], order[2 * t + 1]) for t in range(n)]
    split = jnp.where(r.i_kind[b] == 2, F32(NEG), F32(0.0))

    def project(t):
        out = dot(r.gat[t].reshape(L, D), r.wqkv[...])
        r.qkvst[slot(t)] = (
            jnp.concatenate([out[:, :W] * (1.0 / math.sqrt(HD)), out[:, W:]], axis=1)
            .astype(BF16)
            .reshape(2, HB, 3 * W)
        )

    project(s)
    for k in range(1, pairs):
        gather[k].wait()
        u = 2 * ((pair + pairs - k) % pairs) + core
        relay[k] = remote(r.gat.at[u], r.gat.at[u], at_seq(sibling))
        project(u)
    for k in range(pairs):
        relay[k].wait()
        project(2 * ((pair + pairs - k) % pairs) + 1 - core)

    per = QB // HB
    for i in range(NB):
        at = slice(i * QB, (i + 1) * QB)
        block = jnp.concatenate([r.qkvst[inverse[i * per + m]] for m in range(per)], axis=0)
        for j, (ref, ref_t) in enumerate(((r.q, r.qT), (r.k, None), (r.v, r.vT))):
            part = block[:, j * W : (j + 1) * W]
            for h in range(c.hpd):
                ref[h, at, :] = part[:, h * HD : (h + 1) * HD]
            if ref_t is not None:
                ref_t[:, at] = part.T

    keys_at = lax.broadcasted_iota(jnp.int32, (QB, QB), 0)
    queries_at = lax.broadcasted_iota(jnp.int32, (QB, QB), 1)
    causal = keys_at <= queries_at

    def attend(blocks):
        def head(h, carry):
            hr = pl.ds(pl.multiple_of(h * HD, HD), HD)
            for i in blocks:
                at = slice(i * QB, (i + 1) * QB)
                nk = (i + 1) * QB
                scores = dot(r.k[h, 0:nk, :], r.qT[hr, at])
                diagonal = jnp.where(causal, scores[i * QB :], NEG)
                top = jnp.max(diagonal, axis=0, keepdims=True)
                low_rows = N // 2 if i >= HALF else 0
                low = scores[:low_rows] if low_rows else None
                middle = scores[low_rows : i * QB] if i * QB > low_rows else None
                if middle is not None:
                    top = jnp.maximum(top, jnp.max(middle, axis=0, keepdims=True))
                if low is not None:
                    top = jnp.maximum(top, jnp.max(low, axis=0, keepdims=True) + split)
                terms = []
                if low is not None:
                    terms.append(jnp.exp(low - (top - split)))
                if middle is not None:
                    terms.append(jnp.exp(middle - top))
                terms.append(jnp.exp(diagonal - top))
                total = sum(jnp.sum(t, axis=0, keepdims=True) for t in terms)
                weights = jnp.concatenate([t.astype(BF16) for t in terms], axis=0)
                out = dot(r.vT[hr, 0:nk], weights)
                r.oT[hr, at] = out * (1.0 / total)
                lse = top + jnp.log(total)
                r.lseB[h, :, at] = lse
                r.lseA[h, :, at] = lse - split if i >= HALF else lse
            return carry

        lax.fori_loop(0, c.hpd, head, 0)
        for i in blocks:
            r.osrt[i * per : (i + 1) * per] = (
                r.oT[:, i * QB : (i + 1) * QB].astype(BF16).T.reshape(per, HB, W)
            )

    def send_rows(which, blocks):
        for t in range(n):
            r.ou[2 * t + which] = r.osrt[blocks[t]]
        copies = []
        for k in range(1, n):
            t = (s + k) % n
            copies.append(remote(r.ou.at[2 * t + which], r.orr.at[2 * s + which], at_seq(t)))
        r.orr[2 * s + which] = r.ou[2 * s + which]
        return copies

    attend(range(HALF, NB))
    going = send_rows(1, top_block)
    attend(range(HALF))
    going += send_rows(0, low_block)

    get_wo.wait()
    get_wup.wait()
    get_wfg.wait()
    get_wdn.wait()
    get_cot.wait()
    own = [(r.i_order[i, 2 * s], r.i_order[i, 2 * s + 1]) for i in range(B)]
    which_half = [
        (jnp.where(a > z, 1, 0), jnp.where(a > z, 0, 1)) for a, z in own
    ]
    for copy in going:
        copy.wait()
    for i in range(B):
        for m in range(2):
            for j in range(G):
                r.att[i * L + m * HB : i * L + (m + 1) * HB, j * W : (j + 1) * W] = r.orr[
                    2 * (i * G + j) + which_half[i][m]
                ]
    x = inputs()
    branch = dot(r.att[...], r.wo[...]) - x
    r.bamx[...] = branch
    middle = x + r.ag[...] * branch
    r.mid[...] = middle
    normal, scale = norm_stats(middle)
    n2 = (normal * r.i_g2[...] + r.i_s2[...]).astype(BF16)
    r.n2[...] = n2
    r.n2T[...] = n2.T

    slope = math.sqrt(2.0 / math.pi)
    r.acc[...] = jnp.zeros((T, D), F32)

    def forward_chunk(j, carry):
        cols = pl.ds(pl.multiple_of(j * FC, FC), FC)
        u = dot(r.n2[...], r.wup[:, cols])
        square = u * u
        t = jnp.tanh(slope * u * (1.0 + 0.044715 * square))
        half = 0.5 * (1.0 + t)
        hidden = (u * half).astype(BF16)
        r.hid[j] = hidden
        r.gp[j] = half + 0.5 * u * (1.0 - t * t) * (slope * (1.0 + 3 * 0.044715 * square))
        r.acc[...] += dot(hidden, r.wdn[cols, :])
        return carry

    lax.fori_loop(0, NC, forward_chunk, 0)
    gate = jax.nn.sigmoid(dot(r.n2[...], r.wfg[...]) + r.i_bfg[...])
    middle = r.mid[...]
    apart = r.acc[...] - middle
    mixed = (middle + gate * apart).astype(BF16)
    for i in range(B):
        r.mixst[:, i * D : (i + 1) * D] = mixed[i * L : (i + 1) * L]
    put_mix = local(r.mixst, r.o_mix)
    grad = jnp.concatenate([r.cot[:, i * D : (i + 1) * D].astype(F32) for i in range(B)], axis=0)
    r.dffn[...] = (grad * gate).astype(BF16)
    d_pre = (grad * apart * gate * (1.0 - gate)).astype(BF16)
    r.dpre[...] = d_pre
    r.sm[0:1, :] = jnp.sum(d_pre.astype(F32), axis=0, keepdims=True)
    r.dxr[...] = grad * (1.0 - gate)
    r.acc[...] = dot_nt(d_pre, r.wfg[...])

    def backward_chunk(j, carry):
        cols = pl.ds(pl.multiple_of(j * FC, FC), FC)
        d_hidden = dot_nt(r.dffn[...], r.wdn[cols, :])
        d_up = (d_hidden * r.gp[j]).astype(BF16)
        r.gp[j] = d_up.astype(F32)
        r.acc[...] += dot_nt(d_up, r.wup[:, cols])
        return carry

    lax.fori_loop(0, NC, backward_chunk, 0)
    d_norm = r.acc[...]
    normal, scale = norm_stats(r.mid[...])
    r.sm[1:2, :] = jnp.sum(d_norm * normal, axis=0, keepdims=True)
    r.sm[2:3, :] = jnp.sum(d_norm, axis=0, keepdims=True)
    d_middle = r.dxr[...] + norm_back(d_norm, r.i_g2[...], normal, scale)
    gate = r.ag[...]
    d_att = (d_middle * gate).astype(BF16)
    d_attn_pre = (d_middle * r.bamx[...] * gate * (1.0 - gate)).astype(BF16)
    r.datt[...] = d_att
    r.dapre[...] = d_attn_pre
    r.sm[3:4, :] = jnp.sum(d_attn_pre.astype(F32), axis=0, keepdims=True)
    r.sm[4:8, :] = jnp.zeros((4, D), F32)
    r.dxr[...] = d_middle * (1.0 - gate)
    d_o = dot_nt(d_att, r.wo[...]).astype(BF16)
    for i in range(B):
        for j in range(G):
            r.ou[2 * (i * G + j) : 2 * (i * G + j) + 2] = d_o[
                i * L : (i + 1) * L, j * W : (j + 1) * W
            ].reshape(2, HB, W)
    back = []
    for k in range(1, n):
        t = (s + k) % n
        back.append(remote(r.ou.at[slot(t)], r.dor.at[slot(s)], at_seq(t)))
    r.dor[slot(s)] = r.ou[slot(s)]

    def partner(axis, bit):
        index = s if axis == "seq" else d
        mine = index // 2**bit % 2
        there = index + (1 - 2 * mine) * 2**bit
        return mine, at_seq(there) if axis == "seq" else at_dp(there)

    def add_rows(ref, start, slots, base, length):
        step = math.gcd(length, 512)

        def body(i, carry):
            at = pl.ds(pl.multiple_of(start + i * step, 16), step)
            other = slots[pl.ds(pl.multiple_of(base + i * step, 16), step), :]
            ref[at, :] = (ref[at, :].astype(F32) + other.astype(F32)).astype(BF16)
            return carry

        lax.fori_loop(0, length // step, body, 0)

    def all_reduce(ref, slots, rows, bits):
        start, length, base = jnp.int32(0), rows, 0
        trail = []
        for axis, bit in bits:
            half = length // 2
            mine, device = partner(axis, bit)
            keep = pl.multiple_of(start + mine * half, 16)
            give = pl.multiple_of(start + (1 - mine) * half, 16)
            copy = remote(ref.at[pl.ds(give, half)], slots.at[pl.ds(base, half)], device)
            yield
            copy.wait()
            credit = r.free.at[count["credit"]]
            count["credit"] += 1
            pl.semaphore_signal(credit, inc=1, device_id=device, device_id_type=MESH)
            add_rows(ref, keep, slots, base, half)
            trail.append((keep, half, device, credit))
            start, length, base = keep, half, base + half
        for keep, half, device, credit in reversed(trail):
            at = pl.ds(keep, half)
            pl.semaphore_wait(credit, 1)
            copy = remote(ref.at[at], ref.at[at], device)
            yield
            copy.wait()

    def reduce_small(own_ref, slots, dp_ref, dp_slots, out_ref):
        copies = []
        for k in range(1, n):
            copies.append(remote(own_ref, slots.at[s], at_seq((s + k) % n)))
        slots[s] = own_ref[...]
        yield
        for copy in copies:
            copy.wait()
        dp_ref[...] = sum(slots[i] for i in range(n))
        copies = []
        for k in range(1, nd):
            copies.append(remote(dp_ref, dp_slots.at[d], at_dp((d + k) % nd)))
        dp_slots[d] = dp_ref[...]
        yield
        for copy in copies:
            copy.wait()
        out_ref[...] = sum(dp_slots[i] for i in range(nd))

    running = []

    def tick():
        for job in list(running):
            if next(job, "over") == "over":
                running.remove(job)

    seq = [("seq", i) for i in range(c.seq_bits)]
    dps = [("dp", i) for i in range(c.dp_bits)]
    order_a = seq + dps
    order_b = seq[:1] + seq[1:][::-1] + dps
    order_c = seq[:1] + dps + seq[1:]

    running.append(reduce_small(r.sm, r.smr, r.smd, r.smdr, r.o_sm))

    def down_chunk(j, carry):
        part = dot_tn(r.hid[j], r.dffn[...]).astype(BF16)
        for i in range(c.LP):
            at = pl.ds(pl.multiple_of((j * c.LP + i) * FC, FC), FC)
            r.fa[at, :] = part[:, i * LANES : (i + 1) * LANES]
        return carry

    def up_chunk(j, carry):
        part = dot(r.n2T[...], r.gp[j].astype(BF16)).astype(BF16)
        for i in range(FC // LANES):
            at = pl.ds(pl.multiple_of((j * (FC // LANES) + i) * D, D), D)
            r.fb[at, :] = part[:, i * LANES : (i + 1) * LANES]
        return carry

    lax.fori_loop(0, NC, down_chunk, 0)
    running.append(all_reduce(r.fa, r.sa, c.rows_a, order_a))
    tick()
    lax.fori_loop(0, NC, up_chunk, 0)
    running.append(all_reduce(r.fb, r.sb, c.rows_b, order_b))
    tick()
    for j, part in enumerate(
        (
            dot_tn(r.att[...], r.datt[...]),
            dot_tn(r.n1[...].reshape(T, D), r.dapre[...]),
            dot(r.n2T[...], r.dpre[...]),
        )
    ):
        part = part.astype(BF16)
        for i in range(c.LP):
            at = (j * c.LP + i) * D
            r.fc[at : at + D, :] = part[:, i * LANES : (i + 1) * LANES]
    if c.rows_c > c.used_c:
        r.fc[c.used_c :, :] = jnp.zeros((c.rows_c - c.used_c, LANES), BF16)
    running.append(all_reduce(r.fc, r.sc, c.rows_c, order_c))
    tick()
    r.acc[...] = dot_nt(r.dapre[...], r.wg[...])

    for copy in back:
        copy.wait()
    for i in range(NB):
        at = slice(i * QB, (i + 1) * QB)
        block = jnp.concatenate([r.dor[inverse[i * per + m]] for m in range(per)], axis=0)
        for h in range(c.hpd):
            r.do[h, at, :] = block[:, h * HD : (h + 1) * HD]
        turned = block.T
        r.doT[:, at] = turned
        product = turned.astype(F32) * r.oT[:, at]
        for h in range(c.hpd):
            r.odot[h, :, at] = jnp.sum(product[h * HD : (h + 1) * HD], axis=0, keepdims=True)
    tick()

    def backward_block(j):
        def head(h, carry):
            hr = pl.ds(pl.multiple_of(h * HD, HD), HD)
            at = slice(j * QB, (j + 1) * QB)
            keys, values = r.k[h, at, :], r.v[h, at, :]
            keys_t = keys.T
            lse_ref = r.lseA if j < HALF else r.lseB
            weights, slopes = [], []
            for i in range(j, NB):
                to = slice(i * QB, (i + 1) * QB)
                scores = dot(keys, r.qT[hr, to])
                p = jnp.exp(scores - lse_ref[h, :, to])
                if i == j:
                    p = jnp.where(causal, p, 0.0)
                dp = dot(values, r.doT[hr, to])
                ds = (p * (dp - r.odot[h, :, to])).astype(BF16)
                weights.append(p.astype(BF16))
                slopes.append(ds)
                part = dot(keys_t, ds)
                if j == 0:
                    r.dqT[hr, to] = part
                else:
                    r.dqT[hr, to] += part
            weights = jnp.concatenate(weights, axis=1)
            slopes = jnp.concatenate(slopes, axis=1)
            r.v[h, at, :] = dot(weights, r.do[h, j * QB :, :]).astype(BF16)
            r.k[h, at, :] = dot(slopes, r.q[h, j * QB :, :]).astype(BF16)
            return carry

        lax.fori_loop(0, c.hpd, head, 0)

    def finish_half(which, blocks):
        for i in blocks:
            at = slice(i * QB, (i + 1) * QB)
            parts = [(r.dqT[:, at] * (1.0 / math.sqrt(HD))).astype(BF16).T]
            parts += [r.k[h, at, :] for h in range(c.hpd)]
            parts += [r.v[h, at, :] for h in range(c.hpd)]
            rows = jnp.concatenate(parts, axis=1)
            r.qkvst[i * per : (i + 1) * per] = rows.reshape(per, HB, 3 * W)
            r.dns[i * per : (i + 1) * per] = (
                dot_nt(rows, r.wqkv[...]).astype(BF16).reshape(per, HB, D)
            )
        table = top_block if which else low_block

        def pick(m, parity):
            return jnp.where(parity == 0, table[2 * m], table[2 * m + 1])

        for m in range(pairs):
            r.sibs[which, m] = r.dns[pick(m, 1 - core)]
        return remote(r.sibs.at[which], r.sibr.at[which], at_seq(sibling)), pick

    def pass_on(which, copy, pick):
        copy.wait()
        for m in range(pairs):
            r.sibs[which, m] = (
                r.dns[pick(m, core)].astype(F32) + r.sibr[which, m].astype(F32)
            ).astype(BF16)
        copies = []
        for k in range(1, pairs):
            m = (pair + k) % pairs
            copies.append(
                remote(r.sibs.at[which, m], r.dnr.at[pair, which], at_seq(2 * m + core))
            )
        r.dnr[pair, which] = r.sibs[which, pair]
        return copies

    for j in range(HALF):
        backward_block(j)
        tick()
    low_copy, low_pick = finish_half(0, range(HALF))

    def weight_part(which):
        for i in range(n):
            at = inverse[which * n + i]
            r.nsrt[i * HB : (i + 1) * HB, :] = r.gat[at // 2, at % 2]
        return dot_tn(
            r.nsrt[...], r.qkvst[which * n : (which + 1) * n].reshape(N // 2, 3 * W)
        )

    r.wacc[...] = weight_part(0)
    arriving = pass_on(0, low_copy, low_pick)
    for j in range(HALF, NB):
        backward_block(j)
        tick()
    top_copy, top_pick = finish_half(1, range(HALF, NB))
    part = (r.wacc[...] + weight_part(1)).astype(BF16)
    if c.np3 * LANES > 3 * W:
        part = jnp.concatenate([part, jnp.zeros((D, c.np3 * LANES - 3 * W), BF16)], axis=1)
    for i in range(c.np3):
        r.fq[i * D : (i + 1) * D, :] = part[:, i * LANES : (i + 1) * LANES]
    arriving += pass_on(1, top_copy, top_pick)

    group_bits = log2(G)

    def heads_reduce():
        yield from all_reduce(
            r.fq, r.sq, c.rows_q, [("seq", i) for i in range(group_bits, c.seq_bits)] + dps
        )
        r.resq[g] = r.fq[...]
        held = [g]
        for bit in reversed(range(group_bits)):
            mine, device = partner("seq", bit)
            copies = [remote(r.resq.at[i], r.resq.at[i], device) for i in held]
            yield
            for copy in copies:
                copy.wait()
            held = held + [i + (1 - 2 * mine) * 2**bit for i in held]

    running.append(heads_reduce())
    tick()

    for copy in arriving:
        copy.wait()
    parts = []
    for i in range(B):
        for m in range(2):
            parts.append(
                sum(
                    r.dnr[i * (G // 2) + j, which_half[i][m]].astype(F32) for j in range(G // 2)
                )
            )
    d_norm = jnp.concatenate(parts, axis=0) + r.acc[...]
    normal, scale = norm_stats(inputs())
    r.sm2[0:1, :] = jnp.sum(d_norm * normal, axis=0, keepdims=True)
    r.sm2[1:2, :] = jnp.sum(d_norm, axis=0, keepdims=True)
    r.sm2[2:8, :] = jnp.zeros((6, D), F32)
    running.append(reduce_small(r.sm2, r.sm2r, r.sm2d, r.sm2dr, r.o_sm2))
    tick()
    put_mix.wait()
    grads = (r.dxr[...] + norm_back(d_norm, r.i_g1[...], normal, scale)).astype(BF16)
    for i in range(B):
        r.mixst[:, i * D : (i + 1) * D] = grads[i * L : (i + 1) * L]
    puts = [local(r.mixst, r.o_tok)]
    while running:
        tick()

    for j in range(NC):
        for i in range(c.LP):
            at = (j * c.LP + i) * FC
            puts.append(
                local(
                    r.fa.at[at : at + FC],
                    r.o_dn.at[j * FC : (j + 1) * FC, i * LANES : (i + 1) * LANES],
                )
            )
    for i in range(c.FF // LANES):
        puts.append(
            local(r.fb.at[i * D : (i + 1) * D], r.o_up.at[:, i * LANES : (i + 1) * LANES])
        )
    for j, ref in enumerate((r.o_out, r.o_ag, r.o_fg)):
        for i in range(c.LP):
            at = (j * c.LP + i) * D
            puts.append(local(r.fc.at[at : at + D], ref.at[:, i * LANES : (i + 1) * LANES]))
    outs = (r.o_q, r.o_k, r.o_v)
    for i in range(G):
        if W == LANES:
            for j, ref in enumerate(outs):
                puts.append(
                    local(
                        r.resq.at[i, j * D : (j + 1) * D], ref.at[:, i * LANES : (i + 1) * LANES]
                    )
                )
            continue
        block = jnp.concatenate(
            [r.resq[i, m * D : (m + 1) * D, :] for m in range(c.np3)], axis=1
        )
        for j in range(3):
            r.gqkv[j, :, i * W : (i + 1) * W] = block[:, j * W : (j + 1) * W]
    if W < LANES:
        for j, ref in enumerate(outs):
            puts.append(local(r.gqkv.at[j], ref))
    for put in puts:
        put.wait()


def solution(mesh):
    n, nd = mesh.shape["seq"], mesh.shape["dp"]

    def local(
        tokens,
        cotangent,
        query_weight,
        key_weight,
        value_weight,
        output_weight,
        attn_gate_weight,
        attn_gate_bias,
        up_weight,
        down_weight,
        ffn_gate_weight,
        ffn_gate_bias,
        first_gain,
        first_shift,
        second_gain,
        second_shift,
        row_kind,
        block_order,
    ):
        L, B, D = tokens.shape
        FF = up_weight.shape[1]
        c = sizes(n, nd, L, B, D, FF)
        spaces = scratch(c)
        names = IN_NAMES + OUT_NAMES + list(spaces)
        smem = pl.BlockSpec(memory_space=pltpu.SMEM)
        vmem = pl.BlockSpec(memory_space=pltpu.VMEM)
        hbm = pl.BlockSpec(memory_space=pl.ANY)

        def shape(*dims, dtype=BF16):
            return jax.ShapeDtypeStruct(dims, dtype)

        def row(vector):
            return vector.reshape(1, -1)

        out = pl.pallas_call(
            functools.partial(kernel, c, names),
            out_shape=(
                shape(L, B * D),
                shape(L, B * D),
                shape(D, D),
                shape(D, D),
                shape(D, D),
                shape(D, D),
                shape(D, D),
                shape(D, FF),
                shape(FF, D),
                shape(D, D),
                shape(8, D, dtype=F32),
                shape(8, D, dtype=F32),
            ),
            in_specs=[smem] * 2 + [vmem] * 6 + [hbm] * 10,
            out_specs=(hbm,) * 10 + (vmem,) * 2,
            scratch_shapes=list(spaces.values()),
            compiler_params=pltpu.CompilerParams(
                collective_id=0, has_side_effects=True, vmem_limit_bytes=VMEM_BYTES
            ),
            name="layer",
        )(
            block_order,
            row_kind,
            row(attn_gate_bias),
            row(ffn_gate_bias),
            row(first_gain),
            row(first_shift),
            row(second_gain),
            row(second_shift),
            tokens.reshape(L, B * D),
            cotangent.reshape(L, B * D),
            query_weight,
            key_weight,
            value_weight,
            output_weight,
            attn_gate_weight,
            up_weight,
            down_weight,
            ffn_gate_weight,
        )
        mix, tok, dq, dk, dv, dout, dag, dup, ddn, dfg, small, small2 = out
        wide = [a.astype(F32) for a in (dq, dk, dv, dout, dag, dup, ddn, dfg)]
        return (
            mix.reshape(L, B, D),
            tok.reshape(L, B, D),
            wide[0],
            wide[1],
            wide[2],
            wide[3],
            wide[4],
            small[3],
            wide[5],
            wide[6],
            wide[7],
            small[0],
            small2[0],
            small2[1],
            small[1],
            small[2],
        )

    sharded = P("seq", "dp", None)
    return jax.shard_map(
        local,
        mesh=mesh,
        in_specs=(sharded, sharded) + (P(),) * 14 + (P("dp"), P("dp", None)),
        out_specs=(sharded, sharded) + (P(),) * 14,
        check_vma=False,
    )


VMEM_BYTES = 63 * 2**20
```

```python
import functools
import math
from types import SimpleNamespace

import jax
import jax.numpy as jnp
from jax import lax
from jax.experimental import pallas as pl
from jax.experimental.pallas import tpu as pltpu
from jax.sharding import PartitionSpec as P

H = 8
HD = 64
NEG = -1e30
EPS = 1e-05
MESH = pl.DeviceIdType.MESH
F32 = jnp.float32
BF16 = jnp.bfloat16
LANES = 128


def dot(a, b):
    return jnp.dot(a, b, preferred_element_type=F32)


def dot_nt(a, b):
    return lax.dot_general(a, b, (((1,), (1,)), ((), ())), preferred_element_type=F32)


def dot_tn(a, b):
    return lax.dot_general(a, b, (((0,), (0,)), ((), ())), preferred_element_type=F32)


def log2(value):
    return value.bit_length() - 1


def sizes(n, nd, rows, buffers, features, hidden):
    c = SimpleNamespace(n=n, nd=nd, L=rows, B=buffers, D=features, FF=hidden)
    c.T = rows * buffers
    c.N = rows * n
    c.HB = rows // 2
    c.G = n // buffers
    c.hpd = H // c.G
    c.W = c.hpd * HD
    c.QB = min(256, c.N // 2)
    c.QF = min(512, c.N // 2)
    c.NB = c.N // c.QB
    c.HALF = c.NB // 2
    c.FC = 512
    c.NC = hidden // c.FC
    c.LP = features // LANES
    unit = 16 * n * nd
    c.rows_a = hidden * c.LP
    c.rows_b = (hidden // LANES) * features
    c.rows_c = -(-(3 * features * c.LP) // unit) * unit
    c.used_c = 3 * features * c.LP
    c.np3 = -(-(3 * c.W) // LANES)
    c.rows_q = c.np3 * features
    c.seq_bits = log2(n)
    c.dp_bits = log2(nd)
    c.remotes = 10 * n + 2 * nd + 10 * (c.seq_bits + c.dp_bits)
    c.credits = 5 * (c.seq_bits + c.dp_bits)
    c.locals = 28 + c.NC * c.LP + hidden // LANES + 3 * c.LP + 3 * c.G
    return c


def scratch(c):
    v = pltpu.VMEM
    spaces = dict(
        tok=v((c.L, c.B, c.D), BF16),
        cot=v((c.L, c.B, c.D), BF16),
        xs=v((c.T, c.D), BF16),
        bg=v((1, c.D), F32),
        bfg=v((1, c.D), F32),
        g1=v((1, c.D), F32),
        s1=v((1, c.D), F32),
        g2=v((1, c.D), F32),
        s2=v((1, c.D), F32),
        win=v((3, c.D, LANES) if c.W < LANES else (3, 16, LANES), BF16),
        wqkv=v((c.D, 3 * c.W), BF16),
        wg=v((c.D, c.D), BF16),
        wo=v((c.D, c.D), BF16),
        wup=v((c.D, c.FF), BF16),
        wdn=v((c.FF, c.D), BF16),
        wfg=v((c.D, c.D), BF16),
        n1=v((c.B, 2, c.HB, c.D), BF16),
        gat=v((c.n, 2, c.HB, c.D), BF16),
        qkvst=v((2 * c.n, c.HB, 3 * c.W), BF16),
        q=v((c.N, c.W), BF16),
        k=v((c.hpd, c.N, c.W), BF16),
        v=v((c.hpd, c.N, c.W), BF16),
        do=v((2 * c.n, c.HB, c.W), BF16),
        kT=v((c.W, c.N), BF16),
        qT=v((c.W, c.N), BF16),
        vT=v((c.W, c.N), BF16),
        doT=v((c.W, c.N), BF16),
        oT=v((c.W, c.N), F32),
        dqT=v((c.W, c.N), F32),
        lseA=v((c.hpd, 1, c.N), F32),
        lseB=v((c.hpd, 1, c.N), F32),
        odot=v((c.hpd, 1, c.N), F32),
        ou=v((2 * c.n, c.HB, c.W), BF16),
        orr=v((2 * c.n, c.HB, c.W), BF16),
        dor=v((2 * c.n, c.HB, c.W), BF16),
        att=v((c.T, c.D), BF16),
        ag=v((c.T, c.D), F32),
        mid=v((c.T, c.D), F32),
        bamx=v((c.T, c.D), F32),
        acc=v((c.T, c.D), F32),
        dxr=v((c.T, c.D), F32),
        n2=v((c.T, c.D), BF16),
        n2T=v((c.D, c.T), BF16),
        gp=v((c.NC, c.T, c.FC), F32),
        hid=v((max(c.NC * c.T, c.N), c.FC), BF16),
        dffn=v((c.T, c.D), BF16),
        dpre=v((c.T, c.D), BF16),
        datt=v((c.T, c.D), BF16),
        dapre=v((c.T, c.D), BF16),
        wacc=v((c.D, 3 * c.W), F32),
        sibs=v((2, c.n // 2, c.HB, c.D), BF16),
        sibr=v((2, c.n // 2, c.HB, c.D), BF16),
        dnr=v((c.n // 2, 2, c.HB, c.D), BF16),
        fa=v((c.rows_a, LANES), BF16),
        fb=v((c.rows_b, LANES), BF16),
        fc=v((c.rows_c, LANES), BF16),
        fq=v((c.rows_q, LANES), BF16),
        sa=v((c.rows_a, LANES), BF16),
        sb=v((c.rows_b, LANES), BF16),
        sc=v((c.rows_c, LANES), BF16),
        sq=v((c.rows_q, LANES), BF16),
        resq=v((c.G, c.rows_q, LANES), BF16),
        gqkv=v((3, c.D, c.D) if c.W < LANES else (3, 16, LANES), BF16),
        sm=v((8, c.D), F32),
        smr=v((c.n, 8, c.D), F32),
        smd=v((8, c.D), F32),
        smdr=v((c.nd, 8, c.D), F32),
        sm2=v((8, c.D), F32),
        sm2r=v((c.n, 8, c.D), F32),
        sm2d=v((8, c.D), F32),
        sm2dr=v((c.nd, 8, c.D), F32),
        ss=pltpu.SemaphoreType.DMA((c.remotes,)),
        rs=pltpu.SemaphoreType.DMA((c.remotes,)),
        ls=pltpu.SemaphoreType.DMA((c.locals,)),
        free=pltpu.SemaphoreType.REGULAR((c.credits,)),
    )
    return spaces


ORDERS = dict(a="c1xy2", b="c1yx2", c="cxy21", d="cyx21", e="c1xy2")
SCHEDULE = [
    "down_1",
    "down_2",
    "back_1",
    "a",
    "b",
    "back_2",
    "branch_back",
    "up_1",
    "up_2",
    "other_weights",
    "c",
    "d",
    "e",
    "s",
    "a",
    "b",
    "s",
    "by_position",
    "low_0",
    "d",
    "b",
    "a",
    "low_1",
    "c",
    "a",
    "e",
    "low_2",
    "d",
    "a",
    "b",
    "low_3",
    "c",
    "finish_low",
    "e",
    "weights_low",
    "pass_low",
    "a",
    "top_0",
    "b",
    "e",
    "top_1",
    "d",
    "top_2",
    "top_3",
    "c",
    "a",
    "finish_top",
    "d",
    "b",
    "weights_top",
    "c",
    "e",
    "pass_top",
    "d",
    "c",
    "k",
    "b",
    "a",
    "v",
    "q",
    "e",
    "v",
    "q",
    "k",
    "d",
    "v",
    "k",
    "c",
    "q",
    "b",
    "a",
    "e",
    "v",
    "k",
    "q",
    "a",
    "d",
    "first_back",
    "v",
    "k",
    "q",
    "e",
    "c",
    "b",
    "t",
    "k",
    "q",
    "v",
    "b",
    "d",
    "t",
    "v",
    "d",
    "v",
    "q",
    "k",
    "c",
    "q",
    "k",
    "c",
    "e",
    "e",
]
IN_NAMES = [
    "i_order",
    "i_kind",
    "i_bg",
    "i_bfg",
    "i_g1",
    "i_s1",
    "i_g2",
    "i_s2",
    "i_tok",
    "i_cot",
    "i_wq",
    "i_wk",
    "i_wv",
    "i_wo",
    "i_wg",
    "i_wup",
    "i_wdn",
    "i_wfg",
]
OUT_NAMES = [
    "o_mix",
    "o_tok",
    "o_q",
    "o_k",
    "o_v",
    "o_out",
    "o_ag",
    "o_up",
    "o_dn",
    "o_fg",
    "o_sm",
    "o_sm2",
]


def norm_stats(values):
    average = jnp.mean(values, axis=-1, keepdims=True)
    centred = values - average
    variance = jnp.mean(centred * centred, axis=-1, keepdims=True)
    scale = lax.rsqrt(variance + EPS)
    return centred * scale, scale


def norm_back(grad, gain, normal, scale):
    e = grad * gain
    return scale * (
        e
        - jnp.mean(e, axis=-1, keepdims=True)
        - normal * jnp.mean(e * normal, axis=-1, keepdims=True)
    )


def kernel(c, names, *refs):
    r = SimpleNamespace(**dict(zip(names, refs)))
    n, nd, L, B, D, T, N, HB, G, W = c.n, c.nd, c.L, c.B, c.D, c.T, c.N, c.HB, c.G, c.W
    QB, NB, HALF, FC, NC, QF = c.QB, c.NB, c.HALF, c.FC, c.NC, c.QF
    s = lax.axis_index("seq")
    d = lax.axis_index("dp")
    b = s // G
    g = s % G
    core = s % 2
    pair = s // 2
    pairs = n // 2
    sibling = s + 1 - 2 * core
    count = dict(remote=0, local=0, credit=0)

    def remote(src, dst, device):
        i = count["remote"]
        assert i < c.remotes
        count["remote"] += 1
        copy = pltpu.make_async_remote_copy(
            src_ref=src,
            dst_ref=dst,
            send_sem=r.ss.at[i],
            recv_sem=r.rs.at[i],
            device_id=device,
            device_id_type=MESH,
        )
        copy.start()
        return copy

    def local(src, dst):
        i = count["local"]
        assert i < c.locals
        count["local"] += 1
        copy = pltpu.make_async_copy(src, dst, r.ls.at[i])
        copy.start()
        return copy

    def at_seq(t):
        return {"seq": t, "dp": d}

    def at_dp(t):
        return {"seq": s, "dp": t}

    get_tok = local(r.i_tok, r.tok)
    get_rows = [
        local(getattr(r, "i_" + name), getattr(r, name))
        for name in ("g1", "s1", "bg", "g2", "s2", "bfg")
    ]
    window = pl.multiple_of((g * W) // LANES * LANES, LANES)
    get_win = [
        local(
            ref.at[:, pl.ds(window, LANES)],
            r.win.at[i] if W < LANES else r.wqkv.at[:, i * LANES : (i + 1) * LANES],
        )
        for i, ref in enumerate((r.i_wq, r.i_wk, r.i_wv))
    ]
    get_wg = local(r.i_wg, r.wg)
    get_cot = local(r.i_cot, r.cot)
    get_wo = local(r.i_wo, r.wo)
    get_wup = local(r.i_wup, r.wup)
    get_wfg = local(r.i_wfg, r.wfg)
    get_wdn = local(r.i_wdn, r.wdn)
    barrier = pltpu.get_barrier_semaphore()
    for k in range(1, n):
        pl.semaphore_signal(barrier, inc=1, device_id=at_seq((s + k) % n), device_id_type=MESH)
    for k in range(1, nd):
        pl.semaphore_signal(barrier, inc=1, device_id=at_dp((d + k) % nd), device_id_type=MESH)

    get_tok.wait()
    for i in range(B):
        r.xs[i * L : (i + 1) * L, :] = r.tok[:, i, :]

    def inputs():
        return r.xs[...].astype(F32)

    normal, _ = norm_stats(inputs())
    for copy in get_rows:
        copy.wait()
    n1 = (normal * r.g1[...] + r.s1[...]).astype(BF16)
    for i in range(B):
        r.n1[i] = n1[i * L : (i + 1) * L].reshape(2, HB, D)

    pl.semaphore_wait(barrier, n - 1 + nd - 1)

    def slot(t):
        return pl.ds(2 * t, 2)

    rows_of = r.n1
    gather = {}
    for k in range(1, pairs):
        t = 2 * ((pair + k) % pairs) + core
        gather[k] = remote(rows_of.at[t // G], r.gat.at[s], at_seq(t))
    relay = {0: remote(rows_of.at[b], r.gat.at[s], at_seq(sibling))}
    r.gat[s] = r.n1[b]

    for copy in get_win:
        copy.wait()
    if W < LANES:
        upper = (g * W) % LANES != 0
        r.wqkv[...] = jnp.concatenate(
            [jnp.where(upper, r.win[i][:, W:], r.win[i][:, :W]) for i in range(3)], axis=1
        )
    get_wg.wait()
    r.ag[...] = jax.nn.sigmoid(dot(n1, r.wg[...]) + r.bg[...])

    order = [r.i_order[b, i] for i in range(2 * n)]
    inverse = []
    for p in range(2 * n):
        found = jnp.int32(0)
        for i in range(2 * n):
            found = jnp.where(order[i] == p, i, found)
        inverse.append(found)
    low_block = [jnp.minimum(order[2 * t], order[2 * t + 1]) for t in range(n)]
    top_block = [jnp.maximum(order[2 * t], order[2 * t + 1]) for t in range(n)]
    split = jnp.where(r.i_kind[b] == 2, F32(NEG), F32(0.0))

    def project(t):
        out = dot(r.gat[t].reshape(L, D), r.wqkv[...])
        r.qkvst[slot(t)] = (
            jnp.concatenate([out[:, :W] * (1.0 / math.sqrt(HD)), out[:, W:]], axis=1)
            .astype(BF16)
            .reshape(2, HB, 3 * W)
        )

    project(s)
    for k in range(1, pairs):
        gather[k].wait()
        u = 2 * ((pair + pairs - k) % pairs) + core
        relay[k] = remote(r.gat.at[u], r.gat.at[u], at_seq(sibling))
        project(u)
    for k in range(pairs):
        relay[k].wait()
        project(2 * ((pair + pairs - k) % pairs) + 1 - core)

    per = QB // HB
    head_of = lax.broadcasted_iota(jnp.int32, (QB, W), 1) // HD
    of_head = [head_of == h for h in range(c.hpd)]
    for i in range(NB):
        at = slice(i * QB, (i + 1) * QB)
        block = jnp.concatenate([r.qkvst[inverse[i * per + m]] for m in range(per)], axis=0)
        q, k, v = (block[:, j * W : (j + 1) * W] for j in range(3))
        r.q[at, :] = q
        r.qT[:, at] = q.T
        r.kT[:, at] = k.T
        r.vT[:, at] = v.T
        for h in range(c.hpd):
            r.k[h, at, :] = jnp.where(of_head[h], k, BF16(0.0))
            r.v[h, at, :] = jnp.where(of_head[h], v, BF16(0.0))

    def causal(size):
        keys_at = lax.broadcasted_iota(jnp.int32, (size, size), 0)
        return keys_at <= lax.broadcasted_iota(jnp.int32, (size, size), 1)

    def attend(first, last):
        chunks = [slice(i, i + QF) for i in range(first, last, QF)]

        def head(h, carry):
            hr = pl.ds(pl.multiple_of(h * HD, HD), HD)
            for at in chunks:
                scores = dot(r.k[h, 0 : at.stop, :], r.qT[:, at])
                diagonal = jnp.where(causal(QF), scores[at.start :], NEG)
                top = jnp.max(diagonal, axis=0, keepdims=True)
                low_rows = N // 2 if at.start >= N // 2 else 0
                low = scores[:low_rows] if low_rows else None
                middle = scores[low_rows : at.start] if at.start > low_rows else None
                if middle is not None:
                    top = jnp.maximum(top, jnp.max(middle, axis=0, keepdims=True))
                if low is not None:
                    top = jnp.maximum(top, jnp.max(low, axis=0, keepdims=True) + split)
                terms = []
                if low is not None:
                    terms.append(jnp.exp(low - (top - split)))
                if middle is not None:
                    terms.append(jnp.exp(middle - top))
                terms.append(jnp.exp(diagonal - top))
                total = sum(jnp.sum(t, axis=0, keepdims=True) for t in terms)
                weights = jnp.concatenate([t.astype(BF16) for t in terms], axis=0)
                out = dot(r.vT[hr, 0 : at.stop], weights)
                r.oT[hr, at] = out * (1.0 / total)
                lse = top + jnp.log(total)
                r.lseB[h, :, at] = lse
                r.lseA[h, :, at] = lse - split if low_rows else lse
            return carry

        lax.fori_loop(0, c.hpd, head, 0)
        for at in chunks:
            r.do[at.start // HB : at.stop // HB] = (
                r.oT[:, at].astype(BF16).T.reshape(QF // HB, HB, W)
            )

    def send_rows(which, blocks):
        for t in range(n):
            r.ou[2 * t + which] = r.do[blocks[t]]
        copies = []
        for k in range(1, n):
            t = (s + k) % n
            copies.append(remote(r.ou.at[2 * t + which], r.orr.at[2 * s + which], at_seq(t)))
        r.orr[2 * s + which] = r.ou[2 * s + which]
        return copies

    attend(N // 2, N)
    going = send_rows(1, top_block)
    attend(0, N // 2)
    going += send_rows(0, low_block)

    get_wo.wait()
    get_wup.wait()
    get_wfg.wait()
    get_wdn.wait()
    get_cot.wait()
    own = [(r.i_order[i, 2 * s], r.i_order[i, 2 * s + 1]) for i in range(B)]
    which_half = [
        (jnp.where(a > z, 1, 0), jnp.where(a > z, 0, 1)) for a, z in own
    ]
    for copy in going:
        copy.wait()
    for i in range(B):
        for m in range(2):
            for j in range(G):
                r.att[i * L + m * HB : i * L + (m + 1) * HB, j * W : (j + 1) * W] = r.orr[
                    2 * (i * G + j) + which_half[i][m]
                ]
    x = inputs()
    branch = dot(r.att[...], r.wo[...]) - x
    r.bamx[...] = branch
    middle = x + r.ag[...] * branch
    r.mid[...] = middle
    normal, scale = norm_stats(middle)
    n2 = (normal * r.g2[...] + r.s2[...]).astype(BF16)
    r.n2[...] = n2
    r.n2T[...] = n2.T

    def partner(axis, bit):
        index = s if axis == "seq" else d
        mine = index // 2**bit % 2
        there = index + (1 - 2 * mine) * 2**bit
        return mine, at_seq(there) if axis == "seq" else at_dp(there)

    def add_rows(ref, start, slots, base, length):
        step = math.gcd(length, 512)

        def body(i, carry):
            at = pl.ds(pl.multiple_of(start + i * step, 16), step)
            other = slots[pl.ds(pl.multiple_of(base + i * step, 16), step), :]
            ref[at, :] = (ref[at, :].astype(F32) + other.astype(F32)).astype(BF16)
            return carry

        lax.fori_loop(0, length // step, body, 0)

    def halve(ref, slots, first, rows, bits, trail, credits):
        start, length, base = jnp.int32(first), rows, first
        for axis, bit in bits:
            half = length // 2
            mine, device = partner(axis, bit)
            keep = pl.multiple_of(start + mine * half, 16)
            give = pl.multiple_of(start + (1 - mine) * half, 16)
            copy = remote(ref.at[pl.ds(give, half)], slots.at[pl.ds(base, half)], device)
            yield
            copy.wait()
            credit = None
            if credits:
                assert count["credit"] < c.credits
                credit = r.free.at[count["credit"]]
                count["credit"] += 1
                pl.semaphore_signal(credit, inc=1, device_id=device, device_id_type=MESH)
            add_rows(ref, keep, slots, base, half)
            trail.append((keep, half, device, credit, start))
            start, length, base = keep, half, base + half

    def all_reduce(ref, slots, first, rows, bits, store):
        trail = []
        yield from halve(ref, slots, first, rows, bits, trail, True)
        for keep, half, device, credit, _ in reversed(trail):
            at = pl.ds(keep, half)
            pl.semaphore_wait(credit, 1)
            copy = remote(ref.at[at], ref.at[at], device)
            yield
            copy.wait()
        store()

    def reduce_small(own_ref, slots, dp_ref, dp_slots, out_ref):
        copies = []
        for k in range(1, n):
            copies.append(remote(own_ref, slots.at[s], at_seq((s + k) % n)))
        slots[s] = own_ref[...]
        yield
        for copy in copies:
            copy.wait()
        dp_ref[...] = sum(slots[i] for i in range(n))
        copies = []
        for k in range(1, nd):
            copies.append(remote(dp_ref, dp_slots.at[d], at_dp((d + k) % nd)))
        dp_slots[d] = dp_ref[...]
        yield
        for copy in copies:
            copy.wait()
        out_ref[...] = sum(dp_slots[i] for i in range(nd))

    jobs = {}

    def begin(name, job):
        jobs[name] = job
        next(job)

    def advance(name):
        if next(jobs[name], "over") == "over":
            del jobs[name]

    cores = [("seq", 0)]
    chips = [("seq", i) for i in range(1, c.seq_bits)]
    planes = [("dp", i) for i in range(c.dp_bits)]
    bits_of = dict(c=cores, x=chips[:1], y=chips[1:])
    bits_of["1"], bits_of["2"] = planes[:1], planes[1:]

    def bits_in(name):
        return [bit for mark in ORDERS[name] for bit in bits_of[mark]]

    puts = []

    def down_chunk(j, carry):
        part = dot_tn(r.hid[pl.ds(pl.multiple_of(j * T, T), T), :], r.dffn[...]).astype(BF16)
        for i in range(c.LP):
            at = pl.ds(pl.multiple_of((j * c.LP + i) * FC, FC), FC)
            r.fa[at, :] = part[:, i * LANES : (i + 1) * LANES]
        return carry

    def up_chunk(j, carry):
        part = dot(r.n2T[...], r.gp[j].astype(BF16)).astype(BF16)
        for i in range(FC // LANES):
            at = pl.ds(pl.multiple_of((j * (FC // LANES) + i) * D, D), D)
            r.fb[at, :] = part[:, i * LANES : (i + 1) * LANES]
        return carry

    def put_down(chunks):
        for j in chunks:
            for i in range(c.LP):
                at = (j * c.LP + i) * FC
                puts.append(
                    local(
                        r.fa.at[at : at + FC],
                        r.o_dn.at[j * FC : (j + 1) * FC, i * LANES : (i + 1) * LANES],
                    )
                )

    def put_up(chunks):
        per_chunk = FC // LANES
        for i in range(chunks.start * per_chunk, chunks.stop * per_chunk):
            puts.append(
                local(r.fb.at[i * D : (i + 1) * D], r.o_up.at[:, i * LANES : (i + 1) * LANES])
            )

    def put_rest():
        for j, ref in enumerate((r.o_out, r.o_ag, r.o_fg)):
            for i in range(c.LP):
                at = (j * c.LP + i) * D
                puts.append(
                    local(r.fc.at[at : at + D], ref.at[:, i * LANES : (i + 1) * LANES])
                )

    def feed_forward_sum(name, half, chunk, ref, slots, rows, put):
        chunks = range(half * NC // 2, (half + 1) * NC // 2)
        lax.fori_loop(chunks.start, chunks.stop, chunk, 0, unroll=True)
        begin(
            name,
            all_reduce(
                ref,
                slots,
                chunks.start * (rows // NC),
                rows // 2,
                bits_in(name),
                functools.partial(put, chunks),
            ),
        )

    steps = {}

    def step(function):
        steps[function.__name__] = function

    slope = math.sqrt(2.0 / math.pi)
    r.acc[...] = jnp.zeros((T, D), F32)

    def forward_chunk(j, carry):
        cols = pl.ds(pl.multiple_of(j * FC, FC), FC)
        u = dot(r.n2[...], r.wup[:, cols])
        square = u * u
        t = jnp.tanh(slope * u * (1.0 + 0.044715 * square))
        half = 0.5 * (1.0 + t)
        hidden = (u * half).astype(BF16)
        r.hid[pl.ds(pl.multiple_of(j * T, T), T), :] = hidden
        r.gp[j] = half + 0.5 * u * (1.0 - t * t) * (slope * (1.0 + 3 * 0.044715 * square))
        r.acc[...] += dot(hidden, r.wdn[cols, :])
        return carry

    lax.fori_loop(0, NC, forward_chunk, 0, unroll=2)
    gate = jax.nn.sigmoid(dot(r.n2[...], r.wfg[...]) + r.bfg[...])
    middle = r.mid[...]
    apart = r.acc[...] - middle
    grad = jnp.concatenate([r.cot[:, i, :].astype(F32) for i in range(B)], axis=0)
    mixed = (middle + gate * apart).astype(BF16)
    for i in range(B):
        r.cot[:, i, :] = mixed[i * L : (i + 1) * L]
    puts.append(local(r.cot, r.o_mix))
    r.dffn[...] = (grad * gate).astype(BF16)
    d_pre = (grad * apart * gate * (1.0 - gate)).astype(BF16)
    r.dpre[...] = d_pre
    r.sm[0:1, :] = jnp.sum(d_pre.astype(F32), axis=0, keepdims=True)
    r.dxr[...] = grad * (1.0 - gate)
    r.acc[...] = dot_nt(d_pre, r.wfg[...])

    @step
    def down_1():
        feed_forward_sum("a", 0, down_chunk, r.fa, r.sa, c.rows_a, put_down)

    @step
    def down_2():
        feed_forward_sum("b", 1, down_chunk, r.fa, r.sa, c.rows_a, put_down)

    def backward_chunk(j, carry):
        cols = pl.ds(pl.multiple_of(j * FC, FC), FC)
        d_hidden = dot_nt(r.dffn[...], r.wdn[cols, :])
        d_up = (d_hidden * r.gp[j]).astype(BF16)
        r.gp[j] = d_up.astype(F32)
        r.acc[...] += dot_nt(d_up, r.wup[:, cols])
        return carry

    @step
    def back_1():
        lax.fori_loop(0, NC // 2, backward_chunk, 0, unroll=True)

    @step
    def back_2():
        lax.fori_loop(NC // 2, NC, backward_chunk, 0, unroll=True)

    back = []

    @step
    def branch_back():
        d_norm = r.acc[...]
        normal, scale = norm_stats(r.mid[...])
        r.sm[1:2, :] = jnp.sum(d_norm * normal, axis=0, keepdims=True)
        r.sm[2:3, :] = jnp.sum(d_norm, axis=0, keepdims=True)
        d_middle = r.dxr[...] + norm_back(d_norm, r.g2[...], normal, scale)
        gate = r.ag[...]
        d_att = (d_middle * gate).astype(BF16)
        d_attn_pre = (d_middle * r.bamx[...] * gate * (1.0 - gate)).astype(BF16)
        r.datt[...] = d_att
        r.dapre[...] = d_attn_pre
        r.sm[3:4, :] = jnp.sum(d_attn_pre.astype(F32), axis=0, keepdims=True)
        r.sm[4:8, :] = jnp.zeros((4, D), F32)
        r.dxr[...] = d_middle * (1.0 - gate)
        d_o = dot_nt(d_att, r.wo[...]).astype(BF16)
        for i in range(B):
            for j in range(G):
                r.ou[2 * (i * G + j) : 2 * (i * G + j) + 2] = d_o[
                    i * L : (i + 1) * L, j * W : (j + 1) * W
                ].reshape(2, HB, W)
        for k in range(1, n):
            t = (s + k) % n
            back.append(remote(r.ou.at[slot(t)], r.dor.at[slot(s)], at_seq(t)))
        r.dor[slot(s)] = r.ou[slot(s)]

    @step
    def up_1():
        feed_forward_sum("c", 0, up_chunk, r.fb, r.sb, c.rows_b, put_up)

    @step
    def up_2():
        feed_forward_sum("d", 1, up_chunk, r.fb, r.sb, c.rows_b, put_up)

    @step
    def other_weights():
        begin("s", reduce_small(r.sm, r.smr, r.smd, r.smdr, r.o_sm))
        for j, part in enumerate(
            (
                dot_tn(r.att[...], r.datt[...]),
                dot_tn(r.n1[...].reshape(T, D), r.dapre[...]),
                dot(r.n2T[...], r.dpre[...]),
            )
        ):
            part = part.astype(BF16)
            for i in range(c.LP):
                at = (j * c.LP + i) * D
                r.fc[at : at + D, :] = part[:, i * LANES : (i + 1) * LANES]
        if c.rows_c > c.used_c:
            r.fc[c.used_c :, :] = jnp.zeros((c.rows_c - c.used_c, LANES), BF16)
        begin("e", all_reduce(r.fc, r.sc, 0, c.rows_c, bits_in("e"), put_rest))
        r.acc[...] = dot_nt(r.dapre[...], r.wg[...])

    @step
    def by_position():
        for i in range(2 * n):
            r.hid[i * HB : (i + 1) * HB, :] = r.gat[inverse[i] // 2, inverse[i] % 2]
        for copy in back:
            copy.wait()
        for i in range(NB):
            at = slice(i * QB, (i + 1) * QB)
            block = jnp.concatenate([r.dor[inverse[i * per + m]] for m in range(per)], axis=0)
            r.do[i * per : (i + 1) * per] = block.reshape(per, HB, W)
            turned = block.T
            r.doT[:, at] = turned
            product = turned.astype(F32) * r.oT[:, at]
            for h in range(c.hpd):
                r.odot[h, :, at] = jnp.sum(product[h * HD : (h + 1) * HD], axis=0, keepdims=True)

    def backward_block(j):
        at = slice(j * QB, (j + 1) * QB)
        lse_ref = r.lseA if j < HALF else r.lseB
        keys_t = []
        for h in range(c.hpd):
            own = [
                r.kT[h * HD : (h + 1) * HD, at] if i == h else jnp.zeros((HD, QB), BF16)
                for i in range(c.hpd)
            ]
            keys_t.append(jnp.concatenate(own, axis=0))
        keys_t = jnp.concatenate(keys_t, axis=1)
        d_keys, d_values = [0.0] * c.hpd, [0.0] * c.hpd
        for start in range(j * QB, N, N // 2):
            to = slice(start, min(start + N // 2, N))
            slopes = []
            for h in range(c.hpd):
                p = jnp.exp(dot(r.k[h, at, :], r.qT[:, to]) - lse_ref[h, :, to])
                if start == j * QB:
                    corner = jnp.where(causal(QB), p[:, :QB], 0.0)
                    p = jnp.concatenate([corner, p[:, QB:]], axis=1) if j < NB - 1 else corner
                dp = dot(r.v[h, at, :], r.doT[:, to])
                ds = (p * (dp - r.odot[h, :, to])).astype(BF16)
                slopes.append(ds)
                d_values[h] += dot(
                    p.astype(BF16), r.do[to.start // HB : to.stop // HB].reshape(-1, W)
                )
                d_keys[h] += dot(ds, r.q[to, :])
            part = dot(keys_t, jnp.concatenate(slopes, axis=0))
            if j == 0:
                r.dqT[:, to] = part
            else:
                r.dqT[:, to] += part
        for h in range(c.hpd):
            r.v[h, at, :] = d_values[h].astype(BF16)
            r.k[h, at, :] = d_keys[h].astype(BF16)

    def partial(at):
        return r.gat[at // 2, at % 2]

    def finish_half(which, blocks):
        for i in blocks:
            at = slice(i * QB, (i + 1) * QB)
            parts = [(r.dqT[:, at] * (1.0 / math.sqrt(HD))).astype(BF16).T]
            for ref in (r.k, r.v):
                part = ref[0, at, :]
                for h in range(1, c.hpd):
                    part = jnp.where(of_head[h], ref[h, at, :], part)
                parts.append(part)
            rows = jnp.concatenate(parts, axis=1)
            r.qkvst[i * per : (i + 1) * per] = rows.reshape(per, HB, 3 * W)
            r.gat[i * per // 2 : (i + 1) * per // 2] = (
                dot_nt(rows, r.wqkv[...]).astype(BF16).reshape(per // 2, 2, HB, D)
            )
        table = top_block if which else low_block

        def pick(m, parity):
            return jnp.where(parity == 0, table[2 * m], table[2 * m + 1])

        for m in range(pairs):
            r.sibs[which, m] = partial(pick(m, 1 - core))
        return remote(r.sibs.at[which], r.sibr.at[which], at_seq(sibling)), pick

    def pass_on(which, copy, pick):
        copy.wait()
        for m in range(pairs):
            r.sibs[which, m] = (
                partial(pick(m, core)).astype(F32) + r.sibr[which, m].astype(F32)
            ).astype(BF16)
        copies = []
        for k in range(1, pairs):
            m = (pair + k) % pairs
            copies.append(
                remote(r.sibs.at[which, m], r.dnr.at[pair, which], at_seq(2 * m + core))
            )
        r.dnr[pair, which] = r.sibs[which, pair]
        return copies

    def weight_part(which):
        rows = slice(which * N // 2, (which + 1) * N // 2)
        return dot_tn(r.hid[rows, :], r.qkvst[which * n : (which + 1) * n].reshape(N // 2, 3 * W))

    arriving = []
    held_up = {}

    for j in range(NB):
        steps[f"low_{j}" if j < HALF else f"top_{j - HALF}"] = functools.partial(backward_block, j)

    @step
    def finish_low():
        held_up[0] = finish_half(0, range(HALF))

    @step
    def weights_low():
        r.wacc[...] = weight_part(0)

    @step
    def pass_low():
        arriving.extend(pass_on(0, *held_up[0]))

    @step
    def finish_top():
        held_up[1] = finish_half(1, range(HALF, NB))

    @step
    def pass_top():
        arriving.extend(pass_on(1, *held_up[1]))

    group_bits = log2(G)
    buffers = [("seq", i) for i in range(group_bits, c.seq_bits)]
    members = [("seq", i) for i in range(1, group_bits)]

    def heads_reduce(first, bits, members_at):
        trail = []
        yield from halve(r.fq, r.sq, first, D, bits, trail, False)
        start, length = trail[-1][0], trail[-1][1]
        r.resq[g, pl.ds(start, length), :] = r.fq[pl.ds(start, length), :]
        steps = [("rows", step) for step in reversed(trail)]
        steps[members_at:members_at] = [("members", bit) for bit in members]
        steps.append(("members", cores[0]))
        held = [g]
        for kind, step in steps:
            at = pl.ds(start, length)
            if kind == "rows":
                device = step[2]
            else:
                mine, device = partner(*step)
            copies = [remote(r.resq.at[i, at], r.resq.at[i, at], device) for i in held]
            yield
            for copy in copies:
                copy.wait()
            if kind == "rows":
                start, length = pl.multiple_of(step[4], 16), 2 * length
            else:
                held = held + [i + (1 - 2 * mine) * 2 ** step[1] for i in held]

    splits = len(buffers + planes)

    @step
    def weights_top():
        part = (r.wacc[...] + weight_part(1)).astype(BF16)
        if c.np3 * LANES > 3 * W:
            part = jnp.concatenate([part, jnp.zeros((D, c.np3 * LANES - 3 * W), BF16)], axis=1)
        for i in range(c.np3):
            r.fq[i * D : (i + 1) * D, :] = part[:, i * LANES : (i + 1) * LANES]
            bits, at = (
                (buffers + planes, splits),
                (planes + buffers, 0),
                (buffers + planes, splits - len(buffers)),
            )[i]
            begin("qkv"[i], heads_reduce(i * D, bits, at))

    @step
    def first_back():
        for copy in arriving:
            copy.wait()
        parts = []
        for i in range(B):
            for m in range(2):
                parts.append(
                    sum(
                        r.dnr[i * (G // 2) + j, which_half[i][m]].astype(F32) for j in range(G // 2)
                    )
                )
        d_norm = jnp.concatenate(parts, axis=0) + r.acc[...]
        normal, scale = norm_stats(inputs())
        r.sm2[0:1, :] = jnp.sum(d_norm * normal, axis=0, keepdims=True)
        r.sm2[1:2, :] = jnp.sum(d_norm, axis=0, keepdims=True)
        r.sm2[2:8, :] = jnp.zeros((6, D), F32)
        begin("t", reduce_small(r.sm2, r.sm2r, r.sm2d, r.sm2dr, r.o_sm2))
        grads = (r.dxr[...] + norm_back(d_norm, r.g1[...], normal, scale)).astype(BF16)
        for i in range(B):
            r.tok[:, i, :] = grads[i * L : (i + 1) * L]
        puts.append(local(r.tok, r.o_tok))

    for name in SCHEDULE:
        if name in steps:
            steps.pop(name)()
        elif name in jobs:
            advance(name)
    assert not steps
    while jobs:
        for name in list(jobs):
            advance(name)

    outs = (r.o_q, r.o_k, r.o_v)
    for i in range(G):
        if W == LANES:
            for j, ref in enumerate(outs):
                puts.append(
                    local(
                        r.resq.at[i, j * D : (j + 1) * D], ref.at[:, i * LANES : (i + 1) * LANES]
                    )
                )
            continue
        block = jnp.concatenate(
            [r.resq[i, m * D : (m + 1) * D, :] for m in range(c.np3)], axis=1
        )
        for j in range(3):
            r.gqkv[j, :, i * W : (i + 1) * W] = block[:, j * W : (j + 1) * W]
    if W < LANES:
        for j, ref in enumerate(outs):
            puts.append(local(r.gqkv.at[j], ref))
    for put in puts:
        put.wait()


def blocks_of(shapes):
    blocks = []
    for i, (rows, columns) in enumerate(shapes):
        step = min(rows, 2**18 // columns)
        blocks += [(i, at, step) for at in range(0, rows, step)]
    return blocks


def widen(arrays, blocks, *refs):
    refs = iter(refs)
    take = lambda number: [next(refs) for _ in range(number)]
    grads, rest, small = take(arrays), take(2), take(2)
    wide, rest_out, rows = take(arrays), take(2), take(6)
    held, held_wide, held_rest = take(arrays), take(arrays), take(2)
    (sems,) = take(1)
    loads = []
    for j, (i, at, step) in enumerate(blocks):
        block = pl.ds(at, step)
        loads.append(pltpu.make_async_copy(grads[i].at[block], held[i].at[block], sems.at[0, j]))
    for j in range(2):
        loads.append(
            pltpu.make_async_copy(rest[j], held_rest[j], sems.at[0, len(blocks) + j])
        )
    for load in loads:
        load.start()
    for j, row in enumerate(rows):
        row[...] = small[j // 4][j % 4 : j % 4 + 1, :]
    stores = []
    for j, (i, at, step) in enumerate(blocks):
        block = pl.ds(at, step)
        loads[j].wait()
        part = min(step, 64)

        def body(m, carry):
            here = pl.ds(pl.multiple_of(at + m * part, part), part)
            held_wide[i][here, :] = held[i][here, :].astype(F32)
            return carry

        lax.fori_loop(0, step // part, body, 0)
        stores.append(
            pltpu.make_async_copy(held_wide[i].at[block], wide[i].at[block], sems.at[1, j])
        )
        stores[-1].start()
    for j in range(2):
        loads[len(blocks) + j].wait()
        stores.append(
            pltpu.make_async_copy(held_rest[j], rest_out[j], sems.at[1, len(blocks) + j])
        )
        stores[-1].start()
    for store in stores:
        store.wait()


def solution(mesh):
    n, nd = mesh.shape["seq"], mesh.shape["dp"]

    def local(
        tokens,
        cotangent,
        query_weight,
        key_weight,
        value_weight,
        output_weight,
        attn_gate_weight,
        attn_gate_bias,
        up_weight,
        down_weight,
        ffn_gate_weight,
        ffn_gate_bias,
        first_gain,
        first_shift,
        second_gain,
        second_shift,
        row_kind,
        block_order,
    ):
        L, B, D = tokens.shape
        FF = up_weight.shape[1]
        c = sizes(n, nd, L, B, D, FF)
        spaces = scratch(c)
        names = IN_NAMES + OUT_NAMES + list(spaces)
        smem = pl.BlockSpec(memory_space=pltpu.SMEM)
        vmem = pl.BlockSpec(memory_space=pltpu.VMEM)
        hbm = pl.BlockSpec(memory_space=pl.ANY)

        def shape(*dims, dtype=BF16):
            return jax.ShapeDtypeStruct(dims, dtype)

        def row(vector):
            return vector.reshape(1, -1)

        out = pl.pallas_call(
            functools.partial(kernel, c, names),
            out_shape=(
                shape(L, B, D),
                shape(L, B, D),
                shape(D, D),
                shape(D, D),
                shape(D, D),
                shape(D, D),
                shape(D, D),
                shape(D, FF),
                shape(FF, D),
                shape(D, D),
                shape(8, D, dtype=F32),
                shape(8, D, dtype=F32),
            ),
            in_specs=[smem] * 2 + [hbm] * 16,
            out_specs=(hbm,) * 10 + (vmem,) * 2,
            scratch_shapes=list(spaces.values()),
            compiler_params=pltpu.CompilerParams(
                collective_id=0, has_side_effects=True, vmem_limit_bytes=VMEM_BYTES
            ),
            name="layer",
        )(
            block_order,
            row_kind,
            row(attn_gate_bias),
            row(ffn_gate_bias),
            row(first_gain),
            row(first_shift),
            row(second_gain),
            row(second_shift),
            tokens,
            cotangent,
            query_weight,
            key_weight,
            value_weight,
            output_weight,
            attn_gate_weight,
            up_weight,
            down_weight,
            ffn_gate_weight,
        )
        mix, tok, *grads, small, small2 = out
        shapes = [a.shape for a in grads]
        wide = pl.pallas_call(
            functools.partial(widen, len(grads), blocks_of(shapes)),
            out_shape=tuple(shape(*dims, dtype=F32) for dims in shapes)
            + (shape(L, B, D),) * 2
            + (shape(1, D, dtype=F32),) * 6,
            in_specs=[hbm] * (len(grads) + 2) + [vmem] * 2,
            out_specs=(hbm,) * (len(grads) + 2) + (vmem,) * 6,
            scratch_shapes=[pltpu.VMEM(dims, BF16) for dims in shapes]
            + [pltpu.VMEM(dims, F32) for dims in shapes]
            + [pltpu.VMEM((L, B, D), BF16)] * 2
            + [pltpu.SemaphoreType.DMA((2, len(blocks_of(shapes)) + 2))],
            compiler_params=pltpu.CompilerParams(vmem_limit_bytes=VMEM_BYTES),
            name="widen",
        )(*grads, mix, tok, small, small2)
        dq, dk, dv, dout, dag, dup, ddn, dfg, mix, tok = wide[:10]
        bfg, g2, s2, bg, g1, s1 = (a.reshape(D) for a in wide[10:])
        return mix, tok, dq, dk, dv, dout, dag, bg, dup, ddn, dfg, bfg, g1, s1, g2, s2

    sharded = P("seq", "dp", None)
    return jax.shard_map(
        local,
        mesh=mesh,
        in_specs=(sharded, sharded) + (P(),) * 14 + (P("dp"), P("dp", None)),
        out_specs=(sharded, sharded) + (P(),) * 14,
        check_vma=False,
    )


VMEM_BYTES = 63 * 2**20
```

```python
import functools
import math
from types import SimpleNamespace

import jax
import jax.numpy as jnp
from jax import lax
from jax.experimental import pallas as pl
from jax.experimental.pallas import tpu as pltpu
from jax.sharding import PartitionSpec as P

H = 8
HD = 64
NEG = -1e30
EPS = 1e-05
MESH = pl.DeviceIdType.MESH
F32 = jnp.float32
BF16 = jnp.bfloat16
LANES = 128


def dot(a, b):
    return jnp.dot(a, b, preferred_element_type=F32)


def dot_nt(a, b):
    return lax.dot_general(a, b, (((1,), (1,)), ((), ())), preferred_element_type=F32)


def dot_tn(a, b):
    return lax.dot_general(a, b, (((0,), (0,)), ((), ())), preferred_element_type=F32)


def log2(value):
    return value.bit_length() - 1


def sizes(n, nd, rows, buffers, features, hidden):
    c = SimpleNamespace(n=n, nd=nd, L=rows, B=buffers, D=features, FF=hidden)
    c.T = rows * buffers
    c.N = rows * n
    c.HB = rows // 2
    c.G = n // buffers
    c.hpd = H // c.G
    c.W = c.hpd * HD
    c.QB = min(256, c.N // 2)
    c.QF = min(512, c.N // 2)
    c.NB = c.N // c.QB
    c.HALF = c.NB // 2
    c.FC = 512
    c.NC = hidden // c.FC
    c.LP = features // LANES
    unit = 16 * n * nd
    c.rows_a = hidden * c.LP
    c.rows_b = (hidden // LANES) * features
    c.rows_c = -(-(3 * features * c.LP) // unit) * unit
    c.used_c = 3 * features * c.LP
    c.np3 = -(-(3 * c.W) // LANES)
    c.rows_q = c.np3 * features
    c.seq_bits = log2(n)
    c.dp_bits = log2(nd)
    c.remotes = 10 * n + 2 * nd + 10 * (c.seq_bits + c.dp_bits)
    c.credits = 5 * (c.seq_bits + c.dp_bits)
    c.locals = 28 + c.NC * c.LP + hidden // LANES + 3 * c.LP + 3 * c.G
    return c


def scratch(c):
    v = pltpu.VMEM
    spaces = dict(
        tok=v((c.L, c.B, c.D), BF16),
        cot=v((c.L, c.B, c.D), BF16),
        xs=v((c.T, c.D), BF16),
        bg=v((1, c.D), F32),
        bfg=v((1, c.D), F32),
        g1=v((1, c.D), F32),
        s1=v((1, c.D), F32),
        g2=v((1, c.D), F32),
        s2=v((1, c.D), F32),
        win=v((3, c.D, LANES) if c.W < LANES else (3, 16, LANES), BF16),
        wqkv=v((c.D, 3 * c.W), BF16),
        wg=v((c.D, c.D), BF16),
        wo=v((c.D, c.D), BF16),
        wup=v((c.D, c.FF), BF16),
        wdn=v((c.FF, c.D), BF16),
        wfg=v((c.D, c.D), BF16),
        n1=v((c.B, 2, c.HB, c.D), BF16),
        gat=v((c.n, 2, c.HB, c.D), BF16),
        qkvst=v((2 * c.n, c.HB, 3 * c.W), BF16),
        q=v((c.N, c.W), BF16),
        k=v((c.hpd, c.N, c.W), BF16),
        v=v((c.hpd, c.N, c.W), BF16),
        do=v((2 * c.n, c.HB, c.W), BF16),
        kT=v((c.W, c.N), BF16),
        qT=v((c.W, c.N), BF16),
        vT=v((c.W, c.N), BF16),
        doT=v((c.W, c.N), BF16),
        oT=v((c.W, c.N), F32),
        dqT=v((c.W, c.N), F32),
        lseA=v((c.hpd, 1, c.N), F32),
        lseB=v((c.hpd, 1, c.N), F32),
        odot=v((c.hpd, 1, c.N), F32),
        ou=v((2 * c.n, c.HB, c.W), BF16),
        orr=v((2 * c.n, c.HB, c.W), BF16),
        dor=v((2 * c.n, c.HB, c.W), BF16),
        att=v((c.T, c.D), BF16),
        ag=v((c.T, c.D), F32),
        mid=v((c.T, c.D), F32),
        bamx=v((c.T, c.D), F32),
        acc=v((c.T, c.D), F32),
        dxr=v((c.T, c.D), F32),
        n2=v((c.T, c.D), BF16),
        n2T=v((c.D, c.T), BF16),
        gp=v((c.NC, c.T, c.FC), F32),
        hid=v((max(c.NC * c.T, c.N), c.FC), BF16),
        dffn=v((c.T, c.D), BF16),
        dpre=v((c.T, c.D), BF16),
        datt=v((c.T, c.D), BF16),
        dapre=v((c.T, c.D), BF16),
        wacc=v((c.D, 3 * c.W), F32),
        sibs=v((2, c.n // 2, c.HB, c.D), BF16),
        sibr=v((2, c.n // 2, c.HB, c.D), BF16),
        dnr=v((c.n // 2, 2, c.HB, c.D), BF16),
        fa=v((c.rows_a, LANES), BF16),
        fb=v((c.rows_b, LANES), BF16),
        fc=v((c.rows_c, LANES), BF16),
        fq=v((c.rows_q, LANES), BF16),
        sa=v((c.rows_a, LANES), BF16),
        sb=v((c.rows_b, LANES), BF16),
        sc=v((c.rows_c, LANES), BF16),
        sq=v((c.rows_q, LANES), BF16),
        resq=v((c.G, c.rows_q, LANES), BF16),
        gqkv=v((3, c.D, c.D) if c.W < LANES else (3, 16, LANES), BF16),
        sm=v((8, c.D), F32),
        smr=v((c.n, 8, c.D), F32),
        smd=v((8, c.D), F32),
        smdr=v((c.nd, 8, c.D), F32),
        sm2=v((8, c.D), F32),
        sm2r=v((c.n, 8, c.D), F32),
        sm2d=v((8, c.D), F32),
        sm2dr=v((c.nd, 8, c.D), F32),
        ss=pltpu.SemaphoreType.DMA((c.remotes,)),
        rs=pltpu.SemaphoreType.DMA((c.remotes,)),
        ls=pltpu.SemaphoreType.DMA((c.locals,)),
        free=pltpu.SemaphoreType.REGULAR((c.credits,)),
    )
    return spaces


ORDERS = dict(a="c1xy2", b="cyx21", c="cxy12", d="cy21x", e="c1xy2")
SCHEDULE = [
    "down_1",
    "down_2",
    "back_1",
    "a",
    "b",
    "back_2",
    "branch_back",
    "up_1",
    "up_2",
    "other_weights",
    "a",
    "c",
    "d",
    "e",
    "b",
    "s",
    "s",
    "a",
    "d",
    "by_position",
    "e",
    "b",
    "low_0",
    "c",
    "a",
    "low_1",
    "e",
    "low_2",
    "c",
    "b",
    "a",
    "low_3",
    "e",
    "d",
    "finish_low",
    "b",
    "a",
    "c",
    "weights_low",
    "pass_low",
    "e",
    "top_0",
    "c",
    "b",
    "a",
    "d",
    "top_1",
    "top_2",
    "e",
    "top_3",
    "finish_top",
    "c",
    "d",
    "weights_top",
    "b",
    "pass_top",
    "e",
    "c",
    "d",
    "k",
    "a",
    "q",
    "v",
    "k",
    "d",
    "k",
    "q",
    "v",
    "c",
    "k",
    "b",
    "q",
    "v",
    "k",
    "q",
    "v",
    "e",
    "d",
    "b",
    "first_back",
    "q",
    "b",
    "k",
    "c",
    "a",
    "v",
    "c",
    "a",
    "v",
    "t",
    "q",
    "d",
    "k",
    "v",
    "t",
    "d",
    "q",
    "k",
    "v",
    "e",
    "q",
    "e",
]
IN_NAMES = [
    "i_order",
    "i_kind",
    "i_bg",
    "i_bfg",
    "i_g1",
    "i_s1",
    "i_g2",
    "i_s2",
    "i_tok",
    "i_cot",
    "i_wq",
    "i_wk",
    "i_wv",
    "i_wo",
    "i_wg",
    "i_wup",
    "i_wdn",
    "i_wfg",
]
OUT_NAMES = [
    "o_mix",
    "o_tok",
    "o_q",
    "o_k",
    "o_v",
    "o_out",
    "o_ag",
    "o_up",
    "o_dn",
    "o_fg",
    "o_sm",
    "o_sm2",
]


def norm_stats(values):
    average = jnp.mean(values, axis=-1, keepdims=True)
    centred = values - average
    variance = jnp.mean(centred * centred, axis=-1, keepdims=True)
    scale = lax.rsqrt(variance + EPS)
    return centred * scale, scale


def norm_back(grad, gain, normal, scale):
    e = grad * gain
    return scale * (
        e
        - jnp.mean(e, axis=-1, keepdims=True)
        - normal * jnp.mean(e * normal, axis=-1, keepdims=True)
    )


def kernel(c, names, *refs):
    r = SimpleNamespace(**dict(zip(names, refs)))
    n, nd, L, B, D, T, N, HB, G, W = c.n, c.nd, c.L, c.B, c.D, c.T, c.N, c.HB, c.G, c.W
    QB, NB, HALF, FC, NC, QF = c.QB, c.NB, c.HALF, c.FC, c.NC, c.QF
    s = lax.axis_index("seq")
    d = lax.axis_index("dp")
    b = s // G
    g = s % G
    core = s % 2
    pair = s // 2
    pairs = n // 2
    sibling = s + 1 - 2 * core
    count = dict(remote=0, local=0, credit=0)

    def remote(src, dst, device):
        i = count["remote"]
        assert i < c.remotes
        count["remote"] += 1
        copy = pltpu.make_async_remote_copy(
            src_ref=src,
            dst_ref=dst,
            send_sem=r.ss.at[i],
            recv_sem=r.rs.at[i],
            device_id=device,
            device_id_type=MESH,
        )
        copy.start()
        return copy

    def local(src, dst):
        i = count["local"]
        assert i < c.locals
        count["local"] += 1
        copy = pltpu.make_async_copy(src, dst, r.ls.at[i])
        copy.start()
        return copy

    def at_seq(t):
        return {"seq": t, "dp": d}

    def at_dp(t):
        return {"seq": s, "dp": t}

    get_tok = local(r.i_tok, r.tok)
    get_rows = [
        local(getattr(r, "i_" + name), getattr(r, name))
        for name in ("g1", "s1", "bg", "g2", "s2", "bfg")
    ]
    window = pl.multiple_of((g * W) // LANES * LANES, LANES)
    get_win = [
        local(
            ref.at[:, pl.ds(window, LANES)],
            r.win.at[i] if W < LANES else r.wqkv.at[:, i * LANES : (i + 1) * LANES],
        )
        for i, ref in enumerate((r.i_wq, r.i_wk, r.i_wv))
    ]
    get_wg = local(r.i_wg, r.wg)
    get_cot = local(r.i_cot, r.cot)
    get_wo = local(r.i_wo, r.wo)
    get_wup = local(r.i_wup, r.wup)
    get_wfg = local(r.i_wfg, r.wfg)
    get_wdn = local(r.i_wdn, r.wdn)
    barrier = pltpu.get_barrier_semaphore()
    for k in range(1, n):
        pl.semaphore_signal(barrier, inc=1, device_id=at_seq((s + k) % n), device_id_type=MESH)
    for k in range(1, nd):
        pl.semaphore_signal(barrier, inc=1, device_id=at_dp((d + k) % nd), device_id_type=MESH)

    get_tok.wait()
    for i in range(B):
        r.xs[i * L : (i + 1) * L, :] = r.tok[:, i, :]

    def inputs():
        return r.xs[...].astype(F32)

    normal, _ = norm_stats(inputs())
    for copy in get_rows:
        copy.wait()
    n1 = (normal * r.g1[...] + r.s1[...]).astype(BF16)
    for i in range(B):
        r.n1[i] = n1[i * L : (i + 1) * L].reshape(2, HB, D)

    pl.semaphore_wait(barrier, n - 1 + nd - 1)

    def slot(t):
        return pl.ds(2 * t, 2)

    rows_of = r.n1
    gather = {}
    for k in range(1, pairs):
        t = 2 * ((pair + k) % pairs) + core
        gather[k] = remote(rows_of.at[t // G], r.gat.at[s], at_seq(t))
    relay = {0: remote(rows_of.at[b], r.gat.at[s], at_seq(sibling))}
    r.gat[s] = r.n1[b]

    for copy in get_win:
        copy.wait()
    if W < LANES:
        upper = (g * W) % LANES != 0
        r.wqkv[...] = jnp.concatenate(
            [jnp.where(upper, r.win[i][:, W:], r.win[i][:, :W]) for i in range(3)], axis=1
        )
    get_wg.wait()
    r.ag[...] = jax.nn.sigmoid(dot(n1, r.wg[...]) + r.bg[...])

    order = [r.i_order[b, i] for i in range(2 * n)]
    inverse = []
    for p in range(2 * n):
        found = jnp.int32(0)
        for i in range(2 * n):
            found = jnp.where(order[i] == p, i, found)
        inverse.append(found)
    low_block = [jnp.minimum(order[2 * t], order[2 * t + 1]) for t in range(n)]
    top_block = [jnp.maximum(order[2 * t], order[2 * t + 1]) for t in range(n)]
    split = jnp.where(r.i_kind[b] == 2, F32(NEG), F32(0.0))

    def project(t):
        out = dot(r.gat[t].reshape(L, D), r.wqkv[...])
        r.qkvst[slot(t)] = (
            jnp.concatenate([out[:, :W] * (1.0 / math.sqrt(HD)), out[:, W:]], axis=1)
            .astype(BF16)
            .reshape(2, HB, 3 * W)
        )

    project(s)
    for k in range(1, pairs):
        gather[k].wait()
        u = 2 * ((pair + pairs - k) % pairs) + core
        relay[k] = remote(r.gat.at[u], r.gat.at[u], at_seq(sibling))
        project(u)
    for k in range(pairs):
        relay[k].wait()
        project(2 * ((pair + pairs - k) % pairs) + 1 - core)

    per = QB // HB
    head_of = lax.broadcasted_iota(jnp.int32, (QB, W), 1) // HD
    of_head = [head_of == h for h in range(c.hpd)]
    for i in range(NB):
        at = slice(i * QB, (i + 1) * QB)
        block = jnp.concatenate([r.qkvst[inverse[i * per + m]] for m in range(per)], axis=0)
        q, k, v = (block[:, j * W : (j + 1) * W] for j in range(3))
        r.q[at, :] = q
        r.qT[:, at] = q.T
        r.kT[:, at] = k.T
        r.vT[:, at] = v.T
        for h in range(c.hpd):
            r.k[h, at, :] = jnp.where(of_head[h], k, BF16(0.0))
            r.v[h, at, :] = jnp.where(of_head[h], v, BF16(0.0))

    def causal(size):
        keys_at = lax.broadcasted_iota(jnp.int32, (size, size), 0)
        return keys_at <= lax.broadcasted_iota(jnp.int32, (size, size), 1)

    def attend(first, last):
        chunks = [slice(i, i + QF) for i in range(first, last, QF)]

        def head(h, carry):
            hr = pl.ds(pl.multiple_of(h * HD, HD), HD)
            for at in chunks:
                scores = dot(r.k[h, 0 : at.stop, :], r.qT[:, at])
                diagonal = jnp.where(causal(QF), scores[at.start :], NEG)
                top = jnp.max(diagonal, axis=0, keepdims=True)
                low_rows = N // 2 if at.start >= N // 2 else 0
                low = scores[:low_rows] if low_rows else None
                middle = scores[low_rows : at.start] if at.start > low_rows else None
                if middle is not None:
                    top = jnp.maximum(top, jnp.max(middle, axis=0, keepdims=True))
                if low is not None:
                    top = jnp.maximum(top, jnp.max(low, axis=0, keepdims=True) + split)
                terms = []
                if low is not None:
                    terms.append(jnp.exp(low - (top - split)))
                if middle is not None:
                    terms.append(jnp.exp(middle - top))
                terms.append(jnp.exp(diagonal - top))
                total = sum(jnp.sum(t, axis=0, keepdims=True) for t in terms)
                weights = jnp.concatenate([t.astype(BF16) for t in terms], axis=0)
                out = dot(r.vT[hr, 0 : at.stop], weights)
                r.oT[hr, at] = out * (1.0 / total)
                lse = top + jnp.log(total)
                r.lseB[h, :, at] = lse
                r.lseA[h, :, at] = lse - split if low_rows else lse
            return carry

        lax.fori_loop(0, c.hpd, head, 0)
        for at in chunks:
            r.do[at.start // HB : at.stop // HB] = (
                r.oT[:, at].astype(BF16).T.reshape(QF // HB, HB, W)
            )

    def send_rows(which, blocks):
        for t in range(n):
            r.ou[2 * t + which] = r.do[blocks[t]]
        copies = []
        for k in range(1, n):
            t = (s + k) % n
            copies.append(remote(r.ou.at[2 * t + which], r.orr.at[2 * s + which], at_seq(t)))
        r.orr[2 * s + which] = r.ou[2 * s + which]
        return copies

    attend(N // 2, N)
    going = send_rows(1, top_block)
    attend(0, N // 2)
    going += send_rows(0, low_block)

    get_wo.wait()
    get_wup.wait()
    get_wfg.wait()
    get_wdn.wait()
    get_cot.wait()
    own = [(r.i_order[i, 2 * s], r.i_order[i, 2 * s + 1]) for i in range(B)]
    which_half = [
        (jnp.where(a > z, 1, 0), jnp.where(a > z, 0, 1)) for a, z in own
    ]
    for copy in going:
        copy.wait()
    for i in range(B):
        for m in range(2):
            for j in range(G):
                r.att[i * L + m * HB : i * L + (m + 1) * HB, j * W : (j + 1) * W] = r.orr[
                    2 * (i * G + j) + which_half[i][m]
                ]
    x = inputs()
    branch = dot(r.att[...], r.wo[...]) - x
    r.bamx[...] = branch
    middle = x + r.ag[...] * branch
    r.mid[...] = middle
    normal, scale = norm_stats(middle)
    n2 = (normal * r.g2[...] + r.s2[...]).astype(BF16)
    r.n2[...] = n2
    r.n2T[...] = n2.T

    def partner(axis, bit):
        index = s if axis == "seq" else d
        mine = index // 2**bit % 2
        there = index + (1 - 2 * mine) * 2**bit
        return mine, at_seq(there) if axis == "seq" else at_dp(there)

    def add_rows(ref, start, slots, base, length):
        step = math.gcd(length, 512)

        def body(i, carry):
            at = pl.ds(pl.multiple_of(start + i * step, 16), step)
            other = slots[pl.ds(pl.multiple_of(base + i * step, 16), step), :]
            ref[at, :] = (ref[at, :].astype(F32) + other.astype(F32)).astype(BF16)
            return carry

        lax.fori_loop(0, length // step, body, 0)

    def halve(ref, slots, first, rows, bits, trail, credits):
        start, length, base = jnp.int32(first), rows, first
        for axis, bit in bits:
            half = length // 2
            mine, device = partner(axis, bit)
            keep = pl.multiple_of(start + mine * half, 16)
            give = pl.multiple_of(start + (1 - mine) * half, 16)
            copy = remote(ref.at[pl.ds(give, half)], slots.at[pl.ds(base, half)], device)
            yield
            copy.wait()
            credit = None
            if credits:
                assert count["credit"] < c.credits
                credit = r.free.at[count["credit"]]
                count["credit"] += 1
                pl.semaphore_signal(credit, inc=1, device_id=device, device_id_type=MESH)
            add_rows(ref, keep, slots, base, half)
            trail.append((keep, half, device, credit, start))
            start, length, base = keep, half, base + half

    def all_reduce(ref, slots, first, rows, bits, store):
        trail = []
        yield from halve(ref, slots, first, rows, bits, trail, True)
        for keep, half, device, credit, _ in reversed(trail):
            at = pl.ds(keep, half)
            pl.semaphore_wait(credit, 1)
            copy = remote(ref.at[at], ref.at[at], device)
            yield
            copy.wait()
        store()

    def reduce_small(own_ref, slots, dp_ref, dp_slots, out_ref):
        copies = []
        for k in range(1, n):
            copies.append(remote(own_ref, slots.at[s], at_seq((s + k) % n)))
        slots[s] = own_ref[...]
        yield
        for copy in copies:
            copy.wait()
        dp_ref[...] = sum(slots[i] for i in range(n))
        copies = []
        for k in range(1, nd):
            copies.append(remote(dp_ref, dp_slots.at[d], at_dp((d + k) % nd)))
        dp_slots[d] = dp_ref[...]
        yield
        for copy in copies:
            copy.wait()
        out_ref[...] = sum(dp_slots[i] for i in range(nd))

    jobs = {}

    def begin(name, job):
        jobs[name] = job
        next(job)

    def advance(name):
        if next(jobs[name], "over") == "over":
            del jobs[name]

    cores = [("seq", 0)]
    chips = [("seq", i) for i in range(1, c.seq_bits)]
    planes = [("dp", i) for i in range(c.dp_bits)]
    bits_of = dict(c=cores, x=chips[:1], y=chips[1:])
    bits_of["1"], bits_of["2"] = planes[:1], planes[1:]

    def bits_in(name):
        return [bit for mark in ORDERS[name] for bit in bits_of[mark]]

    puts = []

    def down_chunk(j, carry):
        part = dot_tn(r.hid[pl.ds(pl.multiple_of(j * T, T), T), :], r.dffn[...]).astype(BF16)
        for i in range(c.LP):
            at = pl.ds(pl.multiple_of((j * c.LP + i) * FC, FC), FC)
            r.fa[at, :] = part[:, i * LANES : (i + 1) * LANES]
        return carry

    def up_chunk(j, carry):
        part = dot(r.n2T[...], r.gp[j].astype(BF16)).astype(BF16)
        for i in range(FC // LANES):
            at = pl.ds(pl.multiple_of((j * (FC // LANES) + i) * D, D), D)
            r.fb[at, :] = part[:, i * LANES : (i + 1) * LANES]
        return carry

    def put_down(chunks):
        for j in chunks:
            for i in range(c.LP):
                at = (j * c.LP + i) * FC
                puts.append(
                    local(
                        r.fa.at[at : at + FC],
                        r.o_dn.at[j * FC : (j + 1) * FC, i * LANES : (i + 1) * LANES],
                    )
                )

    def put_up(chunks):
        per_chunk = FC // LANES
        for i in range(chunks.start * per_chunk, chunks.stop * per_chunk):
            puts.append(
                local(r.fb.at[i * D : (i + 1) * D], r.o_up.at[:, i * LANES : (i + 1) * LANES])
            )

    def put_rest():
        for j, ref in enumerate((r.o_out, r.o_ag, r.o_fg)):
            for i in range(c.LP):
                at = (j * c.LP + i) * D
                puts.append(
                    local(r.fc.at[at : at + D], ref.at[:, i * LANES : (i + 1) * LANES])
                )

    def feed_forward_sum(name, half, chunk, ref, slots, rows, put):
        chunks = range(half * NC // 2, (half + 1) * NC // 2)
        lax.fori_loop(chunks.start, chunks.stop, chunk, 0, unroll=True)
        begin(
            name,
            all_reduce(
                ref,
                slots,
                chunks.start * (rows // NC),
                rows // 2,
                bits_in(name),
                functools.partial(put, chunks),
            ),
        )

    steps = {}

    def step(function):
        steps[function.__name__] = function

    slope = math.sqrt(2.0 / math.pi)
    r.acc[...] = jnp.zeros((T, D), F32)

    def forward_chunk(j, carry):
        cols = pl.ds(pl.multiple_of(j * FC, FC), FC)
        u = dot(r.n2[...], r.wup[:, cols])
        square = u * u
        t = jnp.tanh(slope * u * (1.0 + 0.044715 * square))
        half = 0.5 * (1.0 + t)
        hidden = (u * half).astype(BF16)
        r.hid[pl.ds(pl.multiple_of(j * T, T), T), :] = hidden
        r.gp[j] = half + 0.5 * u * (1.0 - t * t) * (slope * (1.0 + 3 * 0.044715 * square))
        r.acc[...] += dot(hidden, r.wdn[cols, :])
        return carry

    lax.fori_loop(0, NC, forward_chunk, 0, unroll=2)
    gate = jax.nn.sigmoid(dot(r.n2[...], r.wfg[...]) + r.bfg[...])
    middle = r.mid[...]
    apart = r.acc[...] - middle
    grad = jnp.concatenate([r.cot[:, i, :].astype(F32) for i in range(B)], axis=0)
    mixed = (middle + gate * apart).astype(BF16)
    for i in range(B):
        r.cot[:, i, :] = mixed[i * L : (i + 1) * L]
    puts.append(local(r.cot, r.o_mix))
    r.dffn[...] = (grad * gate).astype(BF16)
    d_pre = (grad * apart * gate * (1.0 - gate)).astype(BF16)
    r.dpre[...] = d_pre
    r.sm[0:1, :] = jnp.sum(d_pre.astype(F32), axis=0, keepdims=True)
    r.dxr[...] = grad * (1.0 - gate)
    r.acc[...] = dot_nt(d_pre, r.wfg[...])

    @step
    def down_1():
        feed_forward_sum("a", 0, down_chunk, r.fa, r.sa, c.rows_a, put_down)

    @step
    def down_2():
        feed_forward_sum("b", 1, down_chunk, r.fa, r.sa, c.rows_a, put_down)

    def backward_chunk(j, carry):
        cols = pl.ds(pl.multiple_of(j * FC, FC), FC)
        d_hidden = dot_nt(r.dffn[...], r.wdn[cols, :])
        d_up = (d_hidden * r.gp[j]).astype(BF16)
        r.gp[j] = d_up.astype(F32)
        r.acc[...] += dot_nt(d_up, r.wup[:, cols])
        return carry

    @step
    def back_1():
        lax.fori_loop(0, NC // 2, backward_chunk, 0, unroll=True)

    @step
    def back_2():
        lax.fori_loop(NC // 2, NC, backward_chunk, 0, unroll=True)

    back = []

    @step
    def branch_back():
        d_norm = r.acc[...]
        normal, scale = norm_stats(r.mid[...])
        r.sm[1:2, :] = jnp.sum(d_norm * normal, axis=0, keepdims=True)
        r.sm[2:3, :] = jnp.sum(d_norm, axis=0, keepdims=True)
        d_middle = r.dxr[...] + norm_back(d_norm, r.g2[...], normal, scale)
        gate = r.ag[...]
        d_att = (d_middle * gate).astype(BF16)
        d_attn_pre = (d_middle * r.bamx[...] * gate * (1.0 - gate)).astype(BF16)
        r.datt[...] = d_att
        r.dapre[...] = d_attn_pre
        r.sm[3:4, :] = jnp.sum(d_attn_pre.astype(F32), axis=0, keepdims=True)
        r.sm[4:8, :] = jnp.zeros((4, D), F32)
        r.dxr[...] = d_middle * (1.0 - gate)
        d_o = dot_nt(d_att, r.wo[...]).astype(BF16)
        for i in range(B):
            for j in range(G):
                r.ou[2 * (i * G + j) : 2 * (i * G + j) + 2] = d_o[
                    i * L : (i + 1) * L, j * W : (j + 1) * W
                ].reshape(2, HB, W)
        for k in range(1, n):
            t = (s + k) % n
            back.append(remote(r.ou.at[slot(t)], r.dor.at[slot(s)], at_seq(t)))
        r.dor[slot(s)] = r.ou[slot(s)]

    @step
    def up_1():
        feed_forward_sum("c", 0, up_chunk, r.fb, r.sb, c.rows_b, put_up)

    @step
    def up_2():
        feed_forward_sum("d", 1, up_chunk, r.fb, r.sb, c.rows_b, put_up)

    @step
    def other_weights():
        begin("s", reduce_small(r.sm, r.smr, r.smd, r.smdr, r.o_sm))
        for j, part in enumerate(
            (
                dot_tn(r.att[...], r.datt[...]),
                dot_tn(r.n1[...].reshape(T, D), r.dapre[...]),
                dot(r.n2T[...], r.dpre[...]),
            )
        ):
            part = part.astype(BF16)
            for i in range(c.LP):
                at = (j * c.LP + i) * D
                r.fc[at : at + D, :] = part[:, i * LANES : (i + 1) * LANES]
        if c.rows_c > c.used_c:
            r.fc[c.used_c :, :] = jnp.zeros((c.rows_c - c.used_c, LANES), BF16)
        begin("e", all_reduce(r.fc, r.sc, 0, c.rows_c, bits_in("e"), put_rest))
        r.acc[...] = dot_nt(r.dapre[...], r.wg[...])

    @step
    def by_position():
        for i in range(2 * n):
            r.hid[i * HB : (i + 1) * HB, :] = r.gat[inverse[i] // 2, inverse[i] % 2]
        for copy in back:
            copy.wait()
        for i in range(NB):
            at = slice(i * QB, (i + 1) * QB)
            block = jnp.concatenate([r.dor[inverse[i * per + m]] for m in range(per)], axis=0)
            r.do[i * per : (i + 1) * per] = block.reshape(per, HB, W)
            turned = block.T
            r.doT[:, at] = turned
            product = turned.astype(F32) * r.oT[:, at]
            for h in range(c.hpd):
                r.odot[h, :, at] = jnp.sum(product[h * HD : (h + 1) * HD], axis=0, keepdims=True)

    def backward_block(j):
        at = slice(j * QB, (j + 1) * QB)
        lse_ref = r.lseA if j < HALF else r.lseB
        keys_t = []
        for h in range(c.hpd):
            own = [
                r.kT[h * HD : (h + 1) * HD, at] if i == h else jnp.zeros((HD, QB), BF16)
                for i in range(c.hpd)
            ]
            keys_t.append(jnp.concatenate(own, axis=0))
        keys_t = jnp.concatenate(keys_t, axis=1)
        d_keys, d_values = [0.0] * c.hpd, [0.0] * c.hpd
        for start in range(j * QB, N, N // 2):
            to = slice(start, min(start + N // 2, N))
            slopes = []
            for h in range(c.hpd):
                p = jnp.exp(dot(r.k[h, at, :], r.qT[:, to]) - lse_ref[h, :, to])
                if start == j * QB:
                    corner = jnp.where(causal(QB), p[:, :QB], 0.0)
                    p = jnp.concatenate([corner, p[:, QB:]], axis=1) if j < NB - 1 else corner
                dp = dot(r.v[h, at, :], r.doT[:, to])
                ds = (p * (dp - r.odot[h, :, to])).astype(BF16)
                slopes.append(ds)
                d_values[h] += dot(
                    p.astype(BF16), r.do[to.start // HB : to.stop // HB].reshape(-1, W)
                )
                d_keys[h] += dot(ds, r.q[to, :])
            part = dot(keys_t, jnp.concatenate(slopes, axis=0))
            if j == 0:
                r.dqT[:, to] = part
            else:
                r.dqT[:, to] += part
        for h in range(c.hpd):
            r.v[h, at, :] = d_values[h].astype(BF16)
            r.k[h, at, :] = d_keys[h].astype(BF16)

    def partial(at):
        return r.gat[at // 2, at % 2]

    def finish_half(which, blocks):
        for i in blocks:
            at = slice(i * QB, (i + 1) * QB)
            parts = [(r.dqT[:, at] * (1.0 / math.sqrt(HD))).astype(BF16).T]
            for ref in (r.k, r.v):
                part = ref[0, at, :]
                for h in range(1, c.hpd):
                    part = jnp.where(of_head[h], ref[h, at, :], part)
                parts.append(part)
            rows = jnp.concatenate(parts, axis=1)
            r.qkvst[i * per : (i + 1) * per] = rows.reshape(per, HB, 3 * W)
            r.gat[i * per // 2 : (i + 1) * per // 2] = (
                dot_nt(rows, r.wqkv[...]).astype(BF16).reshape(per // 2, 2, HB, D)
            )
        table = top_block if which else low_block

        def pick(m, parity):
            return jnp.where(parity == 0, table[2 * m], table[2 * m + 1])

        for m in range(pairs):
            r.sibs[which, m] = partial(pick(m, 1 - core))
        return remote(r.sibs.at[which], r.sibr.at[which], at_seq(sibling)), pick

    def pass_on(which, copy, pick):
        copy.wait()
        for m in range(pairs):
            r.sibs[which, m] = (
                partial(pick(m, core)).astype(F32) + r.sibr[which, m].astype(F32)
            ).astype(BF16)
        copies = []
        for k in range(1, pairs):
            m = (pair + k) % pairs
            copies.append(
                remote(r.sibs.at[which, m], r.dnr.at[pair, which], at_seq(2 * m + core))
            )
        r.dnr[pair, which] = r.sibs[which, pair]
        return copies

    def weight_part(which):
        rows = slice(which * N // 2, (which + 1) * N // 2)
        return dot_tn(r.hid[rows, :], r.qkvst[which * n : (which + 1) * n].reshape(N // 2, 3 * W))

    arriving = []
    held_up = {}

    for j in range(NB):
        steps[f"low_{j}" if j < HALF else f"top_{j - HALF}"] = functools.partial(backward_block, j)

    @step
    def finish_low():
        held_up[0] = finish_half(0, range(HALF))

    @step
    def weights_low():
        r.wacc[...] = weight_part(0)

    @step
    def pass_low():
        arriving.extend(pass_on(0, *held_up[0]))

    @step
    def finish_top():
        held_up[1] = finish_half(1, range(HALF, NB))

    @step
    def pass_top():
        arriving.extend(pass_on(1, *held_up[1]))

    group_bits = log2(G)
    buffers = [("seq", i) for i in range(group_bits, c.seq_bits)]
    members = [("seq", i) for i in range(1, group_bits)]

    def heads_reduce(first, bits, members_at):
        trail = []
        yield from halve(r.fq, r.sq, first, D, bits, trail, False)
        start, length = trail[-1][0], trail[-1][1]
        r.resq[g, pl.ds(start, length), :] = r.fq[pl.ds(start, length), :]
        steps = [("rows", step) for step in reversed(trail)]
        steps[members_at:members_at] = [("members", bit) for bit in members]
        steps.append(("members", cores[0]))
        held = [g]
        for kind, step in steps:
            at = pl.ds(start, length)
            if kind == "rows":
                device = step[2]
            else:
                mine, device = partner(*step)
            copies = [remote(r.resq.at[i, at], r.resq.at[i, at], device) for i in held]
            yield
            for copy in copies:
                copy.wait()
            if kind == "rows":
                start, length = pl.multiple_of(step[4], 16), 2 * length
            else:
                held = held + [i + (1 - 2 * mine) * 2 ** step[1] for i in held]

    splits = len(buffers + planes)

    @step
    def weights_top():
        part = (r.wacc[...] + weight_part(1)).astype(BF16)
        if c.np3 * LANES > 3 * W:
            part = jnp.concatenate([part, jnp.zeros((D, c.np3 * LANES - 3 * W), BF16)], axis=1)
        for i in range(c.np3):
            r.fq[i * D : (i + 1) * D, :] = part[:, i * LANES : (i + 1) * LANES]
            bits, at = (
                (buffers + planes, splits),
                (planes + buffers, 0),
                (buffers + planes, splits - len(buffers)),
            )[i]
            begin("qkv"[i], heads_reduce(i * D, bits, at))

    @step
    def first_back():
        for copy in arriving:
            copy.wait()
        parts = []
        for i in range(B):
            for m in range(2):
                parts.append(
                    sum(
                        r.dnr[i * (G // 2) + j, which_half[i][m]].astype(F32) for j in range(G // 2)
                    )
                )
        d_norm = jnp.concatenate(parts, axis=0) + r.acc[...]
        normal, scale = norm_stats(inputs())
        r.sm2[0:1, :] = jnp.sum(d_norm * normal, axis=0, keepdims=True)
        r.sm2[1:2, :] = jnp.sum(d_norm, axis=0, keepdims=True)
        r.sm2[2:8, :] = jnp.zeros((6, D), F32)
        begin("t", reduce_small(r.sm2, r.sm2r, r.sm2d, r.sm2dr, r.o_sm2))
        grads = (r.dxr[...] + norm_back(d_norm, r.g1[...], normal, scale)).astype(BF16)
        for i in range(B):
            r.tok[:, i, :] = grads[i * L : (i + 1) * L]
        puts.append(local(r.tok, r.o_tok))

    for name in SCHEDULE:
        if name in steps:
            steps.pop(name)()
        elif name in jobs:
            advance(name)
    assert not steps
    while jobs:
        for name in list(jobs):
            advance(name)

    outs = (r.o_q, r.o_k, r.o_v)
    for i in range(G):
        if W == LANES:
            for j, ref in enumerate(outs):
                puts.append(
                    local(
                        r.resq.at[i, j * D : (j + 1) * D], ref.at[:, i * LANES : (i + 1) * LANES]
                    )
                )
            continue
        block = jnp.concatenate(
            [r.resq[i, m * D : (m + 1) * D, :] for m in range(c.np3)], axis=1
        )
        for j in range(3):
            r.gqkv[j, :, i * W : (i + 1) * W] = block[:, j * W : (j + 1) * W]
    if W < LANES:
        for j, ref in enumerate(outs):
            puts.append(local(r.gqkv.at[j], ref))
    for put in puts:
        put.wait()


def blocks_of(shapes):
    blocks = []
    for i, (rows, columns) in enumerate(shapes):
        step = min(rows, 2**18 // columns)
        blocks += [(i, at, step) for at in range(0, rows, step)]
    return blocks


def widen(arrays, blocks, *refs):
    refs = iter(refs)
    take = lambda number: [next(refs) for _ in range(number)]
    grads, rest, small = take(arrays), take(2), take(2)
    wide, rest_out, rows = take(arrays), take(2), take(6)
    held, held_wide, held_rest = take(arrays), take(arrays), take(2)
    (sems,) = take(1)
    loads = []
    for j, (i, at, step) in enumerate(blocks):
        block = pl.ds(at, step)
        loads.append(pltpu.make_async_copy(grads[i].at[block], held[i].at[block], sems.at[0, j]))
    for j in range(2):
        loads.append(
            pltpu.make_async_copy(rest[j], held_rest[j], sems.at[0, len(blocks) + j])
        )
    for load in loads:
        load.start()
    for j, row in enumerate(rows):
        row[...] = small[j // 4][j % 4 : j % 4 + 1, :]
    stores = []
    for j, (i, at, step) in enumerate(blocks):
        block = pl.ds(at, step)
        loads[j].wait()
        part = min(step, 64)

        def body(m, carry):
            here = pl.ds(pl.multiple_of(at + m * part, part), part)
            held_wide[i][here, :] = held[i][here, :].astype(F32)
            return carry

        lax.fori_loop(0, step // part, body, 0)
        stores.append(
            pltpu.make_async_copy(held_wide[i].at[block], wide[i].at[block], sems.at[1, j])
        )
        stores[-1].start()
    for j in range(2):
        loads[len(blocks) + j].wait()
        stores.append(
            pltpu.make_async_copy(held_rest[j], rest_out[j], sems.at[1, len(blocks) + j])
        )
        stores[-1].start()
    for store in stores:
        store.wait()


def solution(mesh):
    n, nd = mesh.shape["seq"], mesh.shape["dp"]

    def local(
        tokens,
        cotangent,
        query_weight,
        key_weight,
        value_weight,
        output_weight,
        attn_gate_weight,
        attn_gate_bias,
        up_weight,
        down_weight,
        ffn_gate_weight,
        ffn_gate_bias,
        first_gain,
        first_shift,
        second_gain,
        second_shift,
        row_kind,
        block_order,
    ):
        L, B, D = tokens.shape
        FF = up_weight.shape[1]
        c = sizes(n, nd, L, B, D, FF)
        spaces = scratch(c)
        names = IN_NAMES + OUT_NAMES + list(spaces)
        smem = pl.BlockSpec(memory_space=pltpu.SMEM)
        vmem = pl.BlockSpec(memory_space=pltpu.VMEM)
        hbm = pl.BlockSpec(memory_space=pl.ANY)

        def shape(*dims, dtype=BF16):
            return jax.ShapeDtypeStruct(dims, dtype)

        def row(vector):
            return vector.reshape(1, -1)

        out = pl.pallas_call(
            functools.partial(kernel, c, names),
            out_shape=(
                shape(L, B, D),
                shape(L, B, D),
                shape(D, D),
                shape(D, D),
                shape(D, D),
                shape(D, D),
                shape(D, D),
                shape(D, FF),
                shape(FF, D),
                shape(D, D),
                shape(8, D, dtype=F32),
                shape(8, D, dtype=F32),
            ),
            in_specs=[smem] * 2 + [hbm] * 16,
            out_specs=(hbm,) * 10 + (vmem,) * 2,
            scratch_shapes=list(spaces.values()),
            compiler_params=pltpu.CompilerParams(
                collective_id=0, has_side_effects=True, vmem_limit_bytes=VMEM_BYTES
            ),
            name="layer",
        )(
            block_order,
            row_kind,
            row(attn_gate_bias),
            row(ffn_gate_bias),
            row(first_gain),
            row(first_shift),
            row(second_gain),
            row(second_shift),
            tokens,
            cotangent,
            query_weight,
            key_weight,
            value_weight,
            output_weight,
            attn_gate_weight,
            up_weight,
            down_weight,
            ffn_gate_weight,
        )
        mix, tok, *grads, small, small2 = out
        shapes = [a.shape for a in grads]
        wide = pl.pallas_call(
            functools.partial(widen, len(grads), blocks_of(shapes)),
            out_shape=tuple(shape(*dims, dtype=F32) for dims in shapes)
            + (shape(L, B, D),) * 2
            + (shape(1, D, dtype=F32),) * 6,
            in_specs=[hbm] * (len(grads) + 2) + [vmem] * 2,
            out_specs=(hbm,) * (len(grads) + 2) + (vmem,) * 6,
            scratch_shapes=[pltpu.VMEM(dims, BF16) for dims in shapes]
            + [pltpu.VMEM(dims, F32) for dims in shapes]
            + [pltpu.VMEM((L, B, D), BF16)] * 2
            + [pltpu.SemaphoreType.DMA((2, len(blocks_of(shapes)) + 2))],
            compiler_params=pltpu.CompilerParams(vmem_limit_bytes=VMEM_BYTES),
            name="widen",
        )(*grads, mix, tok, small, small2)
        dq, dk, dv, dout, dag, dup, ddn, dfg, mix, tok = wide[:10]
        bfg, g2, s2, bg, g1, s1 = (a.reshape(D) for a in wide[10:])
        return mix, tok, dq, dk, dv, dout, dag, bg, dup, ddn, dfg, bfg, g1, s1, g2, s2

    sharded = P("seq", "dp", None)
    return jax.shard_map(
        local,
        mesh=mesh,
        in_specs=(sharded, sharded) + (P(),) * 14 + (P("dp"), P("dp", None)),
        out_specs=(sharded, sharded) + (P(),) * 14,
        check_vma=False,
    )


VMEM_BYTES = 63 * 2**20
```

```python
import functools
import math
from types import SimpleNamespace

import jax
import jax.numpy as jnp
from jax import lax
from jax.experimental import pallas as pl
from jax.experimental.pallas import tpu as pltpu
from jax.sharding import PartitionSpec as P

H = 8
HD = 64
NEG = -1e30
EPS = 1e-05
MESH = pl.DeviceIdType.MESH
F32 = jnp.float32
BF16 = jnp.bfloat16
LANES = 128


def dot(a, b):
    return jnp.dot(a, b, preferred_element_type=F32)


def dot_nt(a, b):
    return lax.dot_general(a, b, (((1,), (1,)), ((), ())), preferred_element_type=F32)


def dot_tn(a, b):
    return lax.dot_general(a, b, (((0,), (0,)), ((), ())), preferred_element_type=F32)


def log2(value):
    return value.bit_length() - 1


def sizes(n, nd, rows, buffers, features, hidden):
    c = SimpleNamespace(n=n, nd=nd, L=rows, B=buffers, D=features, FF=hidden)
    c.T = rows * buffers
    c.N = rows * n
    c.HB = rows // 2
    c.G = n // buffers
    c.hpd = H // c.G
    c.W = c.hpd * HD
    c.QB = min(256, c.N // 2)
    c.QF = min(512, c.N // 2)
    c.NB = c.N // c.QB
    c.HALF = c.NB // 2
    c.FC = 512
    c.NC = hidden // c.FC
    c.LP = features // LANES
    unit = 16 * n * nd
    c.rows_a = hidden * c.LP
    c.rows_b = (hidden // LANES) * features
    c.rows_c = -(-(3 * features * c.LP) // unit) * unit
    c.used_c = 3 * features * c.LP
    c.np3 = -(-(3 * c.W) // LANES)
    c.rows_q = c.np3 * features
    c.seq_bits = log2(n)
    c.dp_bits = log2(nd)
    c.remotes = 12 * n + 2 * nd + 10 * (c.seq_bits + c.dp_bits)
    c.credits = 5 * (c.seq_bits + c.dp_bits)
    c.locals = 32 + c.NC * c.LP + hidden // LANES + 3 * c.LP + 3 * c.G
    return c


def scratch(c):
    v = pltpu.VMEM
    spaces = dict(
        tok=v((2, c.HB, c.B, c.D), BF16),
        cot=v((2, c.HB, c.B, c.D), BF16),
        xs=v((c.T, c.D), BF16),
        bg=v((1, c.D), F32),
        bfg=v((1, c.D), F32),
        g1=v((1, c.D), F32),
        s1=v((1, c.D), F32),
        g2=v((1, c.D), F32),
        s2=v((1, c.D), F32),
        win=v((3, c.D, LANES) if c.W < LANES else (3, 16, LANES), BF16),
        wqkv=v((c.D, 3 * c.W), BF16),
        wg=v((c.D, c.D), BF16),
        wo=v((c.D, c.D), BF16),
        wup=v((c.D, c.FF), BF16),
        wdn=v((c.FF, c.D), BF16),
        wfg=v((c.D, c.D), BF16),
        n1=v((2, c.B, c.HB, c.D), BF16),
        gat=v((c.n, 2, c.HB, c.D), BF16),
        qkvst=v((2 * c.n, c.HB, 3 * c.W), BF16),
        q=v((c.N, c.W), BF16),
        k=v((c.hpd, c.N, c.W), BF16),
        v=v((c.hpd, c.N, c.W), BF16),
        do=v((2 * c.n, c.HB, c.W), BF16),
        kT=v((c.W, c.N), BF16),
        qT=v((c.W, c.N), BF16),
        vT=v((c.W, c.N), BF16),
        doT=v((c.W, c.N), BF16),
        oT=v((c.W, c.N), F32),
        dqT=v((c.W, c.N), F32),
        lseA=v((c.hpd, 1, c.N), F32),
        lseB=v((c.hpd, 1, c.N), F32),
        odot=v((c.hpd, 1, c.N), F32),
        ou=v((2 * c.n, c.HB, c.W), BF16),
        orr=v((2 * c.n, c.HB, c.W), BF16),
        dor=v((2 * c.n, c.HB, c.W), BF16),
        att=v((c.T, c.D), BF16),
        ag=v((c.T, c.D), F32),
        mid=v((c.T, c.D), F32),
        bamx=v((c.T, c.D), F32),
        acc=v((c.T, c.D), F32),
        dxr=v((c.T, c.D), F32),
        n2=v((c.T, c.D), BF16),
        n2T=v((c.D, c.T), BF16),
        gp=v((c.NC, c.T, c.FC), F32),
        hid=v((max(c.NC * c.T, c.N), c.FC), BF16),
        dffn=v((c.T, c.D), BF16),
        dpre=v((c.T, c.D), BF16),
        datt=v((c.T, c.D), BF16),
        dapre=v((c.T, c.D), BF16),
        wacc=v((c.D, 3 * c.W), F32),
        sibs=v((2, c.n // 2, c.HB, c.D), BF16),
        sibr=v((2, c.n // 2, c.HB, c.D), BF16),
        dnr=v((c.n // 2, 2, c.HB, c.D), BF16),
        fa=v((c.rows_a, LANES), BF16),
        fb=v((c.rows_b, LANES), BF16),
        fc=v((c.rows_c, LANES), BF16),
        fq=v((c.rows_q, LANES), BF16),
        sa=v((c.rows_a, LANES), BF16),
        sb=v((c.rows_b, LANES), BF16),
        sc=v((c.rows_c, LANES), BF16),
        sq=v((c.rows_q, LANES), BF16),
        resq=v((c.G, c.rows_q, LANES), BF16),
        gqkv=v((3, c.D, c.D) if c.W < LANES else (3, 16, LANES), BF16),
        sm=v((8, c.D), F32),
        smr=v((c.n, 8, c.D), F32),
        smd=v((8, c.D), F32),
        smdr=v((c.nd, 8, c.D), F32),
        sm2=v((8, c.D), F32),
        sm2r=v((c.n, 8, c.D), F32),
        sm2d=v((8, c.D), F32),
        sm2dr=v((c.nd, 8, c.D), F32),
        ss=pltpu.SemaphoreType.DMA((c.remotes,)),
        rs=pltpu.SemaphoreType.DMA((c.remotes,)),
        ls=pltpu.SemaphoreType.DMA((c.locals,)),
        free=pltpu.SemaphoreType.REGULAR((c.credits,)),
    )
    return spaces


ORDERS = dict(a="c1xy2", b="cyx21", c="cxy12", d="cy21x", e="c1xy2")
SCHEDULE = [
    "down_1",
    "down_2",
    "back_1",
    "a",
    "b",
    "back_2",
    "branch_back",
    "up_1",
    "up_2",
    "other_weights",
    "a",
    "c",
    "d",
    "e",
    "b",
    "s",
    "s",
    "a",
    "d",
    "by_position",
    "e",
    "b",
    "low_0",
    "c",
    "a",
    "low_1",
    "e",
    "low_2",
    "c",
    "b",
    "a",
    "low_3",
    "e",
    "d",
    "finish_low",
    "b",
    "a",
    "c",
    "weights_low",
    "pass_low",
    "e",
    "top_0",
    "c",
    "b",
    "a",
    "d",
    "top_1",
    "top_2",
    "e",
    "top_3",
    "finish_top",
    "c",
    "d",
    "weights_top",
    "b",
    "pass_top",
    "e",
    "c",
    "d",
    "k",
    "a",
    "q",
    "v",
    "k",
    "d",
    "k",
    "q",
    "v",
    "c",
    "k",
    "b",
    "q",
    "v",
    "k",
    "q",
    "v",
    "e",
    "d",
    "b",
    "first_back",
    "q",
    "b",
    "k",
    "c",
    "a",
    "v",
    "c",
    "a",
    "v",
    "t",
    "q",
    "d",
    "k",
    "v",
    "t",
    "d",
    "q",
    "k",
    "v",
    "e",
    "q",
    "e",
]
IN_NAMES = [
    "i_order",
    "i_kind",
    "i_bg",
    "i_bfg",
    "i_g1",
    "i_s1",
    "i_g2",
    "i_s2",
    "i_tok",
    "i_cot",
    "i_wq",
    "i_wk",
    "i_wv",
    "i_wo",
    "i_wg",
    "i_wup",
    "i_wdn",
    "i_wfg",
]
OUT_NAMES = [
    "o_mix",
    "o_tok",
    "o_q",
    "o_k",
    "o_v",
    "o_out",
    "o_ag",
    "o_up",
    "o_dn",
    "o_fg",
    "o_sm",
    "o_sm2",
]


def norm_stats(values):
    average = jnp.mean(values, axis=-1, keepdims=True)
    centred = values - average
    variance = jnp.mean(centred * centred, axis=-1, keepdims=True)
    scale = lax.rsqrt(variance + EPS)
    return centred * scale, scale


def norm_back(grad, gain, normal, scale):
    e = grad * gain
    return scale * (
        e
        - jnp.mean(e, axis=-1, keepdims=True)
        - normal * jnp.mean(e * normal, axis=-1, keepdims=True)
    )


def kernel(c, names, *refs):
    r = SimpleNamespace(**dict(zip(names, refs)))
    n, nd, L, B, D, T, N, HB, G, W = c.n, c.nd, c.L, c.B, c.D, c.T, c.N, c.HB, c.G, c.W
    QB, NB, HALF, FC, NC, QF = c.QB, c.NB, c.HALF, c.FC, c.NC, c.QF
    s = lax.axis_index("seq")
    d = lax.axis_index("dp")
    b = s // G
    g = s % G
    core = s % 2
    pair = s // 2
    pairs = n // 2
    sibling = s + 1 - 2 * core
    count = dict(remote=0, local=0, credit=0)

    def remote(src, dst, device):
        i = count["remote"]
        assert i < c.remotes
        count["remote"] += 1
        copy = pltpu.make_async_remote_copy(
            src_ref=src,
            dst_ref=dst,
            send_sem=r.ss.at[i],
            recv_sem=r.rs.at[i],
            device_id=device,
            device_id_type=MESH,
        )
        copy.start()
        return copy

    def local(src, dst):
        i = count["local"]
        assert i < c.locals
        count["local"] += 1
        copy = pltpu.make_async_copy(src, dst, r.ls.at[i])
        copy.start()
        return copy

    def at_seq(t):
        return {"seq": t, "dp": d}

    def at_dp(t):
        return {"seq": s, "dp": t}

    def halves(ref):
        return [ref.at[pl.ds(m * HB, HB)] for m in range(2)]

    get_tok = [local(part, r.tok.at[m]) for m, part in enumerate(halves(r.i_tok))]
    get_rows = [
        local(getattr(r, "i_" + name), getattr(r, name))
        for name in ("g1", "s1", "bg", "g2", "s2", "bfg")
    ]
    window = pl.multiple_of((g * W) // LANES * LANES, LANES)
    get_win = [
        local(
            ref.at[:, pl.ds(window, LANES)],
            r.win.at[i] if W < LANES else r.wqkv.at[:, i * LANES : (i + 1) * LANES],
        )
        for i, ref in enumerate((r.i_wq, r.i_wk, r.i_wv))
    ]
    get_wg = local(r.i_wg, r.wg)
    get_cot = [local(part, r.cot.at[m]) for m, part in enumerate(halves(r.i_cot))]
    get_wo = local(r.i_wo, r.wo)
    get_wup = local(r.i_wup, r.wup)
    get_wfg = local(r.i_wfg, r.wfg)
    get_wdn = local(r.i_wdn, r.wdn)
    barrier = pltpu.get_barrier_semaphore()
    for k in range(1, n):
        pl.semaphore_signal(barrier, inc=1, device_id=at_seq((s + k) % n), device_id_type=MESH)
    for k in range(1, nd):
        pl.semaphore_signal(barrier, inc=1, device_id=at_dp((d + k) % nd), device_id_type=MESH)

    low_first = [r.i_order[i, 2 * s] < r.i_order[i, 2 * s + 1] for i in range(B)]

    def by_half(ref):
        return jnp.concatenate(
            [
                jnp.where(low_first[i], ref[m, :, i, :], ref[1 - m, :, i, :])
                for m in range(2)
                for i in range(B)
            ],
            axis=0,
        )

    def as_stored(rows, ref):
        parts = rows.reshape(2, B, HB, D)
        for i in range(B):
            for m in range(2):
                ref[m, :, i, :] = jnp.where(low_first[i], parts[m, i], parts[1 - m, i])

    for copy in get_tok:
        copy.wait()
    r.xs[...] = by_half(r.tok)

    def inputs():
        return r.xs[...].astype(F32)

    normal, _ = norm_stats(inputs())
    for copy in get_rows:
        copy.wait()
    n1 = (normal * r.g1[...] + r.s1[...]).astype(BF16)
    r.n1[...] = n1.reshape(2, B, HB, D)

    pl.semaphore_wait(barrier, n - 1 + nd - 1)

    def slot(t):
        return pl.ds(2 * t, 2)

    gather, relay = ({}, {}), ({}, {})

    def send_half(m):
        for k in range(1, pairs):
            t = 2 * ((pair + k) % pairs) + core
            gather[m][k] = remote(r.n1.at[m, t // G], r.gat.at[s, m], at_seq(t))
        relay[m][0] = remote(r.n1.at[m, b], r.gat.at[s, m], at_seq(sibling))
        r.gat[s, m] = r.n1[m, b]

    send_half(0)

    for copy in get_win:
        copy.wait()
    if W < LANES:
        upper = (g * W) % LANES != 0
        r.wqkv[...] = jnp.concatenate(
            [jnp.where(upper, r.win[i][:, W:], r.win[i][:, :W]) for i in range(3)], axis=1
        )
    get_wg.wait()
    r.ag[...] = jax.nn.sigmoid(dot(n1, r.wg[...]) + r.bg[...])

    order = [r.i_order[b, i] for i in range(2 * n)]
    low_block = [jnp.minimum(order[2 * t], order[2 * t + 1]) for t in range(n)]
    top_block = [jnp.maximum(order[2 * t], order[2 * t + 1]) for t in range(n)]
    holder = []
    for p in range(2 * n):
        found = jnp.int32(0)
        for t in range(n):
            found = jnp.where((low_block if p < n else top_block)[t] == p, t, found)
        holder.append(found)
    split = jnp.where(r.i_kind[b] == 2, F32(NEG), F32(0.0))

    def project(t, m):
        out = dot(r.gat[t, m], r.wqkv[...])
        r.qkvst[2 * t + m] = jnp.concatenate(
            [out[:, :W] * (1.0 / math.sqrt(HD)), out[:, W:]], axis=1
        ).astype(BF16)

    for k in range(1, pairs):
        gather[0][k].wait_send()
    send_half(1)
    for m in range(2):
        project(s, m)

    per = QB // HB
    head_of = lax.broadcasted_iota(jnp.int32, (QB, W), 1) // HD
    of_head = [head_of == h for h in range(c.hpd)]

    def collect(m):
        for k in range(1, pairs):
            gather[m][k].wait_recv() if m == 0 else gather[m][k].wait()
            u = 2 * ((pair + pairs - k) % pairs) + core
            relay[m][k] = remote(r.gat.at[u, m], r.gat.at[u, m], at_seq(sibling))
            project(u, m)
        for k in range(pairs):
            relay[m][k].wait()
            project(2 * ((pair + pairs - k) % pairs) + 1 - core, m)
        for i in range(m * HALF, m * HALF + HALF):
            at = slice(i * QB, (i + 1) * QB)
            block = jnp.concatenate(
                [r.qkvst[2 * holder[i * per + j] + m] for j in range(per)], axis=0
            )
            q, k, v = (block[:, j * W : (j + 1) * W] for j in range(3))
            r.q[at, :] = q
            r.qT[:, at] = q.T
            r.kT[:, at] = k.T
            r.vT[:, at] = v.T
            for h in range(c.hpd):
                r.k[h, at, :] = jnp.where(of_head[h], k, BF16(0.0))
                r.v[h, at, :] = jnp.where(of_head[h], v, BF16(0.0))

    def causal(size):
        keys_at = lax.broadcasted_iota(jnp.int32, (size, size), 0)
        return keys_at <= lax.broadcasted_iota(jnp.int32, (size, size), 1)

    def attend(first, last):
        chunks = [slice(i, i + QF) for i in range(first, last, QF)]

        def head(h, carry):
            hr = pl.ds(pl.multiple_of(h * HD, HD), HD)
            for at in chunks:
                scores = dot(r.k[h, 0 : at.stop, :], r.qT[:, at])
                diagonal = jnp.where(causal(QF), scores[at.start :], NEG)
                top = jnp.max(diagonal, axis=0, keepdims=True)
                low_rows = N // 2 if at.start >= N // 2 else 0
                low = scores[:low_rows] if low_rows else None
                middle = scores[low_rows : at.start] if at.start > low_rows else None
                if middle is not None:
                    top = jnp.maximum(top, jnp.max(middle, axis=0, keepdims=True))
                if low is not None:
                    top = jnp.maximum(top, jnp.max(low, axis=0, keepdims=True) + split)
                terms = []
                if low is not None:
                    terms.append(jnp.exp(low - (top - split)))
                if middle is not None:
                    terms.append(jnp.exp(middle - top))
                terms.append(jnp.exp(diagonal - top))
                total = sum(jnp.sum(t, axis=0, keepdims=True) for t in terms)
                weights = jnp.concatenate([t.astype(BF16) for t in terms], axis=0)
                out = dot(r.vT[hr, 0 : at.stop], weights)
                r.oT[hr, at] = out * (1.0 / total)
                lse = top + jnp.log(total)
                r.lseB[h, :, at] = lse
                r.lseA[h, :, at] = lse - split if low_rows else lse
            return carry

        lax.fori_loop(0, c.hpd, head, 0)
        for at in chunks:
            r.do[at.start // HB : at.stop // HB] = (
                r.oT[:, at].astype(BF16).T.reshape(QF // HB, HB, W)
            )

    def send_rows(which, blocks):
        for t in range(n):
            r.ou[2 * t + which] = r.do[blocks[t]]
        copies = []
        for k in range(1, n):
            t = (s + k) % n
            copies.append(remote(r.ou.at[2 * t + which], r.orr.at[2 * s + which], at_seq(t)))
        r.orr[2 * s + which] = r.ou[2 * s + which]
        return copies

    collect(0)
    attend(0, N // 2)
    going = [send_rows(0, low_block)]
    collect(1)
    attend(N // 2, N)
    going.append(send_rows(1, top_block))

    for copy in (get_wo, get_wup, get_wfg, get_wdn):
        copy.wait()
    slope = math.sqrt(2.0 / math.pi)

    def forward_half(m):
        rows = slice(m * T // 2, (m + 1) * T // 2)
        for copy in going[m]:
            copy.wait()
        for i in range(B):
            for j in range(G):
                at = (m * B + i) * HB
                r.att[at : at + HB, j * W : (j + 1) * W] = r.orr[2 * (i * G + j) + m]
        x = r.xs[rows, :].astype(F32)
        branch = dot(r.att[rows, :], r.wo[...]) - x
        r.bamx[rows, :] = branch
        middle = x + r.ag[rows, :] * branch
        r.mid[rows, :] = middle
        normal, _ = norm_stats(middle)
        n2 = (normal * r.g2[...] + r.s2[...]).astype(BF16)
        r.n2[rows, :] = n2
        r.n2T[:, rows] = n2.T
        r.acc[rows, :] = jnp.zeros((T // 2, D), F32)

        def forward_chunk(j, carry):
            cols = pl.ds(pl.multiple_of(j * FC, FC), FC)
            u = dot(r.n2[rows, :], r.wup[:, cols])
            square = u * u
            t = jnp.tanh(slope * u * (1.0 + 0.044715 * square))
            half = 0.5 * (1.0 + t)
            hidden = (u * half).astype(BF16)
            r.hid[pl.ds(pl.multiple_of(j * T + m * T // 2, T // 2), T // 2), :] = hidden
            r.gp[j, rows, :] = half + 0.5 * u * (1.0 - t * t) * (
                slope * (1.0 + 3 * 0.044715 * square)
            )
            r.acc[rows, :] += dot(hidden, r.wdn[cols, :])
            return carry

        lax.fori_loop(0, NC, forward_chunk, 0, unroll=2)

    forward_half(0)
    forward_half(1)

    def partner(axis, bit):
        index = s if axis == "seq" else d
        mine = index // 2**bit % 2
        there = index + (1 - 2 * mine) * 2**bit
        return mine, at_seq(there) if axis == "seq" else at_dp(there)

    def add_rows(ref, start, slots, base, length):
        step = math.gcd(length, 512)

        def body(i, carry):
            at = pl.ds(pl.multiple_of(start + i * step, 16), step)
            other = slots[pl.ds(pl.multiple_of(base + i * step, 16), step), :]
            ref[at, :] = (ref[at, :].astype(F32) + other.astype(F32)).astype(BF16)
            return carry

        lax.fori_loop(0, length // step, body, 0)

    def halve(ref, slots, first, rows, bits, trail, credits):
        start, length, base = jnp.int32(first), rows, first
        for axis, bit in bits:
            half = length // 2
            mine, device = partner(axis, bit)
            keep = pl.multiple_of(start + mine * half, 16)
            give = pl.multiple_of(start + (1 - mine) * half, 16)
            copy = remote(ref.at[pl.ds(give, half)], slots.at[pl.ds(base, half)], device)
            yield
            copy.wait()
            credit = None
            if credits:
                assert count["credit"] < c.credits
                credit = r.free.at[count["credit"]]
                count["credit"] += 1
                pl.semaphore_signal(credit, inc=1, device_id=device, device_id_type=MESH)
            add_rows(ref, keep, slots, base, half)
            trail.append((keep, half, device, credit, start))
            start, length, base = keep, half, base + half

    def all_reduce(ref, slots, first, rows, bits, store):
        trail = []
        yield from halve(ref, slots, first, rows, bits, trail, True)
        for keep, half, device, credit, _ in reversed(trail):
            at = pl.ds(keep, half)
            pl.semaphore_wait(credit, 1)
            copy = remote(ref.at[at], ref.at[at], device)
            yield
            copy.wait()
        store()

    def reduce_small(own_ref, slots, dp_ref, dp_slots, out_ref):
        copies = []
        for k in range(1, n):
            copies.append(remote(own_ref, slots.at[s], at_seq((s + k) % n)))
        slots[s] = own_ref[...]
        yield
        for copy in copies:
            copy.wait()
        dp_ref[...] = sum(slots[i] for i in range(n))
        copies = []
        for k in range(1, nd):
            copies.append(remote(dp_ref, dp_slots.at[d], at_dp((d + k) % nd)))
        dp_slots[d] = dp_ref[...]
        yield
        for copy in copies:
            copy.wait()
        out_ref[...] = sum(dp_slots[i] for i in range(nd))

    jobs = {}

    def begin(name, job):
        jobs[name] = job
        next(job)

    def advance(name):
        if next(jobs[name], "over") == "over":
            del jobs[name]

    cores = [("seq", 0)]
    chips = [("seq", i) for i in range(1, c.seq_bits)]
    planes = [("dp", i) for i in range(c.dp_bits)]
    bits_of = dict(c=cores, x=chips[:1], y=chips[1:])
    bits_of["1"], bits_of["2"] = planes[:1], planes[1:]

    def bits_in(name):
        return [bit for mark in ORDERS[name] for bit in bits_of[mark]]

    puts = []

    def down_chunk(j, carry):
        part = dot_tn(r.hid[pl.ds(pl.multiple_of(j * T, T), T), :], r.dffn[...]).astype(BF16)
        for i in range(c.LP):
            at = pl.ds(pl.multiple_of((j * c.LP + i) * FC, FC), FC)
            r.fa[at, :] = part[:, i * LANES : (i + 1) * LANES]
        return carry

    def up_chunk(j, carry):
        part = dot(r.n2T[...], r.gp[j].astype(BF16)).astype(BF16)
        for i in range(FC // LANES):
            at = pl.ds(pl.multiple_of((j * (FC // LANES) + i) * D, D), D)
            r.fb[at, :] = part[:, i * LANES : (i + 1) * LANES]
        return carry

    def put_down(chunks):
        for j in chunks:
            for i in range(c.LP):
                at = (j * c.LP + i) * FC
                puts.append(
                    local(
                        r.fa.at[at : at + FC],
                        r.o_dn.at[j * FC : (j + 1) * FC, i * LANES : (i + 1) * LANES],
                    )
                )

    def put_up(chunks):
        per_chunk = FC // LANES
        for i in range(chunks.start * per_chunk, chunks.stop * per_chunk):
            puts.append(
                local(r.fb.at[i * D : (i + 1) * D], r.o_up.at[:, i * LANES : (i + 1) * LANES])
            )

    def put_rest():
        for j, ref in enumerate((r.o_out, r.o_ag, r.o_fg)):
            for i in range(c.LP):
                at = (j * c.LP + i) * D
                puts.append(
                    local(r.fc.at[at : at + D], ref.at[:, i * LANES : (i + 1) * LANES])
                )

    def feed_forward_sum(name, half, chunk, ref, slots, rows, put):
        chunks = range(half * NC // 2, (half + 1) * NC // 2)
        lax.fori_loop(chunks.start, chunks.stop, chunk, 0, unroll=True)
        begin(
            name,
            all_reduce(
                ref,
                slots,
                chunks.start * (rows // NC),
                rows // 2,
                bits_in(name),
                functools.partial(put, chunks),
            ),
        )

    steps = {}

    def step(function):
        steps[function.__name__] = function

    gate = jax.nn.sigmoid(dot(r.n2[...], r.wfg[...]) + r.bfg[...])
    middle = r.mid[...]
    apart = r.acc[...] - middle
    for copy in get_cot:
        copy.wait()
    grad = by_half(r.cot).astype(F32)
    mixed = (middle + gate * apart).astype(BF16)
    as_stored(mixed, r.cot)
    for m, part in enumerate(halves(r.o_mix)):
        puts.append(local(r.cot.at[m], part))
    r.dffn[...] = (grad * gate).astype(BF16)
    d_pre = (grad * apart * gate * (1.0 - gate)).astype(BF16)
    r.dpre[...] = d_pre
    r.sm[0:1, :] = jnp.sum(d_pre.astype(F32), axis=0, keepdims=True)
    r.dxr[...] = grad * (1.0 - gate)
    r.acc[...] = dot_nt(d_pre, r.wfg[...])

    @step
    def down_1():
        feed_forward_sum("a", 0, down_chunk, r.fa, r.sa, c.rows_a, put_down)

    @step
    def down_2():
        feed_forward_sum("b", 1, down_chunk, r.fa, r.sa, c.rows_a, put_down)

    def backward_chunk(j, carry):
        cols = pl.ds(pl.multiple_of(j * FC, FC), FC)
        d_hidden = dot_nt(r.dffn[...], r.wdn[cols, :])
        d_up = (d_hidden * r.gp[j]).astype(BF16)
        r.gp[j] = d_up.astype(F32)
        r.acc[...] += dot_nt(d_up, r.wup[:, cols])
        return carry

    @step
    def back_1():
        lax.fori_loop(0, NC // 2, backward_chunk, 0, unroll=True)

    @step
    def back_2():
        lax.fori_loop(NC // 2, NC, backward_chunk, 0, unroll=True)

    back = []

    @step
    def branch_back():
        d_norm = r.acc[...]
        normal, scale = norm_stats(r.mid[...])
        r.sm[1:2, :] = jnp.sum(d_norm * normal, axis=0, keepdims=True)
        r.sm[2:3, :] = jnp.sum(d_norm, axis=0, keepdims=True)
        d_middle = r.dxr[...] + norm_back(d_norm, r.g2[...], normal, scale)
        gate = r.ag[...]
        d_att = (d_middle * gate).astype(BF16)
        d_attn_pre = (d_middle * r.bamx[...] * gate * (1.0 - gate)).astype(BF16)
        r.datt[...] = d_att
        r.dapre[...] = d_attn_pre
        r.sm[3:4, :] = jnp.sum(d_attn_pre.astype(F32), axis=0, keepdims=True)
        r.sm[4:8, :] = jnp.zeros((4, D), F32)
        r.dxr[...] = d_middle * (1.0 - gate)
        d_o = dot_nt(d_att, r.wo[...]).astype(BF16)
        for i in range(B):
            for j in range(G):
                for m in range(2):
                    at = (m * B + i) * HB
                    r.ou[2 * (i * G + j) + m] = d_o[at : at + HB, j * W : (j + 1) * W]
        for k in range(1, n):
            t = (s + k) % n
            back.append(remote(r.ou.at[slot(t)], r.dor.at[slot(s)], at_seq(t)))
        r.dor[slot(s)] = r.ou[slot(s)]

    @step
    def up_1():
        feed_forward_sum("c", 0, up_chunk, r.fb, r.sb, c.rows_b, put_up)

    @step
    def up_2():
        feed_forward_sum("d", 1, up_chunk, r.fb, r.sb, c.rows_b, put_up)

    @step
    def other_weights():
        begin("s", reduce_small(r.sm, r.smr, r.smd, r.smdr, r.o_sm))
        for j, part in enumerate(
            (
                dot_tn(r.att[...], r.datt[...]),
                dot_tn(r.n1[...].reshape(T, D), r.dapre[...]),
                dot(r.n2T[...], r.dpre[...]),
            )
        ):
            part = part.astype(BF16)
            for i in range(c.LP):
                at = (j * c.LP + i) * D
                r.fc[at : at + D, :] = part[:, i * LANES : (i + 1) * LANES]
        if c.rows_c > c.used_c:
            r.fc[c.used_c :, :] = jnp.zeros((c.rows_c - c.used_c, LANES), BF16)
        begin("e", all_reduce(r.fc, r.sc, 0, c.rows_c, bits_in("e"), put_rest))
        r.acc[...] = dot_nt(r.dapre[...], r.wg[...])

    @step
    def by_position():
        for i in range(2 * n):
            r.hid[i * HB : (i + 1) * HB, :] = r.gat[holder[i], i // n]
        for copy in back:
            copy.wait()
        for i in range(NB):
            at = slice(i * QB, (i + 1) * QB)
            block = jnp.concatenate([r.dor[2 * holder[i * per + m] + i // HALF] for m in range(per)], axis=0)
            r.do[i * per : (i + 1) * per] = block.reshape(per, HB, W)
            turned = block.T
            r.doT[:, at] = turned
            product = turned.astype(F32) * r.oT[:, at]
            for h in range(c.hpd):
                r.odot[h, :, at] = jnp.sum(product[h * HD : (h + 1) * HD], axis=0, keepdims=True)

    def backward_block(j):
        at = slice(j * QB, (j + 1) * QB)
        lse_ref = r.lseA if j < HALF else r.lseB
        keys_t = []
        for h in range(c.hpd):
            own = [
                r.kT[h * HD : (h + 1) * HD, at] if i == h else jnp.zeros((HD, QB), BF16)
                for i in range(c.hpd)
            ]
            keys_t.append(jnp.concatenate(own, axis=0))
        keys_t = jnp.concatenate(keys_t, axis=1)
        d_keys, d_values = [0.0] * c.hpd, [0.0] * c.hpd
        for start in range(j * QB, N, N // 2):
            to = slice(start, min(start + N // 2, N))
            slopes = []
            for h in range(c.hpd):
                p = jnp.exp(dot(r.k[h, at, :], r.qT[:, to]) - lse_ref[h, :, to])
                if start == j * QB:
                    corner = jnp.where(causal(QB), p[:, :QB], 0.0)
                    p = jnp.concatenate([corner, p[:, QB:]], axis=1) if j < NB - 1 else corner
                dp = dot(r.v[h, at, :], r.doT[:, to])
                ds = (p * (dp - r.odot[h, :, to])).astype(BF16)
                slopes.append(ds)
                d_values[h] += dot(
                    p.astype(BF16), r.do[to.start // HB : to.stop // HB].reshape(-1, W)
                )
                d_keys[h] += dot(ds, r.q[to, :])
            part = dot(keys_t, jnp.concatenate(slopes, axis=0))
            if j == 0:
                r.dqT[:, to] = part
            else:
                r.dqT[:, to] += part
        for h in range(c.hpd):
            r.v[h, at, :] = d_values[h].astype(BF16)
            r.k[h, at, :] = d_keys[h].astype(BF16)

    def partial(at):
        return r.gat[at // 2, at % 2]

    def finish_half(which, blocks):
        for i in blocks:
            at = slice(i * QB, (i + 1) * QB)
            parts = [(r.dqT[:, at] * (1.0 / math.sqrt(HD))).astype(BF16).T]
            for ref in (r.k, r.v):
                part = ref[0, at, :]
                for h in range(1, c.hpd):
                    part = jnp.where(of_head[h], ref[h, at, :], part)
                parts.append(part)
            rows = jnp.concatenate(parts, axis=1)
            r.qkvst[i * per : (i + 1) * per] = rows.reshape(per, HB, 3 * W)
            r.gat[i * per // 2 : (i + 1) * per // 2] = (
                dot_nt(rows, r.wqkv[...]).astype(BF16).reshape(per // 2, 2, HB, D)
            )
        table = top_block if which else low_block

        def pick(m, parity):
            return jnp.where(parity == 0, table[2 * m], table[2 * m + 1])

        for m in range(pairs):
            r.sibs[which, m] = partial(pick(m, 1 - core))
        return remote(r.sibs.at[which], r.sibr.at[which], at_seq(sibling)), pick

    def pass_on(which, copy, pick):
        copy.wait()
        for m in range(pairs):
            r.sibs[which, m] = (
                partial(pick(m, core)).astype(F32) + r.sibr[which, m].astype(F32)
            ).astype(BF16)
        copies = []
        for k in range(1, pairs):
            m = (pair + k) % pairs
            copies.append(
                remote(r.sibs.at[which, m], r.dnr.at[pair, which], at_seq(2 * m + core))
            )
        r.dnr[pair, which] = r.sibs[which, pair]
        return copies

    def weight_part(which):
        rows = slice(which * N // 2, (which + 1) * N // 2)
        return dot_tn(r.hid[rows, :], r.qkvst[which * n : (which + 1) * n].reshape(N // 2, 3 * W))

    arriving = []
    held_up = {}

    for j in range(NB):
        steps[f"low_{j}" if j < HALF else f"top_{j - HALF}"] = functools.partial(backward_block, j)

    @step
    def finish_low():
        held_up[0] = finish_half(0, range(HALF))

    @step
    def weights_low():
        r.wacc[...] = weight_part(0)

    @step
    def pass_low():
        arriving.extend(pass_on(0, *held_up[0]))

    @step
    def finish_top():
        held_up[1] = finish_half(1, range(HALF, NB))

    @step
    def pass_top():
        arriving.extend(pass_on(1, *held_up[1]))

    group_bits = log2(G)
    buffers = [("seq", i) for i in range(group_bits, c.seq_bits)]
    members = [("seq", i) for i in range(1, group_bits)]

    def heads_reduce(first, bits, members_at):
        trail = []
        yield from halve(r.fq, r.sq, first, D, bits, trail, False)
        start, length = trail[-1][0], trail[-1][1]
        r.resq[g, pl.ds(start, length), :] = r.fq[pl.ds(start, length), :]
        steps = [("rows", step) for step in reversed(trail)]
        steps[members_at:members_at] = [("members", bit) for bit in members]
        steps.append(("members", cores[0]))
        held = [g]
        for kind, step in steps:
            at = pl.ds(start, length)
            if kind == "rows":
                device = step[2]
            else:
                mine, device = partner(*step)
            copies = [remote(r.resq.at[i, at], r.resq.at[i, at], device) for i in held]
            yield
            for copy in copies:
                copy.wait()
            if kind == "rows":
                start, length = pl.multiple_of(step[4], 16), 2 * length
            else:
                held = held + [i + (1 - 2 * mine) * 2 ** step[1] for i in held]

    splits = len(buffers + planes)

    @step
    def weights_top():
        part = (r.wacc[...] + weight_part(1)).astype(BF16)
        if c.np3 * LANES > 3 * W:
            part = jnp.concatenate([part, jnp.zeros((D, c.np3 * LANES - 3 * W), BF16)], axis=1)
        for i in range(c.np3):
            r.fq[i * D : (i + 1) * D, :] = part[:, i * LANES : (i + 1) * LANES]
            bits, at = (
                (buffers + planes, splits),
                (planes + buffers, 0),
                (buffers + planes, splits - len(buffers)),
            )[i]
            begin("qkv"[i], heads_reduce(i * D, bits, at))

    @step
    def first_back():
        for copy in arriving:
            copy.wait()
        parts = []
        for m in range(2):
            for i in range(B):
                parts.append(
                    sum(r.dnr[i * (G // 2) + j, m].astype(F32) for j in range(G // 2))
                )
        d_norm = jnp.concatenate(parts, axis=0) + r.acc[...]
        normal, scale = norm_stats(inputs())
        r.sm2[0:1, :] = jnp.sum(d_norm * normal, axis=0, keepdims=True)
        r.sm2[1:2, :] = jnp.sum(d_norm, axis=0, keepdims=True)
        r.sm2[2:8, :] = jnp.zeros((6, D), F32)
        begin("t", reduce_small(r.sm2, r.sm2r, r.sm2d, r.sm2dr, r.o_sm2))
        grads = (r.dxr[...] + norm_back(d_norm, r.g1[...], normal, scale)).astype(BF16)
        as_stored(grads, r.tok)
        for m, part in enumerate(halves(r.o_tok)):
            puts.append(local(r.tok.at[m], part))

    for name in SCHEDULE:
        if name in steps:
            steps.pop(name)()
        elif name in jobs:
            advance(name)
    assert not steps
    while jobs:
        for name in list(jobs):
            advance(name)

    outs = (r.o_q, r.o_k, r.o_v)
    for i in range(G):
        if W == LANES:
            for j, ref in enumerate(outs):
                puts.append(
                    local(
                        r.resq.at[i, j * D : (j + 1) * D], ref.at[:, i * LANES : (i + 1) * LANES]
                    )
                )
            continue
        block = jnp.concatenate(
            [r.resq[i, m * D : (m + 1) * D, :] for m in range(c.np3)], axis=1
        )
        for j in range(3):
            r.gqkv[j, :, i * W : (i + 1) * W] = block[:, j * W : (j + 1) * W]
    if W < LANES:
        for j, ref in enumerate(outs):
            puts.append(local(r.gqkv.at[j], ref))
    for put in puts:
        put.wait()


def blocks_of(shapes):
    blocks = []
    for i, (rows, columns) in enumerate(shapes):
        step = min(rows, 2**18 // columns)
        blocks += [(i, at, step) for at in range(0, rows, step)]
    return blocks


def widen(arrays, blocks, *refs):
    refs = iter(refs)
    take = lambda number: [next(refs) for _ in range(number)]
    grads, rest, small = take(arrays), take(2), take(2)
    wide, rest_out, rows = take(arrays), take(2), take(6)
    held, held_wide, held_rest = take(arrays), take(arrays), take(2)
    (sems,) = take(1)
    loads = []
    for j, (i, at, step) in enumerate(blocks):
        block = pl.ds(at, step)
        loads.append(pltpu.make_async_copy(grads[i].at[block], held[i].at[block], sems.at[0, j]))
    for j in range(2):
        loads.append(
            pltpu.make_async_copy(rest[j], held_rest[j], sems.at[0, len(blocks) + j])
        )
    for load in loads:
        load.start()
    for j, row in enumerate(rows):
        row[...] = small[j // 4][j % 4 : j % 4 + 1, :]
    stores = []
    for j, (i, at, step) in enumerate(blocks):
        block = pl.ds(at, step)
        loads[j].wait()
        part = min(step, 64)

        def body(m, carry):
            here = pl.ds(pl.multiple_of(at + m * part, part), part)
            held_wide[i][here, :] = held[i][here, :].astype(F32)
            return carry

        lax.fori_loop(0, step // part, body, 0)
        stores.append(
            pltpu.make_async_copy(held_wide[i].at[block], wide[i].at[block], sems.at[1, j])
        )
        stores[-1].start()
    for j in range(2):
        loads[len(blocks) + j].wait()
        stores.append(
            pltpu.make_async_copy(held_rest[j], rest_out[j], sems.at[1, len(blocks) + j])
        )
        stores[-1].start()
    for store in stores:
        store.wait()


def solution(mesh):
    n, nd = mesh.shape["seq"], mesh.shape["dp"]

    def local(
        tokens,
        cotangent,
        query_weight,
        key_weight,
        value_weight,
        output_weight,
        attn_gate_weight,
        attn_gate_bias,
        up_weight,
        down_weight,
        ffn_gate_weight,
        ffn_gate_bias,
        first_gain,
        first_shift,
        second_gain,
        second_shift,
        row_kind,
        block_order,
    ):
        L, B, D = tokens.shape
        FF = up_weight.shape[1]
        c = sizes(n, nd, L, B, D, FF)
        spaces = scratch(c)
        names = IN_NAMES + OUT_NAMES + list(spaces)
        smem = pl.BlockSpec(memory_space=pltpu.SMEM)
        vmem = pl.BlockSpec(memory_space=pltpu.VMEM)
        hbm = pl.BlockSpec(memory_space=pl.ANY)

        def shape(*dims, dtype=BF16):
            return jax.ShapeDtypeStruct(dims, dtype)

        def row(vector):
            return vector.reshape(1, -1)

        out = pl.pallas_call(
            functools.partial(kernel, c, names),
            out_shape=(
                shape(L, B, D),
                shape(L, B, D),
                shape(D, D),
                shape(D, D),
                shape(D, D),
                shape(D, D),
                shape(D, D),
                shape(D, FF),
                shape(FF, D),
                shape(D, D),
                shape(8, D, dtype=F32),
                shape(8, D, dtype=F32),
            ),
            in_specs=[smem] * 2 + [hbm] * 16,
            out_specs=(hbm,) * 10 + (vmem,) * 2,
            scratch_shapes=list(spaces.values()),
            compiler_params=pltpu.CompilerParams(
                collective_id=0, has_side_effects=True, vmem_limit_bytes=VMEM_BYTES
            ),
            name="layer",
        )(
            block_order,
            row_kind,
            row(attn_gate_bias),
            row(ffn_gate_bias),
            row(first_gain),
            row(first_shift),
            row(second_gain),
            row(second_shift),
            tokens,
            cotangent,
            query_weight,
            key_weight,
            value_weight,
            output_weight,
            attn_gate_weight,
            up_weight,
            down_weight,
            ffn_gate_weight,
        )
        mix, tok, *grads, small, small2 = out
        shapes = [a.shape for a in grads]
        wide = pl.pallas_call(
            functools.partial(widen, len(grads), blocks_of(shapes)),
            out_shape=tuple(shape(*dims, dtype=F32) for dims in shapes)
            + (shape(L, B, D),) * 2
            + (shape(1, D, dtype=F32),) * 6,
            in_specs=[hbm] * (len(grads) + 2) + [vmem] * 2,
            out_specs=(hbm,) * (len(grads) + 2) + (vmem,) * 6,
            scratch_shapes=[pltpu.VMEM(dims, BF16) for dims in shapes]
            + [pltpu.VMEM(dims, F32) for dims in shapes]
            + [pltpu.VMEM((L, B, D), BF16)] * 2
            + [pltpu.SemaphoreType.DMA((2, len(blocks_of(shapes)) + 2))],
            compiler_params=pltpu.CompilerParams(vmem_limit_bytes=VMEM_BYTES),
            name="widen",
        )(*grads, mix, tok, small, small2)
        dq, dk, dv, dout, dag, dup, ddn, dfg, mix, tok = wide[:10]
        bfg, g2, s2, bg, g1, s1 = (a.reshape(D) for a in wide[10:])
        return mix, tok, dq, dk, dv, dout, dag, bg, dup, ddn, dfg, bfg, g1, s1, g2, s2

    sharded = P("seq", "dp", None)
    return jax.shard_map(
        local,
        mesh=mesh,
        in_specs=(sharded, sharded) + (P(),) * 14 + (P("dp"), P("dp", None)),
        out_specs=(sharded, sharded) + (P(),) * 14,
        check_vma=False,
    )


VMEM_BYTES = 63 * 2**20
```

```python
import functools
import math
from types import SimpleNamespace

import jax
import jax.numpy as jnp
from jax import lax
from jax.experimental import pallas as pl
from jax.experimental.pallas import tpu as pltpu
from jax.sharding import PartitionSpec as P

H = 8
HD = 64
NEG = -1e30
EPS = 1e-05
MESH = pl.DeviceIdType.MESH
F32 = jnp.float32
BF16 = jnp.bfloat16
LANES = 128


def dot(a, b):
    return jnp.dot(a, b, preferred_element_type=F32)


def dot_nt(a, b):
    return lax.dot_general(a, b, (((1,), (1,)), ((), ())), preferred_element_type=F32)


def dot_tn(a, b):
    return lax.dot_general(a, b, (((0,), (0,)), ((), ())), preferred_element_type=F32)


def log2(value):
    return value.bit_length() - 1


def sizes(n, nd, rows, buffers, features, hidden):
    c = SimpleNamespace(n=n, nd=nd, L=rows, B=buffers, D=features, FF=hidden)
    c.T = rows * buffers
    c.N = rows * n
    c.HB = rows // 2
    c.G = n // buffers
    c.hpd = H // c.G
    c.W = c.hpd * HD
    c.QB = min(256, c.N // 2)
    c.QF = min(512, c.N // 2)
    c.NB = c.N // c.QB
    c.HALF = c.NB // 2
    c.FC = 512
    c.NC = hidden // c.FC
    c.LP = features // LANES
    unit = 16 * n * nd
    c.rows_a = hidden * c.LP
    c.rows_b = (hidden // LANES) * features
    c.rows_c = -(-(3 * features * c.LP) // unit) * unit
    c.used_c = 3 * features * c.LP
    c.np3 = -(-(3 * c.W) // LANES)
    c.rows_q = c.np3 * features
    c.seq_bits = log2(n)
    c.dp_bits = log2(nd)
    c.remotes = 12 * n + 2 * nd + 10 * (c.seq_bits + c.dp_bits)
    c.credits = 5 * (c.seq_bits + c.dp_bits)
    c.locals = 34 + c.NC * c.LP + hidden // LANES + 3 * c.LP + 3 * c.G
    return c


def scratch(c):
    v = pltpu.VMEM
    spaces = dict(
        tok=v((2, c.HB, c.B, c.D), BF16),
        cot=v((2, c.HB, c.B, c.D), BF16),
        xs=v((c.T, c.D), BF16),
        bg=v((1, c.D), F32),
        bfg=v((1, c.D), F32),
        g1=v((1, c.D), F32),
        s1=v((1, c.D), F32),
        g2=v((1, c.D), F32),
        s2=v((1, c.D), F32),
        win=v((3, c.D, LANES) if c.W < LANES else (3, 16, LANES), BF16),
        wqkv=v((c.D, 3 * c.W), BF16),
        wg=v((c.D, c.D), BF16),
        wo=v((c.D, c.D), BF16),
        wup=v((c.D, c.FF), BF16),
        wdn=v((c.FF, c.D), BF16),
        wfg=v((c.D, c.D), BF16),
        n1=v((2, c.B, c.HB, c.D), BF16),
        gat=v((c.n, 2, c.HB, c.D), BF16),
        qkvst=v((2 * c.n, c.HB, 3 * c.W), BF16),
        q=v((c.N, c.W), BF16),
        k=v((c.hpd, c.N, c.W), BF16),
        v=v((c.hpd, c.N, c.W), BF16),
        do=v((2 * c.n, c.HB, c.W), BF16),
        kT=v((c.W, c.N), BF16),
        qT=v((c.W, c.N), BF16),
        vT=v((c.W, c.N), BF16),
        doT=v((c.W, c.N), BF16),
        oT=v((c.W, c.N), F32),
        dqT=v((c.W, c.N), F32),
        lseA=v((c.hpd, 1, c.N), F32),
        lseB=v((c.hpd, 1, c.N), F32),
        odot=v((c.hpd, 1, c.N), F32),
        ou=v((2 * c.n, c.HB, c.W), BF16),
        orr=v((2 * c.n, c.HB, c.W), BF16),
        dor=v((2 * c.n, c.HB, c.W), BF16),
        att=v((c.T, c.D), BF16),
        ag=v((c.T, c.D), F32),
        mid=v((c.T, c.D), F32),
        mix=v((c.T, c.D), BF16),
        bamx=v((c.T, c.D), F32),
        acc=v((c.T, c.D), F32),
        dxr=v((c.T, c.D), F32),
        n2=v((c.T, c.D), BF16),
        n2T=v((c.D, c.T), BF16),
        gp=v((c.NC, c.T, c.FC), F32),
        hid=v((max(c.NC * c.T, c.N), c.FC), BF16),
        dffn=v((c.T, c.D), BF16),
        dpre=v((c.T, c.D), BF16),
        datt=v((c.T, c.D), BF16),
        dapre=v((c.T, c.D), BF16),
        wacc=v((c.D, 3 * c.W), F32),
        sibs=v((2, c.n // 2, c.HB, c.D), BF16),
        sibr=v((2, c.n // 2, c.HB, c.D), BF16),
        dnr=v((c.n // 2, 2, c.HB, c.D), BF16),
        fa=v((c.rows_a, LANES), BF16),
        fb=v((c.rows_b, LANES), BF16),
        fc=v((c.rows_c, LANES), BF16),
        fq=v((c.rows_q, LANES), BF16),
        sa=v((c.rows_a, LANES), BF16),
        sb=v((c.rows_b, LANES), BF16),
        sc=v((c.rows_c, LANES), BF16),
        sq=v((c.rows_q, LANES), BF16),
        resq=v((c.G, c.rows_q, LANES), BF16),
        gqkv=v((3, c.D, c.D) if c.W < LANES else (3, 16, LANES), BF16),
        sm=v((8, c.D), F32),
        smr=v((c.n, 8, c.D), F32),
        smd=v((8, c.D), F32),
        smdr=v((c.nd, 8, c.D), F32),
        sm2=v((8, c.D), F32),
        sm2r=v((c.n, 8, c.D), F32),
        sm2d=v((8, c.D), F32),
        sm2dr=v((c.nd, 8, c.D), F32),
        ss=pltpu.SemaphoreType.DMA((c.remotes,)),
        rs=pltpu.SemaphoreType.DMA((c.remotes,)),
        ls=pltpu.SemaphoreType.DMA((c.locals,)),
        free=pltpu.SemaphoreType.REGULAR((c.credits,)),
    )
    return spaces


ORDERS = dict(a="c1xy2", b="cyx21", c="cxy12", d="cy21x", e="c1xy2")
SCHEDULE = [
    "down_1",
    "down_2",
    "back_1",
    "a",
    "b",
    "back_2",
    "branch_back",
    "up_1",
    "up_2",
    "other_weights",
    "a",
    "c",
    "d",
    "e",
    "b",
    "s",
    "s",
    "a",
    "d",
    "by_position",
    "e",
    "b",
    "low_0",
    "low_0_rest",
    "c",
    "a",
    "low_1",
    "low_1_rest",
    "e",
    "low_2",
    "low_2_rest",
    "c",
    "b",
    "a",
    "low_3",
    "low_3_rest",
    "e",
    "d",
    "finish_low",
    "b",
    "a",
    "c",
    "weights_low",
    "pass_low",
    "e",
    "top_0",
    "c",
    "b",
    "a",
    "d",
    "top_1",
    "top_2",
    "e",
    "top_3",
    "finish_top",
    "c",
    "d",
    "weights_top",
    "b",
    "pass_top",
    "e",
    "c",
    "d",
    "k",
    "a",
    "q",
    "v",
    "k",
    "d",
    "k",
    "q",
    "v",
    "c",
    "k",
    "b",
    "q",
    "v",
    "k",
    "q",
    "v",
    "e",
    "d",
    "b",
    "first_back",
    "q",
    "b",
    "k",
    "c",
    "a",
    "v",
    "c",
    "a",
    "v",
    "t",
    "q",
    "d",
    "k",
    "v",
    "t",
    "d",
    "q",
    "k",
    "v",
    "e",
    "q",
    "e",
]
IN_NAMES = [
    "i_order",
    "i_kind",
    "i_bg",
    "i_bfg",
    "i_g1",
    "i_s1",
    "i_g2",
    "i_s2",
    "i_tok",
    "i_cot",
    "i_wq",
    "i_wk",
    "i_wv",
    "i_wo",
    "i_wg",
    "i_wup",
    "i_wdn",
    "i_wfg",
]
OUT_NAMES = [
    "o_mix",
    "o_tok",
    "o_q",
    "o_k",
    "o_v",
    "o_out",
    "o_ag",
    "o_up",
    "o_dn",
    "o_fg",
    "o_sm",
    "o_sm2",
]


def norm_stats(values):
    average = jnp.mean(values, axis=-1, keepdims=True)
    centred = values - average
    variance = jnp.mean(centred * centred, axis=-1, keepdims=True)
    scale = lax.rsqrt(variance + EPS)
    return centred * scale, scale


def norm_back(grad, gain, normal, scale):
    e = grad * gain
    return scale * (
        e
        - jnp.mean(e, axis=-1, keepdims=True)
        - normal * jnp.mean(e * normal, axis=-1, keepdims=True)
    )


def kernel(c, names, *refs):
    r = SimpleNamespace(**dict(zip(names, refs)))
    n, nd, L, B, D, T, N, HB, G, W = c.n, c.nd, c.L, c.B, c.D, c.T, c.N, c.HB, c.G, c.W
    QB, NB, HALF, FC, NC, QF = c.QB, c.NB, c.HALF, c.FC, c.NC, c.QF
    s = lax.axis_index("seq")
    d = lax.axis_index("dp")
    b = s // G
    g = s % G
    core = s % 2
    pair = s // 2
    pairs = n // 2
    sibling = s + 1 - 2 * core
    count = dict(remote=0, local=0, credit=0)

    def remote(src, dst, device):
        i = count["remote"]
        assert i < c.remotes
        count["remote"] += 1
        copy = pltpu.make_async_remote_copy(
            src_ref=src,
            dst_ref=dst,
            send_sem=r.ss.at[i],
            recv_sem=r.rs.at[i],
            device_id=device,
            device_id_type=MESH,
        )
        copy.start()
        return copy

    def local(src, dst):
        i = count["local"]
        assert i < c.locals
        count["local"] += 1
        copy = pltpu.make_async_copy(src, dst, r.ls.at[i])
        copy.start()
        return copy

    def at_seq(t):
        return {"seq": t, "dp": d}

    def at_dp(t):
        return {"seq": s, "dp": t}

    def halves(ref):
        return [ref.at[pl.ds(m * HB, HB)] for m in range(2)]

    get_tok = [local(part, r.tok.at[m]) for m, part in enumerate(halves(r.i_tok))]
    get_rows = [
        local(getattr(r, "i_" + name), getattr(r, name))
        for name in ("g1", "s1", "bg", "g2", "s2", "bfg")
    ]
    window = pl.multiple_of((g * W) // LANES * LANES, LANES)
    get_win = [
        local(
            ref.at[:, pl.ds(window, LANES)],
            r.win.at[i] if W < LANES else r.wqkv.at[:, i * LANES : (i + 1) * LANES],
        )
        for i, ref in enumerate((r.i_wq, r.i_wk, r.i_wv))
    ]
    get_wg = local(r.i_wg, r.wg)
    get_cot = [local(part, r.cot.at[m]) for m, part in enumerate(halves(r.i_cot))]
    get_wo = local(r.i_wo, r.wo)
    get_wup = local(r.i_wup, r.wup)
    get_wfg = local(r.i_wfg, r.wfg)
    get_wdn = local(r.i_wdn, r.wdn)
    barrier = pltpu.get_barrier_semaphore()
    for k in range(1, n):
        pl.semaphore_signal(barrier, inc=1, device_id=at_seq((s + k) % n), device_id_type=MESH)
    for k in range(1, nd):
        pl.semaphore_signal(barrier, inc=1, device_id=at_dp((d + k) % nd), device_id_type=MESH)

    low_first = [r.i_order[i, 2 * s] < r.i_order[i, 2 * s + 1] for i in range(B)]

    def by_half(ref):
        return jnp.concatenate(
            [
                jnp.where(low_first[i], ref[m, :, i, :], ref[1 - m, :, i, :])
                for m in range(2)
                for i in range(B)
            ],
            axis=0,
        )

    def as_stored(rows, ref):
        parts = rows.reshape(2, B, HB, D)
        for i in range(B):
            for m in range(2):
                ref[m, :, i, :] = jnp.where(low_first[i], parts[m, i], parts[1 - m, i])

    for copy in get_tok:
        copy.wait()
    r.xs[...] = by_half(r.tok)

    def inputs():
        return r.xs[...].astype(F32)

    normal, _ = norm_stats(inputs())
    for copy in get_rows:
        copy.wait()
    n1 = (normal * r.g1[...] + r.s1[...]).astype(BF16)
    r.n1[...] = n1.reshape(2, B, HB, D)

    pl.semaphore_wait(barrier, n - 1 + nd - 1)

    def slot(t):
        return pl.ds(2 * t, 2)

    gather, relay = ({}, {}), ({}, {})

    def send_half(m):
        for k in range(1, pairs):
            t = 2 * ((pair + k) % pairs) + core
            gather[m][k] = remote(r.n1.at[m, t // G], r.gat.at[s, m], at_seq(t))
        relay[m][0] = remote(r.n1.at[m, b], r.gat.at[s, m], at_seq(sibling))
        r.gat[s, m] = r.n1[m, b]

    send_half(0)

    for copy in get_win:
        copy.wait()
    if W < LANES:
        upper = (g * W) % LANES != 0
        r.wqkv[...] = jnp.concatenate(
            [jnp.where(upper, r.win[i][:, W:], r.win[i][:, :W]) for i in range(3)], axis=1
        )
    get_wg.wait()
    r.ag[...] = jax.nn.sigmoid(dot(n1, r.wg[...]) + r.bg[...])

    order = [r.i_order[b, i] for i in range(2 * n)]
    low_block = [jnp.minimum(order[2 * t], order[2 * t + 1]) for t in range(n)]
    top_block = [jnp.maximum(order[2 * t], order[2 * t + 1]) for t in range(n)]
    holder = []
    for p in range(2 * n):
        found = jnp.int32(0)
        for t in range(n):
            found = jnp.where((low_block if p < n else top_block)[t] == p, t, found)
        holder.append(found)
    split = jnp.where(r.i_kind[b] == 2, F32(NEG), F32(0.0))

    def project(t, m):
        out = dot(r.gat[t, m], r.wqkv[...])
        r.qkvst[2 * t + m] = jnp.concatenate(
            [out[:, :W] * (1.0 / math.sqrt(HD)), out[:, W:]], axis=1
        ).astype(BF16)

    for k in range(1, pairs):
        gather[0][k].wait_send()
    send_half(1)
    for m in range(2):
        project(s, m)

    per = QB // HB
    head_of = lax.broadcasted_iota(jnp.int32, (QB, W), 1) // HD
    of_head = [head_of == h for h in range(c.hpd)]

    def collect(m):
        for k in range(1, pairs):
            gather[m][k].wait_recv() if m == 0 else gather[m][k].wait()
            u = 2 * ((pair + pairs - k) % pairs) + core
            relay[m][k] = remote(r.gat.at[u, m], r.gat.at[u, m], at_seq(sibling))
            project(u, m)
        for k in range(pairs):
            relay[m][k].wait()
            project(2 * ((pair + pairs - k) % pairs) + 1 - core, m)
        for i in range(m * HALF, m * HALF + HALF):
            at = slice(i * QB, (i + 1) * QB)
            block = jnp.concatenate(
                [r.qkvst[2 * holder[i * per + j] + m] for j in range(per)], axis=0
            )
            q, k, v = (block[:, j * W : (j + 1) * W] for j in range(3))
            r.q[at, :] = q
            r.qT[:, at] = q.T
            r.kT[:, at] = k.T
            r.vT[:, at] = v.T
            for h in range(c.hpd):
                r.k[h, at, :] = jnp.where(of_head[h], k, BF16(0.0))
                r.v[h, at, :] = jnp.where(of_head[h], v, BF16(0.0))

    def causal(size):
        keys_at = lax.broadcasted_iota(jnp.int32, (size, size), 0)
        return keys_at <= lax.broadcasted_iota(jnp.int32, (size, size), 1)

    def attend(first, last):
        chunks = [slice(i, i + QF) for i in range(first, last, QF)]

        def head(h, carry):
            hr = pl.ds(pl.multiple_of(h * HD, HD), HD)
            for at in chunks:
                scores = dot(r.k[h, 0 : at.stop, :], r.qT[:, at])
                diagonal = jnp.where(causal(QF), scores[at.start :], NEG)
                top = jnp.max(diagonal, axis=0, keepdims=True)
                low_rows = N // 2 if at.start >= N // 2 else 0
                low = scores[:low_rows] if low_rows else None
                middle = scores[low_rows : at.start] if at.start > low_rows else None
                if middle is not None:
                    top = jnp.maximum(top, jnp.max(middle, axis=0, keepdims=True))
                if low is not None:
                    top = jnp.maximum(top, jnp.max(low, axis=0, keepdims=True) + split)
                terms = []
                if low is not None:
                    terms.append(jnp.exp(low - (top - split)))
                if middle is not None:
                    terms.append(jnp.exp(middle - top))
                terms.append(jnp.exp(diagonal - top))
                total = sum(jnp.sum(t, axis=0, keepdims=True) for t in terms)
                weights = jnp.concatenate([t.astype(BF16) for t in terms], axis=0)
                out = dot(r.vT[hr, 0 : at.stop], weights)
                r.oT[hr, at] = out * (1.0 / total)
                lse = top + jnp.log(total)
                r.lseB[h, :, at] = lse
                r.lseA[h, :, at] = lse - split if low_rows else lse
            return carry

        lax.fori_loop(0, c.hpd, head, 0)
        for at in chunks:
            r.do[at.start // HB : at.stop // HB] = (
                r.oT[:, at].astype(BF16).T.reshape(QF // HB, HB, W)
            )

    def send_rows(which, blocks):
        for t in range(n):
            r.ou[2 * t + which] = r.do[blocks[t]]
        copies = []
        for k in range(1, n):
            t = (s + k) % n
            copies.append(remote(r.ou.at[2 * t + which], r.orr.at[2 * s + which], at_seq(t)))
        r.orr[2 * s + which] = r.ou[2 * s + which]
        return copies

    collect(0)
    attend(0, N // 2)
    going = [send_rows(0, low_block)]
    collect(1)
    attend(N // 2, N)
    going.append(send_rows(1, top_block))

    for copy in (get_wo, get_wup, get_wfg, get_wdn):
        copy.wait()
    slope = math.sqrt(2.0 / math.pi)

    def forward_half(m):
        rows = slice(m * T // 2, (m + 1) * T // 2)
        for copy in going[m]:
            copy.wait()
        for i in range(B):
            for j in range(G):
                at = (m * B + i) * HB
                r.att[at : at + HB, j * W : (j + 1) * W] = r.orr[2 * (i * G + j) + m]
        x = r.xs[rows, :].astype(F32)
        branch = dot(r.att[rows, :], r.wo[...]) - x
        r.bamx[rows, :] = branch
        middle = x + r.ag[rows, :] * branch
        r.mid[rows, :] = middle
        normal, _ = norm_stats(middle)
        n2 = (normal * r.g2[...] + r.s2[...]).astype(BF16)
        r.n2[rows, :] = n2
        r.n2T[:, rows] = n2.T
        r.acc[rows, :] = jnp.zeros((T // 2, D), F32)

        def forward_chunk(j, carry):
            cols = pl.ds(pl.multiple_of(j * FC, FC), FC)
            u = dot(r.n2[rows, :], r.wup[:, cols])
            square = u * u
            t = jnp.tanh(slope * u * (1.0 + 0.044715 * square))
            half = 0.5 * (1.0 + t)
            hidden = (u * half).astype(BF16)
            r.hid[pl.ds(pl.multiple_of(j * T + m * T // 2, T // 2), T // 2), :] = hidden
            r.gp[j, rows, :] = half + 0.5 * u * (1.0 - t * t) * (
                slope * (1.0 + 3 * 0.044715 * square)
            )
            r.acc[rows, :] += dot(hidden, r.wdn[cols, :])
            return carry

        lax.fori_loop(0, NC, forward_chunk, 0, unroll=2)

    forward_half(0)
    forward_half(1)

    puts = []

    def partner(axis, bit):
        index = s if axis == "seq" else d
        mine = index // 2**bit % 2
        there = index + (1 - 2 * mine) * 2**bit
        return mine, at_seq(there) if axis == "seq" else at_dp(there)

    def add_rows(ref, start, slots, base, length):
        step = math.gcd(length, 512)

        def body(i, carry):
            at = pl.ds(pl.multiple_of(start + i * step, 16), step)
            other = slots[pl.ds(pl.multiple_of(base + i * step, 16), step), :]
            ref[at, :] = (ref[at, :].astype(F32) + other.astype(F32)).astype(BF16)
            return carry

        lax.fori_loop(0, length // step, body, 0)

    def halve(ref, slots, first, rows, bits, trail, credits):
        start, length, base = jnp.int32(first), rows, first
        for axis, bit in bits:
            half = length // 2
            mine, device = partner(axis, bit)
            keep = pl.multiple_of(start + mine * half, 16)
            give = pl.multiple_of(start + (1 - mine) * half, 16)
            copy = remote(ref.at[pl.ds(give, half)], slots.at[pl.ds(base, half)], device)
            yield
            copy.wait()
            credit = None
            if credits:
                assert count["credit"] < c.credits
                credit = r.free.at[count["credit"]]
                count["credit"] += 1
                pl.semaphore_signal(credit, inc=1, device_id=device, device_id_type=MESH)
            add_rows(ref, keep, slots, base, half)
            trail.append((keep, half, device, credit, start))
            start, length, base = keep, half, base + half

    def all_reduce(ref, slots, first, rows, bits, store):
        trail = []
        yield from halve(ref, slots, first, rows, bits, trail, True)
        for keep, half, device, credit, _ in reversed(trail):
            at = pl.ds(keep, half)
            pl.semaphore_wait(credit, 1)
            copy = remote(ref.at[at], ref.at[at], device)
            yield
            copy.wait()
        store()

    def reduce_small(own_ref, slots, dp_ref, dp_slots, out_ref):
        copies = []
        for k in range(1, n):
            copies.append(remote(own_ref, slots.at[s], at_seq((s + k) % n)))
        slots[s] = own_ref[...]
        yield
        for copy in copies:
            copy.wait()
        dp_ref[...] = sum(slots[i] for i in range(n))
        copies = []
        for k in range(1, nd):
            copies.append(remote(dp_ref, dp_slots.at[d], at_dp((d + k) % nd)))
        dp_slots[d] = dp_ref[...]
        yield
        for copy in copies:
            copy.wait()
        dp_ref[...] = sum(dp_slots[i] for i in range(nd))
        puts.append(local(dp_ref, out_ref))

    jobs = {}

    def begin(name, job):
        jobs[name] = job
        next(job)

    def advance(name):
        if next(jobs[name], "over") == "over":
            del jobs[name]

    cores = [("seq", 0)]
    chips = [("seq", i) for i in range(1, c.seq_bits)]
    planes = [("dp", i) for i in range(c.dp_bits)]
    bits_of = dict(c=cores, x=chips[:1], y=chips[1:])
    bits_of["1"], bits_of["2"] = planes[:1], planes[1:]

    def bits_in(name):
        return [bit for mark in ORDERS[name] for bit in bits_of[mark]]


    def down_chunk(j, carry):
        part = dot_tn(r.hid[pl.ds(pl.multiple_of(j * T, T), T), :], r.dffn[...]).astype(BF16)
        for i in range(c.LP):
            at = pl.ds(pl.multiple_of((j * c.LP + i) * FC, FC), FC)
            r.fa[at, :] = part[:, i * LANES : (i + 1) * LANES]
        return carry

    def up_chunk(j, carry):
        part = dot(r.n2T[...], r.gp[j].astype(BF16)).astype(BF16)
        for i in range(FC // LANES):
            at = pl.ds(pl.multiple_of((j * (FC // LANES) + i) * D, D), D)
            r.fb[at, :] = part[:, i * LANES : (i + 1) * LANES]
        return carry

    def put_down(chunks):
        for j in chunks:
            for i in range(c.LP):
                at = (j * c.LP + i) * FC
                puts.append(
                    local(
                        r.fa.at[at : at + FC],
                        r.o_dn.at[j * FC : (j + 1) * FC, i * LANES : (i + 1) * LANES],
                    )
                )

    def put_up(chunks):
        per_chunk = FC // LANES
        for i in range(chunks.start * per_chunk, chunks.stop * per_chunk):
            puts.append(
                local(r.fb.at[i * D : (i + 1) * D], r.o_up.at[:, i * LANES : (i + 1) * LANES])
            )

    def put_rest():
        for j, ref in enumerate((r.o_out, r.o_ag, r.o_fg)):
            for i in range(c.LP):
                at = (j * c.LP + i) * D
                puts.append(
                    local(r.fc.at[at : at + D], ref.at[:, i * LANES : (i + 1) * LANES])
                )

    def feed_forward_sum(name, half, chunk, ref, slots, rows, put):
        chunks = range(half * NC // 2, (half + 1) * NC // 2)
        lax.fori_loop(chunks.start, chunks.stop, chunk, 0, unroll=True)
        begin(
            name,
            all_reduce(
                ref,
                slots,
                chunks.start * (rows // NC),
                rows // 2,
                bits_in(name),
                functools.partial(put, chunks),
            ),
        )

    steps = {}

    def step(function):
        steps[function.__name__] = function

    gate = jax.nn.sigmoid(dot(r.n2[...], r.wfg[...]) + r.bfg[...])
    middle = r.mid[...]
    apart = r.acc[...] - middle
    for copy in get_cot:
        copy.wait()
    grad = by_half(r.cot).astype(F32)
    r.mix[...] = (middle + gate * apart).astype(BF16)
    r.dffn[...] = (grad * gate).astype(BF16)
    d_pre = (grad * apart * gate * (1.0 - gate)).astype(BF16)
    r.dpre[...] = d_pre
    r.sm[0:1, :] = jnp.sum(d_pre.astype(F32), axis=0, keepdims=True)
    r.dxr[...] = grad * (1.0 - gate)
    r.acc[...] = dot_nt(d_pre, r.wfg[...])

    @step
    def down_1():
        feed_forward_sum("a", 0, down_chunk, r.fa, r.sa, c.rows_a, put_down)

    @step
    def down_2():
        feed_forward_sum("b", 1, down_chunk, r.fa, r.sa, c.rows_a, put_down)

    def backward_chunk(j, carry):
        cols = pl.ds(pl.multiple_of(j * FC, FC), FC)
        d_hidden = dot_nt(r.dffn[...], r.wdn[cols, :])
        d_up = (d_hidden * r.gp[j]).astype(BF16)
        r.gp[j] = d_up.astype(F32)
        r.acc[...] += dot_nt(d_up, r.wup[:, cols])
        return carry

    @step
    def back_1():
        lax.fori_loop(0, NC // 2, backward_chunk, 0, unroll=True)

    @step
    def back_2():
        lax.fori_loop(NC // 2, NC, backward_chunk, 0, unroll=True)

    back = []

    @step
    def branch_back():
        d_norm = r.acc[...]
        normal, scale = norm_stats(r.mid[...])
        r.sm[1:2, :] = jnp.sum(d_norm * normal, axis=0, keepdims=True)
        r.sm[2:3, :] = jnp.sum(d_norm, axis=0, keepdims=True)
        d_middle = r.dxr[...] + norm_back(d_norm, r.g2[...], normal, scale)
        gate = r.ag[...]
        d_att = (d_middle * gate).astype(BF16)
        d_attn_pre = (d_middle * r.bamx[...] * gate * (1.0 - gate)).astype(BF16)
        r.datt[...] = d_att
        r.dapre[...] = d_attn_pre
        r.sm[3:4, :] = jnp.sum(d_attn_pre.astype(F32), axis=0, keepdims=True)
        r.sm[4:8, :] = jnp.zeros((4, D), F32)
        r.dxr[...] = d_middle * (1.0 - gate)
        d_o = dot_nt(d_att, r.wo[...]).astype(BF16)
        for i in range(B):
            for j in range(G):
                for m in range(2):
                    at = (m * B + i) * HB
                    r.ou[2 * (i * G + j) + m] = d_o[at : at + HB, j * W : (j + 1) * W]
        for k in range(1, n):
            t = (s + k) % n
            back.append(remote(r.ou.at[slot(t)], r.dor.at[slot(s)], at_seq(t)))
        r.dor[slot(s)] = r.ou[slot(s)]

    @step
    def up_1():
        feed_forward_sum("c", 0, up_chunk, r.fb, r.sb, c.rows_b, put_up)

    @step
    def up_2():
        feed_forward_sum("d", 1, up_chunk, r.fb, r.sb, c.rows_b, put_up)

    @step
    def other_weights():
        begin("s", reduce_small(r.sm, r.smr, r.smd, r.smdr, r.o_sm))
        for j, part in enumerate(
            (
                dot_tn(r.att[...], r.datt[...]),
                dot_tn(r.n1[...].reshape(T, D), r.dapre[...]),
                dot(r.n2T[...], r.dpre[...]),
            )
        ):
            part = part.astype(BF16)
            for i in range(c.LP):
                at = (j * c.LP + i) * D
                r.fc[at : at + D, :] = part[:, i * LANES : (i + 1) * LANES]
        if c.rows_c > c.used_c:
            r.fc[c.used_c :, :] = jnp.zeros((c.rows_c - c.used_c, LANES), BF16)
        begin("e", all_reduce(r.fc, r.sc, 0, c.rows_c, bits_in("e"), put_rest))
        r.acc[...] = dot_nt(r.dapre[...], r.wg[...])
        as_stored(r.mix[...], r.cot)
        for m, part in enumerate(halves(r.o_mix)):
            puts.append(local(r.cot.at[m], part))

    @step
    def by_position():
        for i in range(2 * n):
            r.hid[i * HB : (i + 1) * HB, :] = r.gat[holder[i], i // n]
        for copy in back:
            copy.wait()
        for i in range(NB):
            at = slice(i * QB, (i + 1) * QB)
            block = jnp.concatenate([r.dor[2 * holder[i * per + m] + i // HALF] for m in range(per)], axis=0)
            r.do[i * per : (i + 1) * per] = block.reshape(per, HB, W)
            turned = block.T
            r.doT[:, at] = turned
            product = turned.astype(F32) * r.oT[:, at]
            for h in range(c.hpd):
                r.odot[h, :, at] = jnp.sum(product[h * HD : (h + 1) * HD], axis=0, keepdims=True)

    def backward_block(j):
        at = slice(j * QB, (j + 1) * QB)
        lse_ref = r.lseA if j < HALF else r.lseB
        keys_t = []
        for h in range(c.hpd):
            own = [
                r.kT[h * HD : (h + 1) * HD, at] if i == h else jnp.zeros((HD, QB), BF16)
                for i in range(c.hpd)
            ]
            keys_t.append(jnp.concatenate(own, axis=0))
        keys_t = jnp.concatenate(keys_t, axis=1)
        d_keys, d_values = [0.0] * c.hpd, [0.0] * c.hpd
        for start in range(j * QB, N, N // 2):
            if start > j * QB:
                yield
            to = slice(start, min(start + N // 2, N))
            slopes = []
            for h in range(c.hpd):
                p = jnp.exp(dot(r.k[h, at, :], r.qT[:, to]) - lse_ref[h, :, to])
                if start == j * QB:
                    corner = jnp.where(causal(QB), p[:, :QB], 0.0)
                    p = jnp.concatenate([corner, p[:, QB:]], axis=1) if j < NB - 1 else corner
                dp = dot(r.v[h, at, :], r.doT[:, to])
                ds = (p * (dp - r.odot[h, :, to])).astype(BF16)
                slopes.append(ds)
                d_values[h] += dot(
                    p.astype(BF16), r.do[to.start // HB : to.stop // HB].reshape(-1, W)
                )
                d_keys[h] += dot(ds, r.q[to, :])
            part = dot(keys_t, jnp.concatenate(slopes, axis=0))
            if j == 0:
                r.dqT[:, to] = part
            else:
                r.dqT[:, to] += part
        for h in range(c.hpd):
            r.v[h, at, :] = d_values[h].astype(BF16)
            r.k[h, at, :] = d_keys[h].astype(BF16)

    def partial(at):
        return r.gat[at // 2, at % 2]

    def finish_half(which, blocks):
        for i in blocks:
            at = slice(i * QB, (i + 1) * QB)
            parts = [(r.dqT[:, at] * (1.0 / math.sqrt(HD))).astype(BF16).T]
            for ref in (r.k, r.v):
                part = ref[0, at, :]
                for h in range(1, c.hpd):
                    part = jnp.where(of_head[h], ref[h, at, :], part)
                parts.append(part)
            rows = jnp.concatenate(parts, axis=1)
            r.qkvst[i * per : (i + 1) * per] = rows.reshape(per, HB, 3 * W)
            r.gat[i * per // 2 : (i + 1) * per // 2] = (
                dot_nt(rows, r.wqkv[...]).astype(BF16).reshape(per // 2, 2, HB, D)
            )
        table = top_block if which else low_block

        def pick(m, parity):
            return jnp.where(parity == 0, table[2 * m], table[2 * m + 1])

        for m in range(pairs):
            r.sibs[which, m] = partial(pick(m, 1 - core))
        return remote(r.sibs.at[which], r.sibr.at[which], at_seq(sibling)), pick

    def pass_on(which, copy, pick):
        copy.wait()
        for m in range(pairs):
            r.sibs[which, m] = (
                partial(pick(m, core)).astype(F32) + r.sibr[which, m].astype(F32)
            ).astype(BF16)
        copies = []
        for k in range(1, pairs):
            m = (pair + k) % pairs
            copies.append(
                remote(r.sibs.at[which, m], r.dnr.at[pair, which], at_seq(2 * m + core))
            )
        r.dnr[pair, which] = r.sibs[which, pair]
        return copies

    def weight_part(which):
        rows = slice(which * N // 2, (which + 1) * N // 2)
        return dot_tn(r.hid[rows, :], r.qkvst[which * n : (which + 1) * n].reshape(N // 2, 3 * W))

    arriving = []
    held_up = {}

    def continued(block):
        assert next(block, "over") == "over"

    def started(j):
        block = backward_block(j)
        if next(block, "over") != "over":
            steps[f"low_{j}_rest"] = functools.partial(continued, block)

    for j in range(NB):
        steps[f"low_{j}" if j < HALF else f"top_{j - HALF}"] = functools.partial(started, j)

    @step
    def finish_low():
        held_up[0] = finish_half(0, range(HALF))

    @step
    def weights_low():
        r.wacc[...] = weight_part(0)

    @step
    def pass_low():
        arriving.extend(pass_on(0, *held_up[0]))

    @step
    def finish_top():
        held_up[1] = finish_half(1, range(HALF, NB))

    @step
    def pass_top():
        arriving.extend(pass_on(1, *held_up[1]))

    group_bits = log2(G)
    buffers = [("seq", i) for i in range(group_bits, c.seq_bits)]
    members = [("seq", i) for i in range(1, group_bits)]

    def heads_reduce(first, bits, members_at):
        trail = []
        yield from halve(r.fq, r.sq, first, D, bits, trail, False)
        start, length = trail[-1][0], trail[-1][1]
        r.resq[g, pl.ds(start, length), :] = r.fq[pl.ds(start, length), :]
        steps = [("rows", step) for step in reversed(trail)]
        steps[members_at:members_at] = [("members", bit) for bit in members]
        steps.append(("members", cores[0]))
        held = [g]
        for kind, step in steps:
            at = pl.ds(start, length)
            if kind == "rows":
                device = step[2]
            else:
                mine, device = partner(*step)
            copies = [remote(r.resq.at[i, at], r.resq.at[i, at], device) for i in held]
            yield
            for copy in copies:
                copy.wait()
            if kind == "rows":
                start, length = pl.multiple_of(step[4], 16), 2 * length
            else:
                held = held + [i + (1 - 2 * mine) * 2 ** step[1] for i in held]

    splits = len(buffers + planes)

    @step
    def weights_top():
        part = (r.wacc[...] + weight_part(1)).astype(BF16)
        if c.np3 * LANES > 3 * W:
            part = jnp.concatenate([part, jnp.zeros((D, c.np3 * LANES - 3 * W), BF16)], axis=1)
        for i in range(c.np3):
            r.fq[i * D : (i + 1) * D, :] = part[:, i * LANES : (i + 1) * LANES]
            bits, at = (
                (buffers + planes, splits),
                (planes + buffers, 0),
                (buffers + planes, splits - len(buffers)),
            )[i]
            begin("qkv"[i], heads_reduce(i * D, bits, at))

    @step
    def first_back():
        for copy in arriving:
            copy.wait()
        parts = []
        for m in range(2):
            for i in range(B):
                parts.append(
                    sum(r.dnr[i * (G // 2) + j, m].astype(F32) for j in range(G // 2))
                )
        d_norm = jnp.concatenate(parts, axis=0) + r.acc[...]
        normal, scale = norm_stats(inputs())
        r.sm2[0:1, :] = jnp.sum(d_norm * normal, axis=0, keepdims=True)
        r.sm2[1:2, :] = jnp.sum(d_norm, axis=0, keepdims=True)
        r.sm2[2:8, :] = jnp.zeros((6, D), F32)
        begin("t", reduce_small(r.sm2, r.sm2r, r.sm2d, r.sm2dr, r.o_sm2))
        grads = (r.dxr[...] + norm_back(d_norm, r.g1[...], normal, scale)).astype(BF16)
        as_stored(grads, r.tok)
        for m, part in enumerate(halves(r.o_tok)):
            puts.append(local(r.tok.at[m], part))

    for name in SCHEDULE:
        if name in steps:
            steps.pop(name)()
        elif name in jobs:
            advance(name)
    assert not steps
    while jobs:
        for name in list(jobs):
            advance(name)

    outs = (r.o_q, r.o_k, r.o_v)
    for i in range(G):
        if W == LANES:
            for j, ref in enumerate(outs):
                puts.append(
                    local(
                        r.resq.at[i, j * D : (j + 1) * D], ref.at[:, i * LANES : (i + 1) * LANES]
                    )
                )
            continue
        block = jnp.concatenate(
            [r.resq[i, m * D : (m + 1) * D, :] for m in range(c.np3)], axis=1
        )
        for j in range(3):
            r.gqkv[j, :, i * W : (i + 1) * W] = block[:, j * W : (j + 1) * W]
    if W < LANES:
        for j, ref in enumerate(outs):
            puts.append(local(r.gqkv.at[j], ref))
    for put in puts:
        put.wait()


def blocks_of(shapes):
    blocks = []
    for i, (rows, columns) in enumerate(shapes):
        step = min(rows, 2**18 // columns)
        blocks += [(i, at, step) for at in range(0, rows, step)]
    return blocks


def widen(arrays, blocks, *refs):
    refs = iter(refs)
    take = lambda number: [next(refs) for _ in range(number)]
    grads, rest, small = take(arrays), take(2), take(2)
    wide, rest_out, rows = take(arrays), take(2), take(6)
    held, held_wide, held_rest = take(arrays), take(arrays), take(2)
    (sems,) = take(1)
    loads = []
    for j, (i, at, step) in enumerate(blocks):
        block = pl.ds(at, step)
        loads.append(pltpu.make_async_copy(grads[i].at[block], held[i].at[block], sems.at[0, j]))
    for j in range(2):
        loads.append(
            pltpu.make_async_copy(rest[j], held_rest[j], sems.at[0, len(blocks) + j])
        )
    for load in loads:
        load.start()
    for j, row in enumerate(rows):
        row[...] = small[j // 4][j % 4 : j % 4 + 1, :]
    stores = []
    for j, (i, at, step) in enumerate(blocks):
        block = pl.ds(at, step)
        loads[j].wait()
        part = min(step, 64)

        def body(m, carry):
            here = pl.ds(pl.multiple_of(at + m * part, part), part)
            held_wide[i][here, :] = held[i][here, :].astype(F32)
            return carry

        lax.fori_loop(0, step // part, body, 0)
        stores.append(
            pltpu.make_async_copy(held_wide[i].at[block], wide[i].at[block], sems.at[1, j])
        )
        stores[-1].start()
    for j in range(2):
        loads[len(blocks) + j].wait()
        stores.append(
            pltpu.make_async_copy(held_rest[j], rest_out[j], sems.at[1, len(blocks) + j])
        )
        stores[-1].start()
    for store in stores:
        store.wait()


def solution(mesh):
    n, nd = mesh.shape["seq"], mesh.shape["dp"]

    def local(
        tokens,
        cotangent,
        query_weight,
        key_weight,
        value_weight,
        output_weight,
        attn_gate_weight,
        attn_gate_bias,
        up_weight,
        down_weight,
        ffn_gate_weight,
        ffn_gate_bias,
        first_gain,
        first_shift,
        second_gain,
        second_shift,
        row_kind,
        block_order,
    ):
        L, B, D = tokens.shape
        FF = up_weight.shape[1]
        c = sizes(n, nd, L, B, D, FF)
        spaces = scratch(c)
        names = IN_NAMES + OUT_NAMES + list(spaces)
        smem = pl.BlockSpec(memory_space=pltpu.SMEM)
        vmem = pl.BlockSpec(memory_space=pltpu.VMEM)
        hbm = pl.BlockSpec(memory_space=pl.ANY)

        def shape(*dims, dtype=BF16):
            return jax.ShapeDtypeStruct(dims, dtype)

        def row(vector):
            return vector.reshape(1, -1)

        out = pl.pallas_call(
            functools.partial(kernel, c, names),
            out_shape=(
                shape(L, B, D),
                shape(L, B, D),
                shape(D, D),
                shape(D, D),
                shape(D, D),
                shape(D, D),
                shape(D, D),
                shape(D, FF),
                shape(FF, D),
                shape(D, D),
                shape(8, D, dtype=F32),
                shape(8, D, dtype=F32),
            ),
            in_specs=[smem] * 2 + [hbm] * 16,
            out_specs=(hbm,) * 12,
            scratch_shapes=list(spaces.values()),
            compiler_params=pltpu.CompilerParams(
                collective_id=0, has_side_effects=True, vmem_limit_bytes=VMEM_BYTES
            ),
            name="layer",
        )(
            block_order,
            row_kind,
            row(attn_gate_bias),
            row(ffn_gate_bias),
            row(first_gain),
            row(first_shift),
            row(second_gain),
            row(second_shift),
            tokens,
            cotangent,
            query_weight,
            key_weight,
            value_weight,
            output_weight,
            attn_gate_weight,
            up_weight,
            down_weight,
            ffn_gate_weight,
        )
        mix, tok, *grads, small, small2 = out
        shapes = [a.shape for a in grads]
        wide = pl.pallas_call(
            functools.partial(widen, len(grads), blocks_of(shapes)),
            out_shape=tuple(shape(*dims, dtype=F32) for dims in shapes)
            + (shape(L, B, D),) * 2
            + (shape(1, D, dtype=F32),) * 6,
            in_specs=[hbm] * (len(grads) + 2) + [vmem] * 2,
            out_specs=(hbm,) * (len(grads) + 2) + (vmem,) * 6,
            scratch_shapes=[pltpu.VMEM(dims, BF16) for dims in shapes]
            + [pltpu.VMEM(dims, F32) for dims in shapes]
            + [pltpu.VMEM((L, B, D), BF16)] * 2
            + [pltpu.SemaphoreType.DMA((2, len(blocks_of(shapes)) + 2))],
            compiler_params=pltpu.CompilerParams(vmem_limit_bytes=VMEM_BYTES),
            name="widen",
        )(*grads, mix, tok, small, small2)
        dq, dk, dv, dout, dag, dup, ddn, dfg, mix, tok = wide[:10]
        bfg, g2, s2, bg, g1, s1 = (a.reshape(D) for a in wide[10:])
        return mix, tok, dq, dk, dv, dout, dag, bg, dup, ddn, dfg, bfg, g1, s1, g2, s2

    sharded = P("seq", "dp", None)
    return jax.shard_map(
        local,
        mesh=mesh,
        in_specs=(sharded, sharded) + (P(),) * 14 + (P("dp"), P("dp", None)),
        out_specs=(sharded, sharded) + (P(),) * 14,
        check_vma=False,
    )


VMEM_BYTES = 63 * 2**20
```
